32 devices in a mesh: tok: 4 (over y, x), gr: 2 (over core), gc: 4 (over z).
Axes of the slice: x: 2, y: 2, z: 4, core: 2. Of those that a mesh axis runs over, the one named last changes fastest.
Arguments:
- acts: bfloat16 [512, 16384], P('tok', ('gr', 'gc')), may hold values from -24 to 24
- init_basis: float32 [16, 1024, 512], P(('gr', 'gc'), 'tok'), may hold values from -6 to 6
- kept: int32 [16, 16], replicated, may hold values from 0 to 1, as said below
- member: int32 [16], replicated, may hold values from 0 to 1, as said below
Outputs:
- bases: float32 [16, 1024, 512], P(('gr', 'gc'), 'tok')
- latent: bfloat16 [512, 1024], P(('tok', 'gr', 'gc'))
The draws below stay inside these ranges and needn't reach their ends.
Inputs may be any that keep to these rules, and one draw needn't show every extreme that they name: kept is symmetric with ones on the diagonal. `member`: each of the 2 group numbers names exactly 8 blocks.
All inputs are finite; a program needn't handle non-finite values.
Results may differ from the reference program's by a relative error of at most 0.0095.
Values may be sent and summed in bfloat16 or wider, within the bound.
No kernel may reach another device: no remote copies, remote signals or barrier semaphores. Data moves between devices by JAX's collectives and lax.ppermute only.
A program may use at most 64 MiB of HBM per device.

```python
import math
import jax
import jax.numpy as jnp
from jax import lax

BLK = 1024
RANK = 512
NBLK = 16
GBLK = 8
ITERS = 2
TOKENS = 512
COLS = 16384
NGRP = 2
GCOLS = 8192


def draw_acts(key, part):
    key = jax.random.fold_in(key, 37)
    noise_key, order_key = jax.random.split(key)
    noise = jnp.clip(jax.random.normal(noise_key, (TOKENS, COLS), jnp.float32), -6.0, 6.0)
    order = jax.random.permutation(order_key, NBLK).astype(jnp.float32)
    block_scale = jnp.exp(jnp.log(4.0) * order / (NBLK - 1))
    within = jnp.arange(BLK, dtype=jnp.float32) / (BLK - 1)
    row_scale = jnp.exp(jnp.log(16.0) * within)
    column_scale = (block_scale[:, None] * row_scale[None, :]).reshape(COLS) / 16.0
    return (noise * column_scale[None, :]).astype(jnp.bfloat16)


def draw_kept(key, part):
    key = jax.random.fold_in(key, 23)
    coins = jax.random.randint(key, (NBLK, NBLK), 0, 2, dtype=jnp.int32)
    upper = jnp.triu(coins, 1)
    return (upper + upper.T + jnp.eye(NBLK, dtype=jnp.int32)).astype(jnp.int32)


def draw_member(key, part):
    key = jax.random.fold_in(key, 11)
    labels = jnp.arange(NBLK, dtype=jnp.int32) // GBLK
    return jax.random.permutation(key, labels).astype(jnp.int32)


def level_of(stream_key, shape, pieces, low, top_value):
    factor_of = 1.0
    for dim, blocks in pieces:
        steps = jax.random.uniform(jax.random.fold_in(jax.random.fold_in(stream_key, 6), dim), (blocks,), jnp.float32, low / len(pieces), top_value / len(pieces))
        factor_of = factor_of * jnp.repeat(jnp.exp(steps), shape[dim] // blocks).reshape((-1,) + (1,) * (len(shape) - 1 - dim))
    return factor_of


def normal_values(key, dims, deviation, bound, cuts=(), kind=jnp.bfloat16):
    values = deviation * jax.random.normal(key, dims, jnp.float32)
    if cuts:
        values = values * level_of(key, dims, cuts, -0.22, 0.18)
    return jnp.clip(values, -bound, bound).astype(kind)


def setup_inputs(seed: int = 0) -> dict:
    splits = jax.random.split(jax.random.key(seed), 5)
    acts = draw_acts(jax.random.fold_in(splits[4], 71), 0)
    init_basis = normal_values(splits[1], (NBLK, BLK, RANK), 1.0, 6.0, ((0, 8), (1, 4)), jnp.float32)
    kept = draw_kept(jax.random.fold_in(splits[4], 71), 0)
    member = draw_member(jax.random.fold_in(splits[4], 71), 0)
    return {"acts": acts, "init_basis": init_basis, "kept": kept, "member": member}


def project(pair):
    return jnp.dot(pair[0].astype(jnp.float32), pair[1].astype(jnp.float32), preferred_element_type=jnp.float32)

def reference(acts, init_basis, kept, member):
    highest = lax.Precision.HIGHEST
    blocks_x = acts.reshape(TOKENS, NBLK, BLK).transpose(1, 0, 2)
    links = ((member[:, None] == member[None, :]).astype(jnp.int32) * kept).astype(jnp.float32)
    selector = (member[:, None] == jnp.arange(NGRP, dtype=jnp.int32)[None, :]).astype(jnp.float32)
    basis = init_basis
    for step in range(ITERS):
        basis_bf = basis.astype(jnp.bfloat16)
        proj = lax.map(project, (blocks_x, basis_bf)).astype(jnp.bfloat16)
        proj_wide = proj.astype(jnp.float32)

        def combine_row(row):
            return jnp.tensordot(row, proj_wide, axes=1, precision=highest).astype(jnp.bfloat16)
        mixed = lax.map(combine_row, links)

        def cover(pair):
            return jnp.dot(pair[0].T.astype(jnp.float32), pair[1].astype(jnp.float32), preferred_element_type=jnp.float32)
        image = lax.map(cover, (blocks_x, mixed)) / TOKENS + 2.0 * basis_bf.astype(jnp.float32)
        grams = jnp.einsum('irb,irs->ibs', image, image, precision=highest)
        gram = jnp.einsum('ig,ibs->gbs', selector, grams, precision=highest)
        lower = jnp.linalg.cholesky(gram / GCOLS)
        own_lower = jnp.einsum('ig,gbs->ibs', selector, lower, precision=highest)

        def solve_one(pair):
            return jax.scipy.linalg.solve_triangular(pair[0], pair[1].T, lower=True).T
        basis = lax.map(solve_one, (own_lower, image))
    codes = lax.map(project, (blocks_x, basis.astype(jnp.bfloat16)))
    latent = jnp.einsum('jg,jtr->tgr', selector, codes, precision=highest).reshape(TOKENS, NGRP * RANK)
    latent = latent * (1.0 / math.sqrt(GCOLS))
    return (basis, latent.astype(jnp.bfloat16))
```

```python
import functools
import math

import jax
import jax.numpy as jnp
from jax import lax
from jax.experimental import pallas as pl
from jax.experimental.pallas import tpu as pltpu
from jax.sharding import PartitionSpec as P

GBLK = 8
ITERS = 2
PANEL = 128
SUB = 8

ridge = 2.0
HIGHEST = lax.Precision.HIGHEST


def eliminate(tiles, store):
    lane = lax.broadcasted_iota(jnp.int32, (1, PANEL), 1)
    lane_tile = lax.broadcasted_iota(jnp.int32, (SUB, PANEL), 1)
    tiles = list(tiles)
    for j in range(PANEL):
        s, r = divmod(j, SUB)
        row = tiles[s][r : r + 1, :]
        pivot = row[:, j : j + 1]
        unit = jnp.where(lane == j, 1.0, row)
        root = lax.rsqrt(pivot)
        root = root * (1.5 - 0.5 * pivot * root * root)
        store(j, jnp.where(lane <= j, unit, 0.0) * root)
        scaled = jnp.broadcast_to(unit * (1.0 / pivot), (SUB, PANEL))
        first = s if r < SUB - 1 else s + 1
        for q in range(first, PANEL // SUB):
            factor = tiles[q][:, j : j + 1]
            tiles[q] = jnp.where(lane_tile == j, 0.0, tiles[q]) - factor * scaled


def factor_kernel(scale, gram_ref, out_ref, inv_ref):
    groups, rank, _ = gram_ref.shape
    panels = rank // PANEL
    out_ref[...] = gram_ref[...] * scale

    def panel_step(k, carry):
        here = pl.ds(pl.multiple_of(k * PANEL, PANEL), PANEL)
        diag = [out_ref[g, here, here] for g in range(groups)]
        stores = []
        for g in range(groups):

            def store(j, row, g=g):
                inv_ref[g, j : j + 1, :] = row

            stores.append(store)
        for g in range(groups):
            eliminate([diag[g][SUB * q : SUB * (q + 1), :] for q in range(PANEL // SUB)], stores[g])
        for g in range(groups):
            inv = inv_ref[g]
            out_ref[g, here, :] = jnp.dot(
                inv, out_ref[g, here, :], preferred_element_type=jnp.float32, precision=HIGHEST
            )
            out_ref[g, here, here] = inv
        for i in range(1, panels):

            @pl.when(i > k)
            def _():
                for g in range(groups):
                    below = pl.ds(i * PANEL, PANEL)
                    out_ref[g, below, here] = jnp.zeros((PANEL, PANEL), jnp.float32)
                    upper = out_ref[g, here, :]
                    out_ref[g, below, :] -= lax.dot_general(
                        upper[:, i * PANEL : (i + 1) * PANEL],
                        upper,
                        (((0,), (0,)), ((), ())),
                        preferred_element_type=jnp.float32,
                        precision=HIGHEST,
                    )

        return carry

    lax.fori_loop(0, panels, panel_step, 0)
    for i in range(panels - 1):
        out_ref[:, i * PANEL : (i + 1) * PANEL, (i + 1) * PANEL :] = jnp.zeros(
            (groups, PANEL, rank - (i + 1) * PANEL), jnp.float32
        )


def inverse_factor(gram, scale):
    groups, rank, _ = gram.shape
    return pl.pallas_call(
        functools.partial(factor_kernel, scale),
        out_shape=jax.ShapeDtypeStruct(gram.shape, jnp.float32),
        in_specs=[pl.BlockSpec(memory_space=pltpu.VMEM)],
        out_specs=pl.BlockSpec(memory_space=pltpu.VMEM),
        scratch_shapes=[pltpu.VMEM((groups, PANEL, PANEL), jnp.float32)],
        compiler_params=pltpu.CompilerParams(vmem_limit_bytes=32 * 1024 * 1024),
        name="inverse_factor",
    )(gram)


def split(value):
    high = lax.reduce_precision(value, 8, 7)
    return high.astype(jnp.bfloat16), (value - high).astype(jnp.bfloat16)


def per_device(acts, init_basis, kept, member):
    owned = init_basis.shape[0]
    slice_rows = init_basis.shape[1]
    rank = init_basis.shape[2]
    tok_count = lax.axis_size("tok")
    block_cols = slice_rows * tok_count
    tok_rows = acts.shape[0]
    total_tokens = tok_rows * tok_count
    groups = kept.shape[0] // GBLK
    group_cols = GBLK * block_cols
    own_cols = rank // tok_count
    first = lax.axis_index(("gr", "gc")) * owned
    tok_pos = lax.axis_index("tok")
    links = (member[:, None] == member[None, :]).astype(jnp.int32) * kept
    own_links = lax.dynamic_slice_in_dim(links, first, owned, 0).astype(jnp.bfloat16)
    own_groups = lax.dynamic_slice_in_dim(member, first, owned, 0)
    selector = (own_groups[:, None] == jnp.arange(groups, dtype=jnp.int32)[None, :]).astype(
        jnp.float32
    )

    def own_slice(full):
        return lax.dynamic_slice_in_dim(full, tok_pos * own_cols, own_cols, full.ndim - 1)

    own_x = acts.reshape(tok_rows, owned, block_cols)
    full_x = lax.all_gather(acts, "tok", axis=0, tiled=True)
    full_x = full_x.reshape(total_tokens, owned, block_cols)
    basis_bf = lax.all_gather(init_basis.astype(jnp.bfloat16), "tok", axis=1, tiled=True)
    for step in range(ITERS):
        proj = jnp.einsum(
            "tob,obr->otr", full_x, own_slice(basis_bf), preferred_element_type=jnp.float32
        ).astype(jnp.bfloat16)
        mixed = jnp.einsum(
            "ok,ktr->otr",
            own_links,
            lax.all_gather(proj, ("gr", "gc"), axis=0, tiled=True),
            preferred_element_type=jnp.float32,
        ).astype(jnp.bfloat16)
        mixed = lax.all_gather(mixed, "tok", axis=2, tiled=True)
        cover = jnp.einsum("tob,otr->obr", full_x, mixed, preferred_element_type=jnp.float32)
        image = cover / total_tokens + ridge * basis_bf.astype(jnp.float32)
        grams = jnp.einsum("obr,obs->ors", own_slice(image), image, precision=HIGHEST)
        stacked = jnp.sum(selector[:, :, None, None] * grams[:, None], axis=0)
        piece = lax.psum_scatter(stacked, ("gr", "gc"), scatter_dimension=1, tiled=True)
        gram = lax.all_gather(piece, ("tok", "gr", "gc"), axis=1, tiled=True)
        inverse = inverse_factor(gram, 1.0 / group_cols)
        own_inverse = jnp.sum(selector[:, :, None, None] * inverse[None], axis=1)
        if step < ITERS - 1:
            basis_bf = jnp.einsum(
                "obr,osr->obs", image, own_inverse, precision=HIGHEST
            ).astype(jnp.bfloat16)
    rows = lax.dynamic_slice_in_dim(image, tok_pos * slice_rows, slice_rows, 1)
    basis = jnp.einsum("obr,osr->obs", rows, own_inverse, precision=HIGHEST)
    codes = sum(
        jnp.einsum("tob,obr->otr", own_x, part, preferred_element_type=jnp.float32)
        for part in split(image)
    )
    placed = jnp.sum(selector[:, None, :, None] * codes[:, :, None, :], axis=0)
    placed = lax.psum_scatter(
        placed.reshape(tok_rows, groups * rank), ("gr", "gc"), scatter_dimension=0, tiled=True
    )
    latent = jnp.concatenate(
        [
            jnp.einsum(
                "tr,sr->ts",
                placed[:, g * rank : (g + 1) * rank],
                inverse[g],
                precision=HIGHEST,
            )
            for g in range(groups)
        ],
        axis=1,
    )
    latent = latent * (1.0 / math.sqrt(group_cols))
    return (basis, latent.astype(jnp.bfloat16))


def solution(mesh):
    placed = (P("tok", ("gr", "gc")), P(("gr", "gc"), "tok", None), P(), P())
    return jax.shard_map(
        per_device,
        mesh=mesh,
        in_specs=placed,
        out_specs=(P(("gr", "gc"), "tok", None), P(("tok", "gr", "gc"), None)),
        check_vma=False,
    )
```

```python
import functools
import math

import jax
import jax.numpy as jnp
from jax import lax
from jax.experimental import pallas as pl
from jax.experimental.pallas import tpu as pltpu
from jax.sharding import PartitionSpec as P

GBLK = 8
ITERS = 2
PANEL = 128
SUB = 8

ridge = 2.0
HIGHEST = lax.Precision.HIGHEST


def eliminate(tiles, store):
    lane = lax.broadcasted_iota(jnp.int32, (1, PANEL), 1)
    lane_tile = lax.broadcasted_iota(jnp.int32, (SUB, PANEL), 1)
    tiles = list(tiles)
    for j in range(PANEL):
        s, r = divmod(j, SUB)
        row = tiles[s][r : r + 1, :]
        pivot = row[:, j : j + 1]
        unit = jnp.where(lane == j, 1.0, row)
        root = lax.rsqrt(pivot)
        root = root * (1.5 - 0.5 * pivot * root * root)
        store(j, jnp.where(lane <= j, unit, 0.0) * root)
        scaled = jnp.broadcast_to(unit * (1.0 / pivot), (SUB, PANEL))
        first = s if r < SUB - 1 else s + 1
        for q in range(first, PANEL // SUB):
            factor = tiles[q][:, j : j + 1]
            tiles[q] = jnp.where(lane_tile == j, 0.0, tiles[q]) - factor * scaled


def factor_kernel(scale, own_cols, rows_moved, pos_ref, pieces_ref, out_ref, work_ref, inv_ref):
    tok_count, gc_count, rows, rank = pieces_ref.shape
    panels = rank // PANEL
    tok_pos, gc_pos = pos_ref[0], pos_ref[1]
    for k in range(tok_count):
        for i in range(gc_count):
            place = ((tok_pos ^ k) * gc_count + (gc_pos ^ i)) * rows
            work_ref[pl.ds(pl.multiple_of(place, SUB), rows), :] = pieces_ref[k, i] * scale

    def panel_step(k, carry):
        here = pl.ds(pl.multiple_of(k * PANEL, PANEL), PANEL)
        diag = work_ref[here, here]

        def store(j, row):
            inv_ref[j : j + 1, :] = row

        eliminate([diag[SUB * q : SUB * (q + 1), :] for q in range(PANEL // SUB)], store)
        inv = inv_ref[...]
        work_ref[here, :] = jnp.dot(
            inv, work_ref[here, :], preferred_element_type=jnp.float32, precision=HIGHEST
        )
        work_ref[here, here] = inv
        for i in range(1, panels):

            @pl.when(i > k)
            def _():
                below = pl.ds(i * PANEL, PANEL)
                work_ref[below, here] = jnp.zeros((PANEL, PANEL), jnp.float32)
                upper = work_ref[here, :]
                work_ref[below, :] -= lax.dot_general(
                    upper[:, i * PANEL : (i + 1) * PANEL],
                    upper,
                    (((0,), (0,)), ((), ())),
                    preferred_element_type=jnp.float32,
                    precision=HIGHEST,
                )

        return carry

    lax.fori_loop(0, panels, panel_step, 0)
    for i in range(panels - 1):
        work_ref[i * PANEL : (i + 1) * PANEL, (i + 1) * PANEL :] = jnp.zeros(
            (PANEL, rank - (i + 1) * PANEL), jnp.float32
        )
    if own_cols == rank:
        out_ref[...] = work_ref[...]
    else:
        for i in range(rank // own_cols):
            row = (tok_pos ^ i) * own_cols if rows_moved else i * own_cols
            for j in range(rank // own_cols):
                col = (tok_pos ^ j) * own_cols
                out_ref[i * own_cols : (i + 1) * own_cols, j * own_cols : (j + 1) * own_cols] = (
                    work_ref[
                        pl.ds(pl.multiple_of(row, PANEL), own_cols),
                        pl.ds(pl.multiple_of(col, PANEL), own_cols),
                    ]
                )


def inverse_factor(pieces, own_cols, rows_moved, scale):
    tok_count, gc_count, rows, rank = pieces.shape
    tok_pos, gc_pos = lax.axis_index("tok"), lax.axis_index("gc")
    aligned = own_cols % PANEL == 0 and rows % SUB == 0
    moved = (
        (tok_pos ^ jnp.arange(tok_count, dtype=jnp.int32))[:, None] * own_cols
        + jnp.arange(own_cols, dtype=jnp.int32)[None, :]
    ).reshape(rank)
    if aligned:
        pos = jnp.stack([tok_pos, gc_pos]).astype(jnp.int32)
    else:
        pos = jnp.zeros((2,), jnp.int32)
        order = (
            (tok_pos ^ jnp.arange(tok_count, dtype=jnp.int32))[:, None] * gc_count
            + (gc_pos ^ jnp.arange(gc_count, dtype=jnp.int32))[None, :]
        ).reshape(-1)
        place = (order[:, None] * rows + jnp.arange(rows, dtype=jnp.int32)[None, :]).reshape(rank)
        full = jnp.zeros((rank, rank), jnp.float32).at[place].set(pieces.reshape(rank, rank))
        pieces = full.reshape(1, 1, rank, rank)
    inverse = pl.pallas_call(
        functools.partial(factor_kernel, scale, own_cols if aligned else rank, rows_moved),
        out_shape=jax.ShapeDtypeStruct((rank, rank), jnp.float32),
        in_specs=[
            pl.BlockSpec(memory_space=pltpu.SMEM),
            pl.BlockSpec(memory_space=pltpu.VMEM),
        ],
        out_specs=pl.BlockSpec(memory_space=pltpu.VMEM),
        scratch_shapes=[
            pltpu.VMEM((rank, rank), jnp.float32),
            pltpu.VMEM((PANEL, PANEL), jnp.float32),
        ],
        compiler_params=pltpu.CompilerParams(vmem_limit_bytes=32 * 1024 * 1024),
        name="inverse_factor",
    )(pos, pieces)
    if not aligned:
        inverse = jnp.take(inverse, moved, axis=1)
        if rows_moved:
            inverse = jnp.take(inverse, moved, axis=0)
    return inverse


def split(value):
    high = lax.reduce_precision(value, 8, 7)
    return high.astype(jnp.bfloat16), (value - high).astype(jnp.bfloat16)


def swap(value, axis, k):
    if k == 0:
        return value
    return lax.ppermute(value, axis, [(i, i ^ k) for i in range(lax.axis_size(axis))])


def collect(value, axis):
    return [swap(value, axis, k) for k in range(lax.axis_size(axis))]


def per_device(acts, init_basis, kept, member):
    owned = init_basis.shape[0]
    slice_rows = init_basis.shape[1]
    rank = init_basis.shape[2]
    tok_count = lax.axis_size("tok")
    gr_count = lax.axis_size("gr")
    gc_count = lax.axis_size("gc")
    block_cols = slice_rows * tok_count
    tok_rows = acts.shape[0]
    total_tokens = tok_rows * tok_count
    groups = kept.shape[0] // GBLK
    assert groups == gr_count == 2
    group_cols = GBLK * block_cols
    own_cols = rank // tok_count
    tok_pos = lax.axis_index("tok")
    gr_pos = lax.axis_index("gr")
    gc_pos = lax.axis_index("gc")
    first = (gr_pos * gc_count + gc_pos) * owned
    links = ((member[:, None] == member[None, :]).astype(jnp.int32) * kept).astype(jnp.float32)
    own_links = lax.dynamic_slice_in_dim(links, first, owned, 0)
    own_groups = lax.dynamic_slice_in_dim(member, first, owned, 0)

    def columns_of(array, k):
        return lax.dynamic_slice_in_dim(
            array, (tok_pos ^ k) * own_cols, own_cols, array.ndim - 1
        )

    init_bf = init_basis.astype(jnp.bfloat16)
    slices = [swap(columns_of(init_bf, k), "tok", k) for k in range(tok_count)]
    own_basis = jnp.concatenate(
        [lax.select_n(tok_pos ^ a, *slices) for a in range(tok_count)], axis=1
    )
    full_x = jnp.concatenate(collect(acts, "tok"), axis=0).reshape(
        total_tokens, owned, block_cols
    )
    basis_bf = lax.all_gather(init_bf, "tok", axis=1, tiled=True)
    basis_bf = jnp.concatenate([columns_of(basis_bf, k) for k in range(tok_count)], axis=2)

    def mix(own_basis):
        proj = jnp.einsum(
            "tob,obr->otr", full_x, own_basis, preferred_element_type=jnp.float32
        ).astype(jnp.bfloat16)
        total = jnp.zeros(proj.shape, jnp.float32)
        for b, near in enumerate(collect(proj, "gc")):
            for a, piece in enumerate(collect(near, "gr")):
                source = ((gr_pos ^ a) * gc_count + (gc_pos ^ b)) * owned
                weights = lax.dynamic_slice_in_dim(own_links, source, owned, 1)
                for j in range(owned):
                    total += weights[:, j][:, None, None] * piece[j][None].astype(jnp.float32)
        return total.astype(jnp.bfloat16)

    def gather_mixed(mixed):
        blocks = mixed.reshape(owned, tok_count, tok_rows, own_cols)
        pieces = []
        for k, piece in enumerate(collect(blocks, "tok")):
            pieces.append(
                jnp.concatenate([piece[:, i ^ k : (i ^ k) + 1] for i in range(tok_count)], axis=1)
            )
        return jnp.concatenate(pieces, axis=3).reshape(owned, total_tokens, rank)

    def factor(image, rows_moved):
        grams = jnp.einsum("obr,obs->ors", image[:, :, :own_cols], image, precision=HIGHEST)

        def group_sum(g):
            mask = (own_groups == g).astype(jnp.float32)
            return jnp.sum(mask[:, None, None] * grams, axis=0)

        total = group_sum(gr_pos) + swap(group_sum(gr_pos ^ 1), "gr", 1)
        rows = own_cols // gc_count

        def rows_of(i):
            return lax.dynamic_slice_in_dim(total, (gc_pos ^ i) * rows, rows, 0)

        piece = sum(swap(rows_of(i), "gc", i) for i in range(gc_count))
        blocks = [piece[:, k * own_cols : (k + 1) * own_cols] for k in range(tok_count)]
        piece = jnp.concatenate(
            [lax.select_n(tok_pos ^ a, *blocks) for a in range(tok_count)], axis=1
        )
        near = jnp.stack(collect(piece, "gc"))
        pieces = jnp.stack(collect(near, "tok"))
        own = inverse_factor(pieces, own_cols, rows_moved, 1.0 / group_cols)
        other = swap(own, "gr", 1)
        of_block = jnp.stack(
            [jnp.where(own_groups[o] == gr_pos, own, other) for o in range(owned)]
        )
        of_group = [jnp.where(gr_pos == g, own, other) for g in range(groups)]
        return of_block, of_group

    for step in range(ITERS):
        mixed = gather_mixed(mix(own_basis))
        cover = jnp.einsum("tob,otr->obr", full_x, mixed, preferred_element_type=jnp.float32)
        image = cover / total_tokens + ridge * basis_bf.astype(jnp.float32)
        of_block, of_group = factor(image, step < ITERS - 1)
        if step < ITERS - 1:
            basis_bf = jnp.einsum("obr,osr->obs", image, of_block, precision=HIGHEST).astype(
                jnp.bfloat16
            )
            own_basis = basis_bf[:, :, :own_cols]
    rows = lax.dynamic_slice_in_dim(image, tok_pos * slice_rows, slice_rows, 1)
    basis = jnp.einsum("obr,osr->obs", rows, of_block, precision=HIGHEST)
    own_x = acts.reshape(tok_rows, owned, block_cols)
    codes = sum(
        jnp.einsum("tob,obr->otr", own_x, part, preferred_element_type=jnp.float32)
        for part in split(image)
    )
    placed = jnp.concatenate(
        [
            jnp.sum((own_groups == g).astype(jnp.float32)[:, None, None] * codes, axis=0)
            for g in range(groups)
        ],
        axis=1,
    )
    placed = lax.psum_scatter(placed, ("gr", "gc"), scatter_dimension=0, tiled=True)
    latent = jnp.concatenate(
        [
            jnp.einsum(
                "tr,sr->ts",
                placed[:, g * rank : (g + 1) * rank],
                of_group[g],
                precision=HIGHEST,
            )
            for g in range(groups)
        ],
        axis=1,
    )
    latent = latent * (1.0 / math.sqrt(group_cols))
    return (basis, latent.astype(jnp.bfloat16))


def solution(mesh):
    placed = (P("tok", ("gr", "gc")), P(("gr", "gc"), "tok", None), P(), P())
    return jax.shard_map(
        per_device,
        mesh=mesh,
        in_specs=placed,
        out_specs=(P(("gr", "gc"), "tok", None), P(("tok", "gr", "gc"), None)),
        check_vma=False,
    )
```

```python
import functools
import math

import jax
import jax.numpy as jnp
from jax import lax
from jax.experimental import pallas as pl
from jax.experimental.pallas import tpu as pltpu
from jax.sharding import PartitionSpec as P

GBLK = 8
ITERS = 2
PANEL = 128
SUB = 8

ridge = 2.0
HIGHEST = lax.Precision.HIGHEST


def reciprocal(value):
    guess = pl.reciprocal(value, approx=True)
    guess = guess * (2.0 - value * guess)
    return guess * (2.0 - value * guess)


def eliminate(tiles, inv_ref):
    shape = (SUB, PANEL)
    lane = lax.broadcasted_iota(jnp.int32, shape, 1)
    sub = lax.broadcasted_iota(jnp.int32, shape, 0)

    def spread(column):
        return jnp.broadcast_to(column, shape)

    tiles = list(tiles)
    for s in range(PANEL // SUB):
        start = s * SUB
        tile = tiles[s]
        inside = (lane >= start) & (lane < start + SUB)
        columns = [spread(tile[:, start + c : start + c + 1]) for c in range(SUB)]
        pivot = [
            [spread(columns[c][i : i + 1, :]) if c >= i else None for c in range(SUB)]
            for i in range(SUB)
        ]
        base = jnp.where(inside, jnp.where(lane == start + sub, 1.0, 0.0), tile)
        rows = [spread(base[i : i + 1, :]) for i in range(SUB)]
        below = [[None] * SUB for _ in range(SUB)]
        inverse = []
        for b in range(SUB):
            inverse.append(reciprocal(pivot[b][b]))
            for i in range(b + 1, SUB):
                factor = pivot[b][i] * inverse[b]
                below[i][b] = factor
                for c in range(i, SUB):
                    pivot[i][c] = pivot[i][c] - factor * pivot[b][c]
                rows[i] = rows[i] - factor * rows[b]
        result = jnp.zeros(shape, jnp.float32)
        for b in range(SUB):
            root = lax.rsqrt(pivot[b][b])
            root = root * (1.5 - 0.5 * pivot[b][b] * root * root)
            result = jnp.where(sub == b, rows[b] * root, result)
        inv_ref[start : start + SUB, :] = jnp.where(lane < start + SUB, result, 0.0)
        solved = [None] * SUB
        for b in reversed(range(SUB)):
            value = rows[b] * inverse[b]
            for i in reversed(range(b + 1, SUB)):
                value = value - below[i][b] * solved[i]
            solved[b] = value
        for q in range(s + 1, PANEL // SUB):
            parts = [
                spread(tiles[q][:, start + b : start + b + 1]) * solved[b] for b in range(SUB)
            ]
            while len(parts) > 1:
                parts = [x + y for x, y in zip(parts[::2], parts[1::2])]
            tiles[q] = jnp.where(inside, 0.0, tiles[q]) - parts[0]


def factor_kernel(scale, own_cols, rows_moved, pos_ref, pieces_ref, out_ref, work_ref, inv_ref):
    tok_count, gc_count, rows, rank = pieces_ref.shape
    panels = rank // PANEL
    tok_pos, gc_pos = pos_ref[0], pos_ref[1]
    for k in range(tok_count):
        for i in range(gc_count):
            place = ((tok_pos ^ k) * gc_count + (gc_pos ^ i)) * rows
            work_ref[pl.ds(pl.multiple_of(place, SUB), rows), :] = pieces_ref[k, i] * scale

    def panel_step(k, carry):
        here = pl.ds(pl.multiple_of(k * PANEL, PANEL), PANEL)
        diag = work_ref[here, here]

        eliminate([diag[SUB * q : SUB * (q + 1), :] for q in range(PANEL // SUB)], inv_ref)
        inv = inv_ref[...]
        work_ref[here, :] = jnp.dot(
            inv, work_ref[here, :], preferred_element_type=jnp.float32, precision=HIGHEST
        )
        work_ref[here, here] = inv
        for i in range(1, panels):

            @pl.when(i > k)
            def _():
                below = pl.ds(i * PANEL, PANEL)
                work_ref[below, here] = jnp.zeros((PANEL, PANEL), jnp.float32)
                upper = work_ref[here, :]
                work_ref[below, :] -= lax.dot_general(
                    upper[:, i * PANEL : (i + 1) * PANEL],
                    upper,
                    (((0,), (0,)), ((), ())),
                    preferred_element_type=jnp.float32,
                    precision=HIGHEST,
                )

        return carry

    lax.fori_loop(0, panels, panel_step, 0)
    for i in range(panels - 1):
        work_ref[i * PANEL : (i + 1) * PANEL, (i + 1) * PANEL :] = jnp.zeros(
            (PANEL, rank - (i + 1) * PANEL), jnp.float32
        )
    if own_cols == rank:
        out_ref[...] = work_ref[...]
    else:
        for i in range(rank // own_cols):
            row = (tok_pos ^ i) * own_cols if rows_moved else i * own_cols
            for j in range(rank // own_cols):
                col = (tok_pos ^ j) * own_cols
                out_ref[i * own_cols : (i + 1) * own_cols, j * own_cols : (j + 1) * own_cols] = (
                    work_ref[
                        pl.ds(pl.multiple_of(row, PANEL), own_cols),
                        pl.ds(pl.multiple_of(col, PANEL), own_cols),
                    ]
                )


def inverse_factor(pieces, own_cols, rows_moved, scale):
    tok_count, gc_count, rows, rank = pieces.shape
    tok_pos, gc_pos = lax.axis_index("tok"), lax.axis_index("gc")
    aligned = own_cols % PANEL == 0 and rows % SUB == 0
    moved = (
        (tok_pos ^ jnp.arange(tok_count, dtype=jnp.int32))[:, None] * own_cols
        + jnp.arange(own_cols, dtype=jnp.int32)[None, :]
    ).reshape(rank)
    if aligned:
        pos = jnp.stack([tok_pos, gc_pos]).astype(jnp.int32)
    else:
        pos = jnp.zeros((2,), jnp.int32)
        order = (
            (tok_pos ^ jnp.arange(tok_count, dtype=jnp.int32))[:, None] * gc_count
            + (gc_pos ^ jnp.arange(gc_count, dtype=jnp.int32))[None, :]
        ).reshape(-1)
        place = (order[:, None] * rows + jnp.arange(rows, dtype=jnp.int32)[None, :]).reshape(rank)
        full = jnp.zeros((rank, rank), jnp.float32).at[place].set(pieces.reshape(rank, rank))
        pieces = full.reshape(1, 1, rank, rank)
    inverse = pl.pallas_call(
        functools.partial(factor_kernel, scale, own_cols if aligned else rank, rows_moved),
        out_shape=jax.ShapeDtypeStruct((rank, rank), jnp.float32),
        in_specs=[
            pl.BlockSpec(memory_space=pltpu.SMEM),
            pl.BlockSpec(memory_space=pltpu.VMEM),
        ],
        out_specs=pl.BlockSpec(memory_space=pltpu.VMEM),
        scratch_shapes=[
            pltpu.VMEM((rank, rank), jnp.float32),
            pltpu.VMEM((PANEL, PANEL), jnp.float32),
        ],
        compiler_params=pltpu.CompilerParams(vmem_limit_bytes=32 * 1024 * 1024),
        name="inverse_factor",
    )(pos, pieces)
    if not aligned:
        inverse = jnp.take(inverse, moved, axis=1)
        if rows_moved:
            inverse = jnp.take(inverse, moved, axis=0)
    return inverse


def split(value):
    high = lax.reduce_precision(value, 8, 7)
    return high.astype(jnp.bfloat16), (value - high).astype(jnp.bfloat16)


def swap(value, axis, k):
    if k == 0:
        return value
    return lax.ppermute(value, axis, [(i, i ^ k) for i in range(lax.axis_size(axis))])


def collect(value, axis):
    return [swap(value, axis, k) for k in range(lax.axis_size(axis))]


def per_device(acts, init_basis, kept, member):
    owned = init_basis.shape[0]
    slice_rows = init_basis.shape[1]
    rank = init_basis.shape[2]
    tok_count = lax.axis_size("tok")
    gr_count = lax.axis_size("gr")
    gc_count = lax.axis_size("gc")
    block_cols = slice_rows * tok_count
    tok_rows = acts.shape[0]
    total_tokens = tok_rows * tok_count
    groups = kept.shape[0] // GBLK
    assert groups == gr_count == 2
    group_cols = GBLK * block_cols
    own_cols = rank // tok_count
    tok_pos = lax.axis_index("tok")
    gr_pos = lax.axis_index("gr")
    gc_pos = lax.axis_index("gc")
    first = (gr_pos * gc_count + gc_pos) * owned
    links = ((member[:, None] == member[None, :]).astype(jnp.int32) * kept).astype(jnp.float32)
    own_links = lax.dynamic_slice_in_dim(links, first, owned, 0)
    own_groups = lax.dynamic_slice_in_dim(member, first, owned, 0)

    def columns_of(array, k):
        return lax.dynamic_slice_in_dim(
            array, (tok_pos ^ k) * own_cols, own_cols, array.ndim - 1
        )

    init_bf = init_basis.astype(jnp.bfloat16)
    slices = [swap(columns_of(init_bf, k), "tok", k) for k in range(tok_count)]
    own_basis = jnp.concatenate(
        [lax.select_n(tok_pos ^ a, *slices) for a in range(tok_count)], axis=1
    )
    acts_pieces = collect(acts, "tok")
    acts_pieces, init_late = lax.optimization_barrier((acts_pieces, init_bf))
    full_x = jnp.concatenate(acts_pieces, axis=0).reshape(total_tokens, owned, block_cols)
    basis_bf = lax.all_gather(init_late, "tok", axis=1, tiled=True)
    basis_bf = jnp.concatenate([columns_of(basis_bf, k) for k in range(tok_count)], axis=2)

    def mix(own_basis):
        proj = jnp.einsum(
            "tob,obr->otr", full_x, own_basis, preferred_element_type=jnp.float32
        ).astype(jnp.bfloat16)
        total = jnp.zeros(proj.shape, jnp.float32)
        for b, near in enumerate(collect(proj, "gc")):
            for a, piece in enumerate(collect(near, "gr")):
                source = ((gr_pos ^ a) * gc_count + (gc_pos ^ b)) * owned
                weights = lax.dynamic_slice_in_dim(own_links, source, owned, 1)
                for j in range(owned):
                    total += weights[:, j][:, None, None] * piece[j][None].astype(jnp.float32)
        return total.astype(jnp.bfloat16)

    def gather_mixed(mixed):
        blocks = mixed.reshape(owned, tok_count, tok_rows, own_cols)
        pieces = []
        for k, piece in enumerate(collect(blocks, "tok")):
            pieces.append(
                jnp.concatenate([piece[:, i ^ k : (i ^ k) + 1] for i in range(tok_count)], axis=1)
            )
        return jnp.concatenate(pieces, axis=3).reshape(owned, total_tokens, rank)

    def factor(image, rows_moved):
        grams = jnp.einsum("obr,obs->ors", image[:, :, :own_cols], image, precision=HIGHEST)

        def group_sum(g):
            mask = (own_groups == g).astype(jnp.float32)
            return jnp.sum(mask[:, None, None] * grams, axis=0)

        total = group_sum(gr_pos) + swap(group_sum(gr_pos ^ 1), "gr", 1)
        rows = own_cols // gc_count

        def rows_of(i):
            return lax.dynamic_slice_in_dim(total, (gc_pos ^ i) * rows, rows, 0)

        piece = sum(swap(rows_of(i), "gc", i) for i in range(gc_count))
        blocks = [piece[:, k * own_cols : (k + 1) * own_cols] for k in range(tok_count)]
        piece = jnp.concatenate(
            [lax.select_n(tok_pos ^ a, *blocks) for a in range(tok_count)], axis=1
        )
        near = jnp.stack(collect(piece, "gc"))
        pieces = jnp.stack(collect(near, "tok"))
        own = inverse_factor(pieces, own_cols, rows_moved, 1.0 / group_cols)
        other = swap(own, "gr", 1)
        of_block = jnp.stack(
            [jnp.where(own_groups[o] == gr_pos, own, other) for o in range(owned)]
        )
        of_group = [jnp.where(gr_pos == g, own, other) for g in range(groups)]
        return of_block, of_group

    for step in range(ITERS):
        mixed = gather_mixed(mix(own_basis))
        cover = jnp.einsum("tob,otr->obr", full_x, mixed, preferred_element_type=jnp.float32)
        image = cover / total_tokens + ridge * basis_bf.astype(jnp.float32)
        of_block, of_group = factor(image, step < ITERS - 1)
        if step < ITERS - 1:
            own_basis = jnp.einsum(
                "obr,osr->obs", image, of_block[:, :own_cols], precision=HIGHEST
            ).astype(jnp.bfloat16)
            other_basis = jnp.einsum(
                "obr,osr->obs", image, of_block[:, own_cols:], precision=HIGHEST
            ).astype(jnp.bfloat16)
            basis_bf = jnp.concatenate([own_basis, other_basis], axis=2)
    rows = lax.dynamic_slice_in_dim(image, tok_pos * slice_rows, slice_rows, 1)
    basis = jnp.einsum("obr,osr->obs", rows, of_block, precision=HIGHEST)
    own_x = acts.reshape(tok_rows, owned, block_cols)
    codes = sum(
        jnp.einsum("tob,obr->otr", own_x, part, preferred_element_type=jnp.float32)
        for part in split(image)
    )
    placed = jnp.concatenate(
        [
            jnp.sum((own_groups == g).astype(jnp.float32)[:, None, None] * codes, axis=0)
            for g in range(groups)
        ],
        axis=1,
    )
    placed = lax.psum_scatter(placed, ("gr", "gc"), scatter_dimension=0, tiled=True)
    latent = jnp.concatenate(
        [
            jnp.einsum(
                "tr,sr->ts",
                placed[:, g * rank : (g + 1) * rank],
                of_group[g],
                precision=HIGHEST,
            )
            for g in range(groups)
        ],
        axis=1,
    )
    latent = latent * (1.0 / math.sqrt(group_cols))
    return (basis, latent.astype(jnp.bfloat16))


def solution(mesh):
    placed = (P("tok", ("gr", "gc")), P(("gr", "gc"), "tok", None), P(), P())
    return jax.shard_map(
        per_device,
        mesh=mesh,
        in_specs=placed,
        out_specs=(P(("gr", "gc"), "tok", None), P(("tok", "gr", "gc"), None)),
        check_vma=False,
    )
```

```python
import functools
import math

import jax
import jax.numpy as jnp
from jax import lax
from jax.experimental import pallas as pl
from jax.experimental.pallas import tpu as pltpu
from jax.sharding import PartitionSpec as P

GBLK = 8
ITERS = 2
PANEL = 128
SUB = 8

ridge = 2.0
HIGHEST = lax.Precision.HIGHEST
HIGH = lax.Precision.HIGH


def split(value):
    high = lax.reduce_precision(value, 8, 7)
    return high.astype(jnp.bfloat16), (value - high).astype(jnp.bfloat16)


def kernel_dot(left, right, exact):
    if exact:
        return jnp.dot(left, right, preferred_element_type=jnp.float32, precision=HIGHEST)
    parts = []
    for value in (left, right):
        high = value.astype(jnp.bfloat16)
        parts.append((high, (value - high.astype(jnp.float32)).astype(jnp.bfloat16)))
    (a, b), (c, d) = parts
    return sum(
        jnp.dot(x, y, preferred_element_type=jnp.float32) for x, y in ((b, c), (a, d), (a, c))
    )


def eliminate(tiles, inv_ref):
    shape = (SUB, PANEL)
    lane = lax.broadcasted_iota(jnp.int32, shape, 1)
    sub = lax.broadcasted_iota(jnp.int32, shape, 0)

    def spread(column):
        return jnp.broadcast_to(column, shape)

    tiles = list(tiles)
    for s in range(PANEL // SUB):
        start = s * SUB
        tile = tiles[s]
        inside = (lane >= start) & (lane < start + SUB)
        columns = [spread(tile[:, start + c : start + c + 1]) for c in range(SUB)]
        pivot = [
            [spread(columns[c][i : i + 1, :]) if c >= i else None for c in range(SUB)]
            for i in range(SUB)
        ]
        base = jnp.where(inside, jnp.where(lane == start + sub, 1.0, 0.0), tile)
        rows = [spread(base[i : i + 1, :]) for i in range(SUB)]
        below = [[None] * SUB for _ in range(SUB)]
        inverse = []
        for b in range(SUB):
            inverse.append(pl.reciprocal(pivot[b][b], approx=True))
            for i in range(b + 1, SUB):
                factor = pivot[b][i] * inverse[b]
                below[i][b] = factor
                for c in range(i, SUB):
                    pivot[i][c] = pivot[i][c] - factor * pivot[b][c]
                rows[i] = rows[i] - factor * rows[b]
        result = jnp.zeros(shape, jnp.float32)
        for b in range(SUB):
            result = jnp.where(sub == b, rows[b] * lax.rsqrt(pivot[b][b]), result)
        inv_ref[start : start + SUB, :] = jnp.where(lane < start + SUB, result, 0.0)
        solved = [None] * SUB
        for b in reversed(range(SUB)):
            value = rows[b] * inverse[b]
            for i in reversed(range(b + 1, SUB)):
                value = value - below[i][b] * solved[i]
            solved[b] = value
        for q in range(s + 1, PANEL // SUB):
            parts = [
                spread(tiles[q][:, start + b : start + b + 1]) * solved[b] for b in range(SUB)
            ]
            while len(parts) > 1:
                parts = [x + y for x, y in zip(parts[::2], parts[1::2])]
            tiles[q] = jnp.where(inside, 0.0, tiles[q]) - parts[0]


def factor_kernel(scale, own_cols, rows_moved, exact, pos_ref, pieces_ref, out_ref, work_ref, inv_ref):
    tok_count, gc_count, rows, rank = pieces_ref.shape
    panels = rank // PANEL
    tok_pos, gc_pos = pos_ref[0], pos_ref[1]
    for k in range(tok_count):
        for i in range(gc_count):
            place = ((tok_pos ^ k) * gc_count + (gc_pos ^ i)) * rows
            work_ref[pl.ds(pl.multiple_of(place, SUB), rows), :] = pieces_ref[k, i] * scale

    def panel_step(k, carry):
        here = pl.ds(pl.multiple_of(k * PANEL, PANEL), PANEL)
        diag = work_ref[here, here]

        eliminate([diag[SUB * q : SUB * (q + 1), :] for q in range(PANEL // SUB)], inv_ref)
        for here_k in range(panels):

            @pl.when(k == here_k)
            def _():
                panel = slice(here_k * PANEL, (here_k + 1) * PANEL)
                rest = slice((here_k + 1) * PANEL, rank)
                inv = inv_ref[...]
                work_ref[panel, :] = kernel_dot(inv, work_ref[panel, :], exact)
                work_ref[panel, panel] = inv
                if here_k < panels - 1:
                    lower = work_ref[panel, rest].T
                    work_ref[rest, panel] = jnp.zeros((rank - rest.start, PANEL), jnp.float32)
                    work_ref[rest, :] -= kernel_dot(lower, work_ref[panel, :], exact)

        return carry

    lax.fori_loop(0, panels, panel_step, 0)
    for i in range(panels - 1):
        work_ref[i * PANEL : (i + 1) * PANEL, (i + 1) * PANEL :] = jnp.zeros(
            (PANEL, rank - (i + 1) * PANEL), jnp.float32
        )
    if own_cols == rank:
        out_ref[...] = work_ref[...]
    else:
        for i in range(rank // own_cols):
            row = (tok_pos ^ i) * own_cols if rows_moved else i * own_cols
            for j in range(rank // own_cols):
                col = (tok_pos ^ j) * own_cols
                out_ref[i * own_cols : (i + 1) * own_cols, j * own_cols : (j + 1) * own_cols] = (
                    work_ref[
                        pl.ds(pl.multiple_of(row, PANEL), own_cols),
                        pl.ds(pl.multiple_of(col, PANEL), own_cols),
                    ]
                )


def inverse_factor(pieces, own_cols, rows_moved, exact, scale):
    tok_count, gc_count, rows, rank = pieces.shape
    tok_pos, gc_pos = lax.axis_index("tok"), lax.axis_index("gc")
    aligned = own_cols % PANEL == 0 and rows % SUB == 0
    moved = (
        (tok_pos ^ jnp.arange(tok_count, dtype=jnp.int32))[:, None] * own_cols
        + jnp.arange(own_cols, dtype=jnp.int32)[None, :]
    ).reshape(rank)
    if aligned:
        pos = jnp.stack([tok_pos, gc_pos]).astype(jnp.int32)
    else:
        pos = jnp.zeros((2,), jnp.int32)
        order = (
            (tok_pos ^ jnp.arange(tok_count, dtype=jnp.int32))[:, None] * gc_count
            + (gc_pos ^ jnp.arange(gc_count, dtype=jnp.int32))[None, :]
        ).reshape(-1)
        place = (order[:, None] * rows + jnp.arange(rows, dtype=jnp.int32)[None, :]).reshape(rank)
        full = jnp.zeros((rank, rank), jnp.float32).at[place].set(pieces.reshape(rank, rank))
        pieces = full.reshape(1, 1, rank, rank)
    inverse = pl.pallas_call(
        functools.partial(factor_kernel, scale, own_cols if aligned else rank, rows_moved, exact),
        out_shape=jax.ShapeDtypeStruct((rank, rank), jnp.float32),
        in_specs=[
            pl.BlockSpec(memory_space=pltpu.SMEM),
            pl.BlockSpec(memory_space=pltpu.VMEM),
        ],
        out_specs=pl.BlockSpec(memory_space=pltpu.VMEM),
        scratch_shapes=[
            pltpu.VMEM((rank, rank), jnp.float32),
            pltpu.VMEM((PANEL, PANEL), jnp.float32),
        ],
        compiler_params=pltpu.CompilerParams(vmem_limit_bytes=32 * 1024 * 1024),
        name="inverse_factor",
    )(pos, pieces)
    if not aligned:
        inverse = jnp.take(inverse, moved, axis=1)
        if rows_moved:
            inverse = jnp.take(inverse, moved, axis=0)
    return inverse


def swap(value, axis, k):
    if k == 0:
        return value
    return lax.ppermute(value, axis, [(i, i ^ k) for i in range(lax.axis_size(axis))])


def collect(value, axis):
    return [swap(value, axis, k) for k in range(lax.axis_size(axis))]


def collect_relayed(value, axis):
    if lax.axis_size(axis) != 4:
        return collect(value, axis)
    half = value.shape[0] // 2
    near, side = swap(value, axis, 1), swap(value, axis, 2)
    far = [swap(side[:half], axis, 1), swap(near[half:], axis, 2)]
    return [value, near, side, jnp.concatenate(far, axis=0)]


def per_device(acts, init_basis, kept, member):
    owned = init_basis.shape[0]
    slice_rows = init_basis.shape[1]
    rank = init_basis.shape[2]
    tok_count = lax.axis_size("tok")
    gr_count = lax.axis_size("gr")
    gc_count = lax.axis_size("gc")
    block_cols = slice_rows * tok_count
    tok_rows = acts.shape[0]
    total_tokens = tok_rows * tok_count
    groups = kept.shape[0] // GBLK
    assert groups == gr_count == 2
    group_cols = GBLK * block_cols
    own_cols = rank // tok_count
    tok_pos = lax.axis_index("tok")
    gr_pos = lax.axis_index("gr")
    gc_pos = lax.axis_index("gc")
    first = (gr_pos * gc_count + gc_pos) * owned
    links = ((member[:, None] == member[None, :]).astype(jnp.int32) * kept).astype(jnp.float32)
    own_links = lax.dynamic_slice_in_dim(links, first, owned, 0)
    own_groups = lax.dynamic_slice_in_dim(member, first, owned, 0)

    def columns_of(array, k):
        return lax.dynamic_slice_in_dim(
            array, (tok_pos ^ k) * own_cols, own_cols, array.ndim - 1
        )

    init_bf = init_basis.astype(jnp.bfloat16)
    slices = [swap(columns_of(init_bf, k), "tok", k) for k in range(tok_count)]
    own_basis = jnp.concatenate(
        [lax.select_n(tok_pos ^ a, *slices) for a in range(tok_count)], axis=1
    )
    acts_pieces = collect_relayed(acts, "tok")
    early = 3 * len(acts_pieces) // 4
    acts_pieces[-1], init_late = lax.optimization_barrier((acts_pieces[-1], init_bf))
    chunks = [
        jnp.concatenate(part, axis=0).reshape(-1, owned, block_cols)
        for part in (acts_pieces[:early], acts_pieces[early:])
    ]
    full_x = jnp.concatenate(acts_pieces, axis=0).reshape(total_tokens, owned, block_cols)
    init_pieces = collect(init_late, "tok")
    basis_bf = jnp.concatenate(
        [lax.select_n(tok_pos ^ a, *init_pieces) for a in range(tok_count)], axis=1
    )
    basis_bf = jnp.concatenate([columns_of(basis_bf, k) for k in range(tok_count)], axis=2)

    def mix(x, own_basis):
        proj = jnp.einsum(
            "tob,obr->otr", x, own_basis, preferred_element_type=jnp.float32
        ).astype(jnp.bfloat16)
        total = jnp.zeros(proj.shape, jnp.float32)
        near = collect(proj, "gc")
        across = swap(jnp.stack(near), "gr", 1)
        for a in range(gr_count):
            for b in range(gc_count):
                piece = across[b] if a else near[b]
                source = ((gr_pos ^ a) * gc_count + (gc_pos ^ b)) * owned
                weights = lax.dynamic_slice_in_dim(own_links, source, owned, 1)
                for j in range(owned):
                    total += weights[:, j][:, None, None] * piece[j][None].astype(jnp.float32)
        return total.astype(jnp.bfloat16)

    def gather_mixed(mixed):
        blocks = mixed.reshape(owned, tok_count, tok_rows, own_cols)
        pieces = []
        for k, piece in enumerate(collect(blocks, "tok")):
            pieces.append(
                jnp.concatenate([piece[:, i ^ k : (i ^ k) + 1] for i in range(tok_count)], axis=1)
            )
        return jnp.concatenate(pieces, axis=3).reshape(owned, total_tokens, rank)

    def factor(image, last):
        precision = HIGHEST if last else HIGH
        grams = jnp.einsum("obr,obs->ors", image[:, :, :own_cols], image, precision=precision)

        def group_sum(g):
            mask = (own_groups == g).astype(jnp.float32)
            return jnp.sum(mask[:, None, None] * grams, axis=0)

        total = group_sum(gr_pos) + swap(group_sum(gr_pos ^ 1), "gr", 1)
        rows = own_cols // gc_count

        def rows_of(i):
            return lax.dynamic_slice_in_dim(total, (gc_pos ^ i) * rows, rows, 0)

        piece = sum(swap(rows_of(i), "gc", i) for i in range(gc_count))
        blocks = [piece[:, k * own_cols : (k + 1) * own_cols] for k in range(tok_count)]
        piece = jnp.concatenate(
            [lax.select_n(tok_pos ^ a, *blocks) for a in range(tok_count)], axis=1
        )
        near = jnp.stack(collect(piece, "gc"))
        pieces = jnp.stack(collect(near, "tok"))
        own = inverse_factor(pieces, own_cols, not last, last, 1.0 / group_cols)
        other = swap(own, "gr", 1)
        of_block = jnp.stack(
            [jnp.where(own_groups[o] == gr_pos, own, other) for o in range(owned)]
        )
        of_group = [jnp.where(gr_pos == g, own, other) for g in range(groups)]
        return of_block, of_group

    for step in range(ITERS):
        if step == 0:
            mixed = jnp.concatenate([mix(x, own_basis) for x in chunks], axis=1)
        else:
            mixed = mix(full_x, own_basis)
        mixed = gather_mixed(mixed)
        cover = jnp.einsum("tob,otr->obr", full_x, mixed, preferred_element_type=jnp.float32)
        image = cover / total_tokens + ridge * basis_bf.astype(jnp.float32)
        of_block, of_group = factor(image, step == ITERS - 1)
        if step < ITERS - 1:
            own_basis = jnp.einsum(
                "obr,osr->obs", image, of_block[:, :own_cols], precision=HIGH
            ).astype(jnp.bfloat16)
            other_basis = jnp.einsum(
                "obr,osr->obs", image, of_block[:, own_cols:], precision=HIGH
            ).astype(jnp.bfloat16)
            basis_bf = jnp.concatenate([own_basis, other_basis], axis=2)
    rows = lax.dynamic_slice_in_dim(image, tok_pos * slice_rows, slice_rows, 1)
    basis = jnp.einsum("obr,osr->obs", rows, of_block, precision=HIGH)
    own_x = acts.reshape(tok_rows, owned, block_cols)
    codes = sum(
        jnp.einsum("tob,obr->otr", own_x, part, preferred_element_type=jnp.float32)
        for part in split(image)
    )
    placed = jnp.concatenate(
        [
            jnp.sum((own_groups == g).astype(jnp.float32)[:, None, None] * codes, axis=0)
            for g in range(groups)
        ],
        axis=1,
    )
    placed = lax.psum_scatter(placed, ("gr", "gc"), scatter_dimension=0, tiled=True)
    latent = jnp.concatenate(
        [
            jnp.einsum(
                "tr,sr->ts",
                placed[:, g * rank : (g + 1) * rank],
                of_group[g],
                precision=HIGH,
            )
            for g in range(groups)
        ],
        axis=1,
    )
    latent = latent * (1.0 / math.sqrt(group_cols))
    return (basis, latent.astype(jnp.bfloat16))


def solution(mesh):
    placed = (P("tok", ("gr", "gc")), P(("gr", "gc"), "tok", None), P(), P())
    return jax.shard_map(
        per_device,
        mesh=mesh,
        in_specs=placed,
        out_specs=(P(("gr", "gc"), "tok", None), P(("tok", "gr", "gc"), None)),
        check_vma=False,
    )
```

```python
import functools
import math

import jax
import jax.numpy as jnp
from jax import lax
from jax.experimental import pallas as pl
from jax.experimental.pallas import tpu as pltpu
from jax.sharding import PartitionSpec as P

GBLK = 8
PANEL = 128
SUB = 8

ridge = 2.0
HIGHEST = lax.Precision.HIGHEST
HIGH = lax.Precision.HIGH


def split(value):
    high = lax.reduce_precision(value, 8, 7)
    return high.astype(jnp.bfloat16), (value - high).astype(jnp.bfloat16)


def kernel_dot(left, right, exact):
    if exact:
        return jnp.dot(left, right, preferred_element_type=jnp.float32, precision=HIGHEST)
    parts = []
    for value in (left, right):
        high = value.astype(jnp.bfloat16)
        parts.append((high, (value - high.astype(jnp.float32)).astype(jnp.bfloat16)))
    (a, b), (c, d) = parts
    return sum(
        jnp.dot(x, y, preferred_element_type=jnp.float32) for x, y in ((b, c), (a, d), (a, c))
    )


def eliminate(tiles, inv_ref):
    shape = (SUB, PANEL)
    lane = lax.broadcasted_iota(jnp.int32, shape, 1)
    sub = lax.broadcasted_iota(jnp.int32, shape, 0)

    def spread(column):
        return jnp.broadcast_to(column, shape)

    tiles = list(tiles)
    for s in range(PANEL // SUB):
        start = s * SUB
        tile = tiles[s]
        inside = (lane >= start) & (lane < start + SUB)
        columns = [spread(tile[:, start + c : start + c + 1]) for c in range(SUB)]
        pivot = [
            [spread(columns[c][i : i + 1, :]) if c >= i else None for c in range(SUB)]
            for i in range(SUB)
        ]
        base = jnp.where(inside, jnp.where(lane == start + sub, 1.0, 0.0), tile)
        rows = [spread(base[i : i + 1, :]) for i in range(SUB)]
        below = [[None] * SUB for _ in range(SUB)]
        inverse = []
        for b in range(SUB):
            inverse.append(pl.reciprocal(pivot[b][b], approx=True))
            for i in range(b + 1, SUB):
                factor = pivot[b][i] * inverse[b]
                below[i][b] = factor
                for c in range(i, SUB):
                    pivot[i][c] = pivot[i][c] - factor * pivot[b][c]
                rows[i] = rows[i] - factor * rows[b]
        result = jnp.zeros(shape, jnp.float32)
        for b in range(SUB):
            result = jnp.where(sub == b, rows[b] * lax.rsqrt(pivot[b][b]), result)
        inv_ref[start : start + SUB, :] = jnp.where(lane < start + SUB, result, 0.0)
        solved = [None] * SUB
        for b in reversed(range(SUB)):
            value = rows[b] * inverse[b]
            for i in reversed(range(b + 1, SUB)):
                value = value - below[i][b] * solved[i]
            solved[b] = value
        for q in range(s + 1, PANEL // SUB):
            parts = [
                spread(tiles[q][:, start + b : start + b + 1]) * solved[b] for b in range(SUB)
            ]
            while len(parts) > 1:
                parts = [x + y for x, y in zip(parts[::2], parts[1::2])]
            tiles[q] = jnp.where(inside, 0.0, tiles[q]) - parts[0]


def factor_kernel(scale, own_cols, rows_moved, exact, pos_ref, pieces_ref, out_ref, work_ref, inv_ref):
    tok_count, gc_count, rows, rank = pieces_ref.shape
    panels = rank // PANEL
    tok_pos, gc_pos = pos_ref[0], pos_ref[1]
    for k in range(tok_count):
        for i in range(gc_count):
            place = ((tok_pos ^ k) * gc_count + (gc_pos ^ i)) * rows
            work_ref[pl.ds(pl.multiple_of(place, SUB), rows), :] = pieces_ref[k, i] * scale

    def panel_step(k, carry):
        here = pl.ds(pl.multiple_of(k * PANEL, PANEL), PANEL)
        diag = work_ref[here, here]

        eliminate([diag[SUB * q : SUB * (q + 1), :] for q in range(PANEL // SUB)], inv_ref)
        for here_k in range(panels):

            @pl.when(k == here_k)
            def _():
                panel = slice(here_k * PANEL, (here_k + 1) * PANEL)
                rest = slice((here_k + 1) * PANEL, rank)
                inv = inv_ref[...]
                work_ref[panel, :] = kernel_dot(inv, work_ref[panel, :], exact)
                work_ref[panel, panel] = inv
                if here_k < panels - 1:
                    lower = work_ref[panel, rest].T
                    work_ref[rest, panel] = jnp.zeros((rank - rest.start, PANEL), jnp.float32)
                    work_ref[rest, :] -= kernel_dot(lower, work_ref[panel, :], exact)

        return carry

    lax.fori_loop(0, panels, panel_step, 0)
    for i in range(panels - 1):
        work_ref[i * PANEL : (i + 1) * PANEL, (i + 1) * PANEL :] = jnp.zeros(
            (PANEL, rank - (i + 1) * PANEL), jnp.float32
        )
    if own_cols == rank:
        out_ref[...] = work_ref[...]
    else:
        for i in range(rank // own_cols):
            row = (tok_pos ^ i) * own_cols if rows_moved else i * own_cols
            for j in range(rank // own_cols):
                col = (tok_pos ^ j) * own_cols
                out_ref[i * own_cols : (i + 1) * own_cols, j * own_cols : (j + 1) * own_cols] = (
                    work_ref[
                        pl.ds(pl.multiple_of(row, PANEL), own_cols),
                        pl.ds(pl.multiple_of(col, PANEL), own_cols),
                    ]
                )


def inverse_factor(pieces, own_cols, rows_moved, exact, scale):
    tok_count, gc_count, rows, rank = pieces.shape
    tok_pos, gc_pos = lax.axis_index("tok"), lax.axis_index("gc")
    aligned = own_cols % PANEL == 0 and rows % SUB == 0
    moved = (
        (tok_pos ^ jnp.arange(tok_count, dtype=jnp.int32))[:, None] * own_cols
        + jnp.arange(own_cols, dtype=jnp.int32)[None, :]
    ).reshape(rank)
    if aligned:
        pos = jnp.stack([tok_pos, gc_pos]).astype(jnp.int32)
    else:
        pos = jnp.zeros((2,), jnp.int32)
        order = (
            (tok_pos ^ jnp.arange(tok_count, dtype=jnp.int32))[:, None] * gc_count
            + (gc_pos ^ jnp.arange(gc_count, dtype=jnp.int32))[None, :]
        ).reshape(-1)
        place = (order[:, None] * rows + jnp.arange(rows, dtype=jnp.int32)[None, :]).reshape(rank)
        full = jnp.zeros((rank, rank), jnp.float32).at[place].set(pieces.reshape(rank, rank))
        pieces = full.reshape(1, 1, rank, rank)
    inverse = pl.pallas_call(
        functools.partial(factor_kernel, scale, own_cols if aligned else rank, rows_moved, exact),
        out_shape=jax.ShapeDtypeStruct((rank, rank), jnp.float32),
        in_specs=[
            pl.BlockSpec(memory_space=pltpu.SMEM),
            pl.BlockSpec(memory_space=pltpu.VMEM),
        ],
        out_specs=pl.BlockSpec(memory_space=pltpu.VMEM),
        scratch_shapes=[
            pltpu.VMEM((rank, rank), jnp.float32),
            pltpu.VMEM((PANEL, PANEL), jnp.float32),
        ],
        compiler_params=pltpu.CompilerParams(vmem_limit_bytes=32 * 1024 * 1024),
        cost_estimate=pl.CostEstimate(
            flops=96 * rank**3, bytes_accessed=8 * rank**2, transcendentals=0
        ),
        name="inverse_factor",
    )(pos, pieces)
    if not aligned:
        inverse = jnp.take(inverse, moved, axis=1)
        if rows_moved:
            inverse = jnp.take(inverse, moved, axis=0)
    return inverse


def swap(value, axis, k):
    if k == 0:
        return value
    return lax.ppermute(value, axis, [(i, i ^ k) for i in range(lax.axis_size(axis))])


def collect(value, axis):
    return [swap(value, axis, k) for k in range(lax.axis_size(axis))]


def per_device(acts, init_basis, kept, member):
    owned = init_basis.shape[0]
    slice_rows = init_basis.shape[1]
    rank = init_basis.shape[2]
    tok_count = lax.axis_size("tok")
    gr_count = lax.axis_size("gr")
    gc_count = lax.axis_size("gc")
    block_cols = slice_rows * tok_count
    tok_rows = acts.shape[0]
    total_tokens = tok_rows * tok_count
    groups = kept.shape[0] // GBLK
    assert groups == gr_count == 2
    group_cols = GBLK * block_cols
    own_cols = rank // tok_count
    tok_pos = lax.axis_index("tok")
    gr_pos = lax.axis_index("gr")
    gc_pos = lax.axis_index("gc")
    first = (gr_pos * gc_count + gc_pos) * owned
    links = ((member[:, None] == member[None, :]).astype(jnp.int32) * kept).astype(jnp.float32)
    own_links = lax.dynamic_slice_in_dim(links, first, owned, 0)
    partner = ((gr_pos ^ 1) * gc_count + gc_pos) * owned
    partner_links = lax.dynamic_slice_in_dim(links, partner, owned, 0)
    own_groups = lax.dynamic_slice_in_dim(member, first, owned, 0)

    def columns_of(array, k):
        return lax.dynamic_slice_in_dim(
            array, (tok_pos ^ k) * own_cols, own_cols, array.ndim - 1
        )

    init_bf = init_basis.astype(jnp.bfloat16)
    slices = [swap(columns_of(init_bf, k), "tok", k) for k in range(tok_count)]
    own_basis = jnp.concatenate(
        [lax.select_n(tok_pos ^ a, *slices) for a in range(tok_count)], axis=1
    )
    near = [acts] + [swap(acts, "tok", k) for k in (1, 2)]
    near[1], near[2], init_late = lax.optimization_barrier((near[1], near[2], init_bf))
    if tok_count == 4:
        half = tok_rows // 2
        far = [
            jnp.concatenate([swap(near[2][:half], "tok", 1), swap(near[1][half:], "tok", 2)])
        ]
    else:
        far = [swap(acts, "tok", k) for k in range(3, tok_count)]
    chunks = [near[:1], near[1:], far]
    init_pieces = collect(init_late, "tok")
    basis_bf = jnp.concatenate(
        [lax.select_n(tok_pos ^ a, *init_pieces) for a in range(tok_count)], axis=1
    )
    basis_bf = jnp.concatenate([columns_of(basis_bf, k) for k in range(tok_count)], axis=2)
    full_x = jnp.concatenate(near + far, axis=0).reshape(total_tokens, owned, block_cols)

    def combine(rows_of_links, pieces, sources):
        total = 0.0
        for piece, source in zip(pieces, sources):
            weights = lax.dynamic_slice_in_dim(rows_of_links, source, owned, 1)
            for j in range(owned):
                total += weights[:, j][:, None, None] * piece[j][None].astype(jnp.float32)
        return total

    def mix_first():
        sources = [(gr_pos * gc_count + (gc_pos ^ b)) * owned for b in range(gc_count)]
        own, other = [], []
        for part in chunks:
            x = jnp.concatenate(part, axis=0).reshape(-1, owned, block_cols)
            proj = jnp.einsum(
                "tob,obr->otr", x, own_basis, preferred_element_type=jnp.float32
            ).astype(jnp.bfloat16)
            pieces = collect(proj, "gc")
            own.append(combine(own_links, pieces, sources))
            other.append(combine(partner_links, pieces, sources))
        total = jnp.concatenate(own, axis=1) + swap(jnp.concatenate(other, axis=1), "gr", 1)
        return total.astype(jnp.bfloat16)

    def gather_mixed(mixed):
        blocks = mixed.reshape(owned, tok_count, tok_rows, own_cols)
        pieces = []
        for k, piece in enumerate(collect(blocks, "tok")):
            pieces.append(
                jnp.concatenate([piece[:, i ^ k : (i ^ k) + 1] for i in range(tok_count)], axis=1)
            )
        return jnp.concatenate(pieces, axis=3).reshape(owned, total_tokens, rank)

    def factor(image, last, beside=None):
        precision = HIGHEST if last else HIGH
        grams = jnp.einsum("obr,obs->ors", image[:, :, :own_cols], image, precision=precision)

        def group_sum(g):
            mask = (own_groups == g).astype(jnp.float32)
            return jnp.sum(mask[:, None, None] * grams, axis=0)

        total = group_sum(gr_pos) + swap(group_sum(gr_pos ^ 1), "gr", 1)
        rows = own_cols // gc_count

        def rows_of(i):
            return lax.dynamic_slice_in_dim(total, (gc_pos ^ i) * rows, rows, 0)

        piece = sum(swap(rows_of(i), "gc", i) for i in range(gc_count))
        blocks = [piece[:, k * own_cols : (k + 1) * own_cols] for k in range(tok_count)]
        piece = jnp.concatenate(
            [lax.select_n(tok_pos ^ a, *blocks) for a in range(tok_count)], axis=1
        )
        rows_near = jnp.stack(collect(piece, "gc"))
        pieces = jnp.stack(collect(rows_near, "tok"))
        if beside is not None:
            pieces, beside = lax.optimization_barrier((pieces, beside))
            beside = gather_mixed(beside)
        own = inverse_factor(pieces, own_cols, not last, last, 1.0 / group_cols)
        other = swap(own, "gr", 1)
        of_block = jnp.stack(
            [jnp.where(own_groups[o] == gr_pos, own, other) for o in range(owned)]
        )
        of_group = [jnp.where(gr_pos == g, own, other) for g in range(groups)]
        return of_block, of_group, beside

    def cover(mixed):
        return jnp.einsum("tob,otr->obr", full_x, mixed, preferred_element_type=jnp.float32)

    own_mixed = mix_first()
    own_image = cover(own_mixed) / total_tokens + ridge * own_basis.astype(jnp.float32)
    seen = sum(
        jnp.einsum("tob,obr->otr", full_x, part, preferred_element_type=jnp.float32)
        for part in split(own_image)
    )
    seen = lax.all_gather(seen, ("gr", "gc"), axis=0, tiled=True)
    own_second = 0.0
    for j in range(seen.shape[0]):
        own_second += own_links[:, j][:, None, None] * seen[j][None]
    image = cover(gather_mixed(own_mixed)) / total_tokens + ridge * basis_bf.astype(jnp.float32)
    of_block, _, second = factor(image, False, own_second)

    image = sum(cover(part) for part in split(second)) / total_tokens + ridge * image
    image = jnp.einsum("obr,osr->obs", image, of_block, precision=HIGH)
    of_block, of_group, _ = factor(image, True)
    rows = lax.dynamic_slice_in_dim(image, tok_pos * slice_rows, slice_rows, 1)
    basis = jnp.einsum("obr,osr->obs", rows, of_block, precision=HIGH)
    own_x = acts.reshape(tok_rows, owned, block_cols)
    codes = sum(
        jnp.einsum("tob,obr->otr", own_x, part, preferred_element_type=jnp.float32)
        for part in split(image)
    )
    placed = jnp.concatenate(
        [
            jnp.sum((own_groups == g).astype(jnp.float32)[:, None, None] * codes, axis=0)
            for g in range(groups)
        ],
        axis=1,
    )
    placed = lax.psum_scatter(placed, ("gr", "gc"), scatter_dimension=0, tiled=True)
    latent = jnp.concatenate(
        [
            jnp.einsum(
                "tr,sr->ts",
                placed[:, g * rank : (g + 1) * rank],
                of_group[g],
                precision=HIGH,
            )
            for g in range(groups)
        ],
        axis=1,
    )
    latent = latent * (1.0 / math.sqrt(group_cols))
    return (basis, latent.astype(jnp.bfloat16))


def solution(mesh):
    placed = (P("tok", ("gr", "gc")), P(("gr", "gc"), "tok", None), P(), P())
    return jax.shard_map(
        per_device,
        mesh=mesh,
        in_specs=placed,
        out_specs=(P(("gr", "gc"), "tok", None), P(("tok", "gr", "gc"), None)),
        check_vma=False,
    )
```

```python
import functools
import math

import jax
import jax.numpy as jnp
from jax import lax
from jax.experimental import pallas as pl
from jax.experimental.pallas import tpu as pltpu
from jax.sharding import PartitionSpec as P

GBLK = 8
PANEL = 128
SUB = 8
CHUNKS = 2

ridge = 2.0
HIGHEST = lax.Precision.HIGHEST
HIGH = lax.Precision.HIGH


def split(value):
    high = lax.reduce_precision(value, 8, 7)
    return high.astype(jnp.bfloat16), (value - high).astype(jnp.bfloat16)


def kernel_dot(left, right, exact):
    if exact:
        return jnp.dot(left, right, preferred_element_type=jnp.float32, precision=HIGHEST)
    parts = []
    for value in (left, right):
        high = value.astype(jnp.bfloat16)
        parts.append((high, (value - high.astype(jnp.float32)).astype(jnp.bfloat16)))
    (a, b), (c, d) = parts
    return sum(
        jnp.dot(x, y, preferred_element_type=jnp.float32) for x, y in ((b, c), (a, d), (a, c))
    )


def eliminate(tiles, inv_ref):
    shape = (SUB, PANEL)
    lane = lax.broadcasted_iota(jnp.int32, shape, 1)
    sub = lax.broadcasted_iota(jnp.int32, shape, 0)

    def spread(column):
        return jnp.broadcast_to(column, shape)

    tiles = list(tiles)
    for s in range(PANEL // SUB):
        start = s * SUB
        tile = tiles[s]
        inside = (lane >= start) & (lane < start + SUB)
        columns = [spread(tile[:, start + c : start + c + 1]) for c in range(SUB)]
        pivot = [
            [spread(columns[c][i : i + 1, :]) if c >= i else None for c in range(SUB)]
            for i in range(SUB)
        ]
        base = jnp.where(inside, jnp.where(lane == start + sub, 1.0, 0.0), tile)
        rows = [spread(base[i : i + 1, :]) for i in range(SUB)]
        below = [[None] * SUB for _ in range(SUB)]
        inverse = []
        for b in range(SUB):
            inverse.append(pl.reciprocal(pivot[b][b], approx=True))
            for i in range(b + 1, SUB):
                factor = pivot[b][i] * inverse[b]
                below[i][b] = factor
                for c in range(i, SUB):
                    pivot[i][c] = pivot[i][c] - factor * pivot[b][c]
                rows[i] = rows[i] - factor * rows[b]
        result = jnp.zeros(shape, jnp.float32)
        for b in range(SUB):
            result = jnp.where(sub == b, rows[b] * lax.rsqrt(pivot[b][b]), result)
        inv_ref[start : start + SUB, :] = jnp.where(lane < start + SUB, result, 0.0)
        solved = [None] * SUB
        for b in reversed(range(SUB)):
            value = rows[b] * inverse[b]
            for i in reversed(range(b + 1, SUB)):
                value = value - below[i][b] * solved[i]
            solved[b] = value
        for q in range(s + 1, PANEL // SUB):
            parts = [
                spread(tiles[q][:, start + b : start + b + 1]) * solved[b] for b in range(SUB)
            ]
            while len(parts) > 1:
                parts = [x + y for x, y in zip(parts[::2], parts[1::2])]
            tiles[q] = jnp.where(inside, 0.0, tiles[q]) - parts[0]


def factor_kernel(scale, exact, pos_ref, pieces_ref, out_ref, work_ref, inv_ref):
    tok_count, gc_count, rows, rank = pieces_ref.shape
    panels = rank // PANEL
    tok_pos, gc_pos = pos_ref[0], pos_ref[1]
    for k in range(tok_count):
        for i in range(gc_count):
            place = ((tok_pos ^ k) * gc_count + (gc_pos ^ i)) * rows
            work_ref[pl.ds(pl.multiple_of(place, SUB), rows), :] = pieces_ref[k, i] * scale

    def panel_step(k, carry):
        here = pl.ds(pl.multiple_of(k * PANEL, PANEL), PANEL)
        diag = work_ref[here, here]

        eliminate([diag[SUB * q : SUB * (q + 1), :] for q in range(PANEL // SUB)], inv_ref)
        for here_k in range(panels):

            @pl.when(k == here_k)
            def _():
                panel = slice(here_k * PANEL, (here_k + 1) * PANEL)
                rest = slice((here_k + 1) * PANEL, rank)
                inv = inv_ref[...]
                work_ref[panel, :] = kernel_dot(inv, work_ref[panel, :], exact)
                work_ref[panel, panel] = inv
                if here_k < panels - 1:
                    lower = work_ref[panel, rest].T
                    work_ref[rest, panel] = jnp.zeros((rank - rest.start, PANEL), jnp.float32)
                    work_ref[rest, :] -= kernel_dot(lower, work_ref[panel, :], exact)

        return carry

    lax.fori_loop(0, panels, panel_step, 0)
    for i in range(panels - 1):
        work_ref[i * PANEL : (i + 1) * PANEL, (i + 1) * PANEL :] = jnp.zeros(
            (PANEL, rank - (i + 1) * PANEL), jnp.float32
        )
    out_ref[...] = work_ref[...]


def inverse_factor(pieces, exact, scale):
    tok_count, gc_count, rows, rank = pieces.shape
    tok_pos, gc_pos = lax.axis_index("tok"), lax.axis_index("gc")
    if rows % SUB == 0:
        pos = jnp.stack([tok_pos, gc_pos]).astype(jnp.int32)
    else:
        pos = jnp.zeros((2,), jnp.int32)
        order = (
            (tok_pos ^ jnp.arange(tok_count, dtype=jnp.int32))[:, None] * gc_count
            + (gc_pos ^ jnp.arange(gc_count, dtype=jnp.int32))[None, :]
        ).reshape(-1)
        place = (order[:, None] * rows + jnp.arange(rows, dtype=jnp.int32)[None, :]).reshape(rank)
        full = jnp.zeros((rank, rank), jnp.float32).at[place].set(pieces.reshape(rank, rank))
        pieces = full.reshape(1, 1, rank, rank)
    return pl.pallas_call(
        functools.partial(factor_kernel, scale, exact),
        out_shape=jax.ShapeDtypeStruct((rank, rank), jnp.float32),
        in_specs=[
            pl.BlockSpec(memory_space=pltpu.SMEM),
            pl.BlockSpec(memory_space=pltpu.VMEM),
        ],
        out_specs=pl.BlockSpec(memory_space=pltpu.VMEM),
        scratch_shapes=[
            pltpu.VMEM((rank, rank), jnp.float32),
            pltpu.VMEM((PANEL, PANEL), jnp.float32),
        ],
        compiler_params=pltpu.CompilerParams(vmem_limit_bytes=32 * 1024 * 1024),
        cost_estimate=pl.CostEstimate(
            flops=96 * rank**3, bytes_accessed=8 * rank**2, transcendentals=0
        ),
        name="inverse_factor",
    )(pos, pieces)


def swap(value, axis, k):
    if k == 0:
        return value
    return lax.ppermute(value, axis, [(i, i ^ k) for i in range(lax.axis_size(axis))])


def collect(value, axis):
    return [swap(value, axis, k) for k in range(lax.axis_size(axis))]


def per_device(acts, init_basis, kept, member):
    owned = init_basis.shape[0]
    slice_rows = init_basis.shape[1]
    rank = init_basis.shape[2]
    tok_count = lax.axis_size("tok")
    gr_count = lax.axis_size("gr")
    gc_count = lax.axis_size("gc")
    block_cols = slice_rows * tok_count
    tok_rows = acts.shape[0]
    total_tokens = tok_rows * tok_count
    groups = kept.shape[0] // GBLK
    assert groups == gr_count == 2
    group_cols = GBLK * block_cols
    own_cols = rank // tok_count
    tok_pos = lax.axis_index("tok")
    gr_pos = lax.axis_index("gr")
    gc_pos = lax.axis_index("gc")
    first = (gr_pos * gc_count + gc_pos) * owned
    links = ((member[:, None] == member[None, :]).astype(jnp.int32) * kept).astype(jnp.float32)
    own_links = lax.dynamic_slice_in_dim(links, first, owned, 0)
    partner = ((gr_pos ^ 1) * gc_count + gc_pos) * owned
    partner_links = lax.dynamic_slice_in_dim(links, partner, owned, 0)
    own_groups = lax.dynamic_slice_in_dim(member, first, owned, 0)

    own_x = acts.reshape(tok_rows, owned, block_cols)
    turned_x = jnp.concatenate(
        [
            lax.dynamic_slice_in_dim(own_x, (tok_pos ^ k) * slice_rows, slice_rows, 2)
            for k in range(tok_count)
        ],
        axis=2,
    )
    init_bf = init_basis.astype(jnp.bfloat16)
    width = rank // CHUNKS
    init_pieces = [
        collect(init_bf[:, :, c * width : (c + 1) * width], "tok") for c in range(CHUNKS)
    ]
    init_pieces[-1], acts_late = lax.optimization_barrier((init_pieces[-1], acts))
    x_pieces = collect(acts_late, "tok")

    def combine(rows_of_links, pieces, sources):
        total = 0.0
        for piece, source in zip(pieces, sources):
            weights = lax.dynamic_slice_in_dim(rows_of_links, source, owned, 1)
            for j in range(owned):
                total += weights[:, j][:, None, None] * piece[j][None].astype(jnp.float32)
        return total

    near = []
    for part in init_pieces:
        proj = jnp.einsum(
            "tob,obr->otr",
            turned_x,
            jnp.concatenate(part, axis=1),
            preferred_element_type=jnp.float32,
        ).astype(jnp.bfloat16)
        near.append(collect(proj, "gc"))
    near, x_pieces = lax.optimization_barrier((near, x_pieces))
    full_x = jnp.concatenate(x_pieces, axis=0).reshape(total_tokens, owned, block_cols)
    basis_bf = jnp.concatenate(
        [
            jnp.concatenate(
                [lax.select_n(tok_pos ^ a, *part) for a in range(tok_count)], axis=1
            )
            for part in init_pieces
        ],
        axis=2,
    )
    sources = [(gr_pos * gc_count + (gc_pos ^ b)) * owned for b in range(gc_count)]
    own_part = [combine(own_links, pieces, sources) for pieces in near]
    other_part = [combine(partner_links, pieces, sources) for pieces in near]
    mixed = jnp.concatenate(
        [own + swap(other, "gr", 1) for own, other in zip(own_part, other_part)], axis=2
    ).astype(jnp.bfloat16)

    def image_of(mixed, basis_bf):
        full = jnp.concatenate(collect(mixed, "tok"), axis=1)
        cover = jnp.einsum("tob,otr->obr", full_x, full, preferred_element_type=jnp.float32)
        return cover / total_tokens + ridge * basis_bf.astype(jnp.float32)

    def seen_by(image):
        return sum(
            jnp.einsum("tob,obr->otr", own_x, part, preferred_element_type=jnp.float32)
            for part in split(image)
        )

    def factor(image, last):
        precision = HIGHEST if last else HIGH
        own = lax.dynamic_slice_in_dim(image, tok_pos * own_cols, own_cols, 2)
        grams = jnp.einsum("obr,obs->ors", own, image, precision=precision)

        def group_sum(g):
            mask = (own_groups == g).astype(jnp.float32)
            return jnp.sum(mask[:, None, None] * grams, axis=0)

        total = group_sum(gr_pos) + swap(group_sum(gr_pos ^ 1), "gr", 1)
        rows = own_cols // gc_count

        def rows_of(i):
            return lax.dynamic_slice_in_dim(total, (gc_pos ^ i) * rows, rows, 0)

        piece = sum(swap(rows_of(i), "gc", i) for i in range(gc_count))
        rows_near = jnp.stack(collect(piece, "gc"))
        pieces = jnp.stack(collect(rows_near, "tok"))
        own = inverse_factor(pieces, last, 1.0 / group_cols)
        other = swap(own, "gr", 1)
        of_block = jnp.stack(
            [jnp.where(own_groups[o] == gr_pos, own, other) for o in range(owned)]
        )
        of_group = [jnp.where(gr_pos == g, own, other) for g in range(groups)]
        return of_block, of_group

    image = image_of(mixed, basis_bf)
    seen = lax.all_gather(seen_by(image), ("gr", "gc"), axis=0, tiled=True)
    second = 0.0
    for j in range(seen.shape[0]):
        second += own_links[:, j][:, None, None] * seen[j][None]
    of_block, _ = factor(image, False)
    mixed = jnp.einsum("otr,osr->ots", second, of_block, precision=HIGH).astype(jnp.bfloat16)
    basis_bf = jnp.einsum("obr,osr->obs", image, of_block, precision=HIGH).astype(jnp.bfloat16)
    image = image_of(mixed, basis_bf)
    of_block, of_group = factor(image, True)
    rows = lax.dynamic_slice_in_dim(image, tok_pos * slice_rows, slice_rows, 1)
    basis = jnp.einsum("obr,osr->obs", rows, of_block, precision=HIGH)
    codes = seen_by(image)
    placed = jnp.concatenate(
        [
            jnp.sum((own_groups == g).astype(jnp.float32)[:, None, None] * codes, axis=0)
            for g in range(groups)
        ],
        axis=1,
    )
    placed = lax.psum_scatter(placed, ("gr", "gc"), scatter_dimension=0, tiled=True)
    latent = jnp.concatenate(
        [
            jnp.einsum(
                "tr,sr->ts",
                placed[:, g * rank : (g + 1) * rank],
                of_group[g],
                precision=HIGH,
            )
            for g in range(groups)
        ],
        axis=1,
    )
    latent = latent * (1.0 / math.sqrt(group_cols))
    return (basis, latent.astype(jnp.bfloat16))


def solution(mesh):
    placed = (P("tok", ("gr", "gc")), P(("gr", "gc"), "tok", None), P(), P())
    return jax.shard_map(
        per_device,
        mesh=mesh,
        in_specs=placed,
        out_specs=(P(("gr", "gc"), "tok", None), P(("tok", "gr", "gc"), None)),
        check_vma=False,
    )
```

```python
import functools
import math

import jax
import jax.numpy as jnp
from jax import lax
from jax.experimental import pallas as pl
from jax.experimental.pallas import tpu as pltpu
from jax.sharding import PartitionSpec as P

GBLK = 8
PANEL = 128
SUB = 8
CHUNKS = 2

ridge = 2.0
HIGHEST = lax.Precision.HIGHEST
HIGH = lax.Precision.HIGH


def split(value):
    high = lax.reduce_precision(value, 8, 7)
    return high.astype(jnp.bfloat16), (value - high).astype(jnp.bfloat16)


def kernel_dot(left, right, exact):
    if exact:
        return jnp.dot(left, right, preferred_element_type=jnp.float32, precision=HIGHEST)
    parts = []
    for value in (left, right):
        high = value.astype(jnp.bfloat16)
        parts.append((high, (value - high.astype(jnp.float32)).astype(jnp.bfloat16)))
    (a, b), (c, d) = parts
    return sum(
        jnp.dot(x, y, preferred_element_type=jnp.float32) for x, y in ((b, c), (a, d), (a, c))
    )


def eliminate(tiles, inv_ref):
    shape = (SUB, PANEL)
    lane = lax.broadcasted_iota(jnp.int32, shape, 1)
    sub = lax.broadcasted_iota(jnp.int32, shape, 0)

    def spread(column):
        return jnp.broadcast_to(column, shape)

    tiles = list(tiles)
    for s in range(PANEL // SUB):
        start = s * SUB
        tile = tiles[s]
        inside = (lane >= start) & (lane < start + SUB)
        columns = [spread(tile[:, start + c : start + c + 1]) for c in range(SUB)]
        pivot = [
            [spread(columns[c][i : i + 1, :]) if c >= i else None for c in range(SUB)]
            for i in range(SUB)
        ]
        base = jnp.where(inside, jnp.where(lane == start + sub, 1.0, 0.0), tile)
        rows = [spread(base[i : i + 1, :]) for i in range(SUB)]
        below = [[None] * SUB for _ in range(SUB)]
        inverse = []
        for b in range(0, SUB, 2):
            head, side, tail = pivot[b][b], pivot[b][b + 1], pivot[b + 1][b + 1]
            det = head * tail - side * side
            inverse.append(pl.reciprocal(head, approx=True))
            inverse.append(head * pl.reciprocal(det, approx=True))
            link = side * inverse[b]
            below[b + 1][b] = link
            rows[b + 1] = rows[b + 1] - link * rows[b]
            pivot[b + 1][b + 1] = det * inverse[b]
            for i in range(b + 2, SUB):
                pivot[b + 1][i] = pivot[b + 1][i] - link * pivot[b][i]
                below[i][b] = pivot[b][i] * inverse[b]
                below[i][b + 1] = pivot[b + 1][i] * inverse[b + 1]
            for i in range(b + 2, SUB):
                for c in range(i, SUB):
                    pivot[i][c] = (pivot[i][c] - below[i][b] * pivot[b][c]) - (
                        below[i][b + 1] * pivot[b + 1][c]
                    )
                rows[i] = (rows[i] - below[i][b] * rows[b]) - below[i][b + 1] * rows[b + 1]
        result = jnp.zeros(shape, jnp.float32)
        for b in range(SUB):
            result = jnp.where(sub == b, rows[b] * lax.rsqrt(pivot[b][b]), result)
        inv_ref[start : start + SUB, :] = jnp.where(lane < start + SUB, result, 0.0)
        solved = [None] * SUB
        for b in reversed(range(SUB)):
            value = rows[b] * inverse[b]
            for i in reversed(range(b + 1, SUB)):
                value = value - below[i][b] * solved[i]
            solved[b] = value
        for q in range(s + 1, PANEL // SUB):
            parts = [
                spread(tiles[q][:, start + b : start + b + 1]) * solved[b] for b in range(SUB)
            ]
            while len(parts) > 1:
                parts = [x + y for x, y in zip(parts[::2], parts[1::2])]
            tiles[q] = jnp.where(inside, 0.0, tiles[q]) - parts[0]


def factor_kernel(scale, exact, pos_ref, pieces_ref, out_ref, work_ref, inv_ref):
    tok_count, gc_count, rows, rank = pieces_ref.shape
    panels = rank // PANEL
    tok_pos, gc_pos = pos_ref[0], pos_ref[1]
    for k in range(tok_count):
        for i in range(gc_count):
            place = ((tok_pos ^ k) * gc_count + (gc_pos ^ i)) * rows
            work_ref[pl.ds(pl.multiple_of(place, SUB), rows), :] = pieces_ref[k, i] * scale

    on_diag = lax.broadcasted_iota(jnp.int32, (PANEL, PANEL), 0) == lax.broadcasted_iota(
        jnp.int32, (PANEL, PANEL), 1
    )
    by_column = []
    for k in range(panels):
        panel = slice(k * PANEL, (k + 1) * PANEL)
        diag = jnp.where(on_diag, work_ref[panel, panel], 0.0)
        by_column.append(lax.rsqrt(jnp.sum(diag, axis=0, keepdims=True)))
        work_ref[panel, :] *= lax.rsqrt(jnp.sum(diag, axis=1, keepdims=True))
    for k in range(panels):
        work_ref[:, k * PANEL : (k + 1) * PANEL] *= by_column[k]

    def panel_step(k, carry):
        here = pl.ds(pl.multiple_of(k * PANEL, PANEL), PANEL)
        diag = work_ref[here, here]

        eliminate([diag[SUB * q : SUB * (q + 1), :] for q in range(PANEL // SUB)], inv_ref)
        for here_k in range(panels):

            @pl.when(k == here_k)
            def _():
                panel = slice(here_k * PANEL, (here_k + 1) * PANEL)
                rest = slice((here_k + 1) * PANEL, rank)
                inv = inv_ref[...]
                work_ref[panel, :] = kernel_dot(inv, work_ref[panel, :], exact)
                work_ref[panel, panel] = inv
                if here_k < panels - 1:
                    lower = work_ref[panel, rest].T
                    work_ref[rest, panel] = jnp.zeros((rank - rest.start, PANEL), jnp.float32)
                    work_ref[rest, :] -= kernel_dot(lower, work_ref[panel, :], exact)

        return carry

    lax.fori_loop(0, panels, panel_step, 0)
    for i in range(panels - 1):
        work_ref[i * PANEL : (i + 1) * PANEL, (i + 1) * PANEL :] = jnp.zeros(
            (PANEL, rank - (i + 1) * PANEL), jnp.float32
        )
    for k in range(panels):
        panel = slice(k * PANEL, (k + 1) * PANEL)
        out_ref[:, panel] = work_ref[:, panel] * by_column[k]


def inverse_factor(pieces, exact, scale):
    tok_count, gc_count, rows, rank = pieces.shape
    tok_pos, gc_pos = lax.axis_index("tok"), lax.axis_index("gc")
    if rows % SUB == 0:
        pos = jnp.stack([tok_pos, gc_pos]).astype(jnp.int32)
    else:
        pos = jnp.zeros((2,), jnp.int32)
        order = (
            (tok_pos ^ jnp.arange(tok_count, dtype=jnp.int32))[:, None] * gc_count
            + (gc_pos ^ jnp.arange(gc_count, dtype=jnp.int32))[None, :]
        ).reshape(-1)
        place = (order[:, None] * rows + jnp.arange(rows, dtype=jnp.int32)[None, :]).reshape(rank)
        full = jnp.zeros((rank, rank), jnp.float32).at[place].set(pieces.reshape(rank, rank))
        pieces = full.reshape(1, 1, rank, rank)
    return pl.pallas_call(
        functools.partial(factor_kernel, scale, exact),
        out_shape=jax.ShapeDtypeStruct((rank, rank), jnp.float32),
        in_specs=[
            pl.BlockSpec(memory_space=pltpu.SMEM),
            pl.BlockSpec(memory_space=pltpu.VMEM),
        ],
        out_specs=pl.BlockSpec(memory_space=pltpu.VMEM),
        scratch_shapes=[
            pltpu.VMEM((rank, rank), jnp.float32),
            pltpu.VMEM((PANEL, PANEL), jnp.float32),
        ],
        compiler_params=pltpu.CompilerParams(vmem_limit_bytes=32 * 1024 * 1024),
        cost_estimate=pl.CostEstimate(
            flops=96 * rank**3, bytes_accessed=8 * rank**2, transcendentals=0
        ),
        name="inverse_factor",
    )(pos, pieces)


def swap(value, axis, k):
    if k == 0:
        return value
    return lax.ppermute(value, axis, [(i, i ^ k) for i in range(lax.axis_size(axis))])


def collect(value, axis):
    return [swap(value, axis, k) for k in range(lax.axis_size(axis))]


def per_device(acts, init_basis, kept, member):
    owned = init_basis.shape[0]
    slice_rows = init_basis.shape[1]
    rank = init_basis.shape[2]
    tok_count = lax.axis_size("tok")
    gr_count = lax.axis_size("gr")
    gc_count = lax.axis_size("gc")
    block_cols = slice_rows * tok_count
    tok_rows = acts.shape[0]
    total_tokens = tok_rows * tok_count
    groups = kept.shape[0] // GBLK
    assert groups == gr_count == 2
    group_cols = GBLK * block_cols
    own_cols = rank // tok_count
    tok_pos = lax.axis_index("tok")
    gr_pos = lax.axis_index("gr")
    gc_pos = lax.axis_index("gc")
    first = (gr_pos * gc_count + gc_pos) * owned
    links = ((member[:, None] == member[None, :]).astype(jnp.int32) * kept).astype(jnp.float32)
    own_links = lax.dynamic_slice_in_dim(links, first, owned, 0)
    partner = ((gr_pos ^ 1) * gc_count + gc_pos) * owned
    partner_links = lax.dynamic_slice_in_dim(links, partner, owned, 0)
    own_groups = lax.dynamic_slice_in_dim(member, first, owned, 0)

    own_x = acts.reshape(tok_rows, owned, block_cols)
    turned_x = jnp.concatenate(
        [
            lax.dynamic_slice_in_dim(own_x, (tok_pos ^ k) * slice_rows, slice_rows, 2)
            for k in range(tok_count)
        ],
        axis=2,
    )
    init_bf = init_basis.astype(jnp.bfloat16)
    width = rank // CHUNKS
    init_pieces = [
        collect(init_bf[:, :, c * width : (c + 1) * width], "tok") for c in range(CHUNKS)
    ]
    init_pieces[-1], acts_late = lax.optimization_barrier((init_pieces[-1], acts))
    x_pieces = collect(acts_late, "tok")

    def combine(rows_of_links, pieces, sources):
        total = 0.0
        for piece, source in zip(pieces, sources):
            weights = lax.dynamic_slice_in_dim(rows_of_links, source, owned, 1)
            for j in range(owned):
                total += weights[:, j][:, None, None] * piece[j][None].astype(jnp.float32)
        return total

    near = []
    for part in init_pieces:
        proj = jnp.einsum(
            "tob,obr->otr",
            turned_x,
            jnp.concatenate(part, axis=1),
            preferred_element_type=jnp.float32,
        ).astype(jnp.bfloat16)
        near.append(collect(proj, "gc"))
    near[-1], x_pieces = lax.optimization_barrier((near[-1], x_pieces))
    full_x = jnp.concatenate(x_pieces, axis=0).reshape(total_tokens, owned, block_cols)
    basis_bf = jnp.concatenate(
        [
            jnp.concatenate(
                [lax.select_n(tok_pos ^ a, *part) for a in range(tok_count)], axis=1
            )
            for part in init_pieces
        ],
        axis=2,
    )
    sources = [(gr_pos * gc_count + (gc_pos ^ b)) * owned for b in range(gc_count)]
    mixed = []
    for pieces in near:
        own = combine(own_links, pieces, sources)
        other = combine(partner_links, pieces, sources)
        mixed.append((own + swap(other, "gr", 1)).astype(jnp.bfloat16))

    def image_of(parts, basis_bf):
        full = jnp.concatenate(
            [jnp.concatenate(collect(part, "tok"), axis=1) for part in parts], axis=2
        )
        cover = jnp.einsum("tob,otr->obr", full_x, full, preferred_element_type=jnp.float32)
        return cover / total_tokens + ridge * basis_bf.astype(jnp.float32)

    def seen_by(image):
        return sum(
            jnp.einsum("tob,obr->otr", own_x, part, preferred_element_type=jnp.float32)
            for part in split(image)
        )

    def factor(image, last, beside=None):
        precision = HIGHEST if last else HIGH
        own = lax.dynamic_slice_in_dim(image, tok_pos * own_cols, own_cols, 2)
        grams = jnp.einsum("obr,obs->ors", own, image, precision=precision)

        def group_sum(g):
            mask = (own_groups == g).astype(jnp.float32)
            return jnp.sum(mask[:, None, None] * grams, axis=0)

        total = group_sum(gr_pos) + swap(group_sum(gr_pos ^ 1), "gr", 1)
        rows = own_cols // gc_count

        def rows_of(i):
            return lax.dynamic_slice_in_dim(total, (gc_pos ^ i) * rows, rows, 0)

        piece = sum(swap(rows_of(i), "gc", i) for i in range(gc_count))
        rows_near = jnp.stack(collect(piece, "gc"))
        pieces = jnp.stack(collect(rows_near, "tok"))
        own = inverse_factor(pieces, last, 1.0 / group_cols)
        other = swap(own, "gr", 1)
        if beside is not None:
            other, beside = lax.optimization_barrier((other, beside))
        of_block = jnp.stack(
            [jnp.where(own_groups[o] == gr_pos, own, other) for o in range(owned)]
        )
        of_group = [jnp.where(gr_pos == g, own, other) for g in range(groups)]
        return of_block, of_group, beside

    image = image_of(mixed, basis_bf)
    seen = lax.all_gather(seen_by(image), ("gr", "gc"), axis=0, tiled=True)
    second = 0.0
    for j in range(seen.shape[0]):
        second += own_links[:, j][:, None, None] * seen[j][None]
    of_block, _, second = factor(image, False, second)
    mixed = jnp.einsum("otr,osr->ots", second, of_block, precision=HIGH).astype(jnp.bfloat16)
    basis_bf = jnp.einsum("obr,osr->obs", image, of_block, precision=HIGH).astype(jnp.bfloat16)
    image = image_of([mixed], basis_bf)
    of_block, of_group, _ = factor(image, True)
    rows = lax.dynamic_slice_in_dim(image, tok_pos * slice_rows, slice_rows, 1)
    basis = jnp.einsum("obr,osr->obs", rows, of_block, precision=HIGH)
    codes = seen_by(image)
    placed = jnp.concatenate(
        [
            jnp.sum((own_groups == g).astype(jnp.float32)[:, None, None] * codes, axis=0)
            for g in range(groups)
        ],
        axis=1,
    )
    placed = lax.psum_scatter(placed, ("gr", "gc"), scatter_dimension=0, tiled=True)
    latent = jnp.concatenate(
        [
            jnp.einsum(
                "tr,sr->ts",
                placed[:, g * rank : (g + 1) * rank],
                of_group[g],
                precision=HIGH,
            )
            for g in range(groups)
        ],
        axis=1,
    )
    latent = latent * (1.0 / math.sqrt(group_cols))
    return (basis, latent.astype(jnp.bfloat16))


def solution(mesh):
    placed = (P("tok", ("gr", "gc")), P(("gr", "gc"), "tok", None), P(), P())
    return jax.shard_map(
        per_device,
        mesh=mesh,
        in_specs=placed,
        out_specs=(P(("gr", "gc"), "tok", None), P(("tok", "gr", "gc"), None)),
        check_vma=False,
    )
```

```python
import functools
import math

import jax
import jax.numpy as jnp
from jax import lax
from jax.experimental import pallas as pl
from jax.experimental.pallas import tpu as pltpu
from jax.sharding import PartitionSpec as P

GBLK = 8
PANEL = 128
SUB = 8
CHUNKS = 2

ridge = 2.0
HIGHEST = lax.Precision.HIGHEST
HIGH = lax.Precision.HIGH


def split(value):
    high = lax.reduce_precision(value, 8, 7)
    return high.astype(jnp.bfloat16), (value - high).astype(jnp.bfloat16)


def kernel_dot(left, right, exact):
    if exact:
        return jnp.dot(left, right, preferred_element_type=jnp.float32, precision=HIGHEST)
    parts = []
    for value in (left, right):
        high = value.astype(jnp.bfloat16)
        parts.append((high, (value - high.astype(jnp.float32)).astype(jnp.bfloat16)))
    (a, b), (c, d) = parts
    return sum(
        jnp.dot(x, y, preferred_element_type=jnp.float32) for x, y in ((b, c), (a, d), (a, c))
    )


def eliminate(tiles, inv_ref):
    shape = (SUB, PANEL)
    lane = lax.broadcasted_iota(jnp.int32, shape, 1)
    sub = lax.broadcasted_iota(jnp.int32, shape, 0)

    def spread(column):
        return jnp.broadcast_to(column, shape)

    tiles = list(tiles)
    for s in range(PANEL // SUB):
        start = s * SUB
        tile = tiles[s]
        inside = (lane >= start) & (lane < start + SUB)
        columns = [spread(tile[:, start + c : start + c + 1]) for c in range(SUB)]
        pivot = [
            [spread(columns[c][i : i + 1, :]) if c >= i else None for c in range(SUB)]
            for i in range(SUB)
        ]
        base = jnp.where(inside, jnp.where(lane == start + sub, 1.0, 0.0), tile)
        rows = [spread(base[i : i + 1, :]) for i in range(SUB)]
        below = [[None] * SUB for _ in range(SUB)]
        inverse = []
        for b in range(0, SUB, 2):
            head, side, tail = pivot[b][b], pivot[b][b + 1], pivot[b + 1][b + 1]
            det = head * tail - side * side
            inverse.append(pl.reciprocal(head, approx=True))
            inverse.append(head * pl.reciprocal(det, approx=True))
            link = side * inverse[b]
            below[b + 1][b] = link
            rows[b + 1] = rows[b + 1] - link * rows[b]
            pivot[b + 1][b + 1] = det * inverse[b]
            for i in range(b + 2, SUB):
                pivot[b + 1][i] = pivot[b + 1][i] - link * pivot[b][i]
                below[i][b] = pivot[b][i] * inverse[b]
                below[i][b + 1] = pivot[b + 1][i] * inverse[b + 1]
            for i in range(b + 2, SUB):
                for c in range(i, SUB):
                    pivot[i][c] = (pivot[i][c] - below[i][b] * pivot[b][c]) - (
                        below[i][b + 1] * pivot[b + 1][c]
                    )
                rows[i] = (rows[i] - below[i][b] * rows[b]) - below[i][b + 1] * rows[b + 1]
        result = jnp.zeros(shape, jnp.float32)
        for b in range(SUB):
            result = jnp.where(sub == b, rows[b] * lax.rsqrt(pivot[b][b]), result)
        inv_ref[start : start + SUB, :] = jnp.where(lane < start + SUB, result, 0.0)
        solved = [None] * SUB
        for b in reversed(range(SUB)):
            value = rows[b] * inverse[b]
            for i in reversed(range(b + 1, SUB)):
                value = value - below[i][b] * solved[i]
            solved[b] = value
        for q in range(s + 1, PANEL // SUB):
            parts = [
                spread(tiles[q][:, start + b : start + b + 1]) * solved[b] for b in range(SUB)
            ]
            while len(parts) > 1:
                parts = [x + y for x, y in zip(parts[::2], parts[1::2])]
            tiles[q] = jnp.where(inside, 0.0, tiles[q]) - parts[0]


def factor_kernel(scale, exact, pos_ref, *refs):
    *piece_refs, out_ref, work_ref, inv_ref = refs
    rank = work_ref.shape[0]
    panels = rank // PANEL
    count = len(piece_refs)
    if count == 1:
        work_ref[...] = piece_refs[0][...] * scale
    else:
        work_ref[...] = jnp.zeros((rank, rank), jnp.float32)
    own_cols = rank // count
    for k in range(count if count > 1 else 0):
        for s in range(count):

            @pl.when(pos_ref[0] ^ k == s)
            def _():
                for d in range(piece_refs[k].shape[1] // own_cols):
                    other = (s + d) % count
                    block = piece_refs[k][:, d * own_cols : (d + 1) * own_cols] * scale
                    low, high = min(s, other), max(s, other)
                    if s > other and 2 * d == count:
                        continue
                    work_ref[
                        low * own_cols : (low + 1) * own_cols,
                        high * own_cols : (high + 1) * own_cols,
                    ] = block.T if s > other else block

    on_diag = lax.broadcasted_iota(jnp.int32, (PANEL, PANEL), 0) == lax.broadcasted_iota(
        jnp.int32, (PANEL, PANEL), 1
    )
    by_column = []
    for k in range(panels):
        panel = slice(k * PANEL, (k + 1) * PANEL)
        diag = jnp.where(on_diag, work_ref[panel, panel], 0.0)
        by_column.append(lax.rsqrt(jnp.sum(diag, axis=0, keepdims=True)))
        work_ref[panel, :] *= lax.rsqrt(jnp.sum(diag, axis=1, keepdims=True))
    for k in range(panels):
        work_ref[:, k * PANEL : (k + 1) * PANEL] *= by_column[k]

    def panel_step(k, carry):
        here = pl.ds(pl.multiple_of(k * PANEL, PANEL), PANEL)
        diag = work_ref[here, here]

        eliminate([diag[SUB * q : SUB * (q + 1), :] for q in range(PANEL // SUB)], inv_ref)
        for here_k in range(panels):

            @pl.when(k == here_k)
            def _():
                panel = slice(here_k * PANEL, (here_k + 1) * PANEL)
                rest = slice((here_k + 1) * PANEL, rank)
                inv = inv_ref[...]
                work_ref[panel, :] = kernel_dot(inv, work_ref[panel, :], exact)
                work_ref[panel, panel] = inv
                if here_k < panels - 1:
                    lower = work_ref[panel, rest].T
                    work_ref[rest, panel] = jnp.zeros((rank - rest.start, PANEL), jnp.float32)
                    work_ref[rest, :] -= kernel_dot(lower, work_ref[panel, :], exact)

        return carry

    lax.fori_loop(0, panels, panel_step, 0)
    for i in range(panels - 1):
        work_ref[i * PANEL : (i + 1) * PANEL, (i + 1) * PANEL :] = jnp.zeros(
            (PANEL, rank - (i + 1) * PANEL), jnp.float32
        )
    for k in range(panels):
        panel = slice(k * PANEL, (k + 1) * PANEL)
        out_ref[:, panel] = work_ref[:, panel] * by_column[k]


def inverse_factor(pieces, exact, scale):
    rank = pieces[0].shape[0] * len(pieces)
    pos = lax.axis_index("tok").astype(jnp.int32).reshape(1)
    return pl.pallas_call(
        functools.partial(factor_kernel, scale, exact),
        out_shape=jax.ShapeDtypeStruct((rank, rank), jnp.float32),
        in_specs=[
            pl.BlockSpec(memory_space=pltpu.SMEM),
            *[pl.BlockSpec(memory_space=pltpu.VMEM) for _ in pieces],
        ],
        out_specs=pl.BlockSpec(memory_space=pltpu.VMEM),
        scratch_shapes=[
            pltpu.VMEM((rank, rank), jnp.float32),
            pltpu.VMEM((PANEL, PANEL), jnp.float32),
        ],
        compiler_params=pltpu.CompilerParams(vmem_limit_bytes=32 * 1024 * 1024),
        cost_estimate=pl.CostEstimate(
            flops=96 * rank**3, bytes_accessed=8 * rank**2, transcendentals=0
        ),
        name="inverse_factor",
    )(pos, *pieces)


def swap(value, axis, k):
    if k == 0:
        return value
    return lax.ppermute(value, axis, [(i, i ^ k) for i in range(lax.axis_size(axis))])


def collect(value, axis):
    return [swap(value, axis, k) for k in range(lax.axis_size(axis))]


def collect_relayed(value, axis):
    if lax.axis_size(axis) != 4:
        return collect(value, axis)
    half = value.shape[0] // 2
    near, side = swap(value, axis, 1), swap(value, axis, 2)
    far = [swap(side[:half], axis, 1), swap(near[half:], axis, 2)]
    return [value, near, side, jnp.concatenate(far, axis=0)]


def per_device(acts, init_basis, kept, member):
    owned = init_basis.shape[0]
    slice_rows = init_basis.shape[1]
    rank = init_basis.shape[2]
    tok_count = lax.axis_size("tok")
    gr_count = lax.axis_size("gr")
    gc_count = lax.axis_size("gc")
    block_cols = slice_rows * tok_count
    tok_rows = acts.shape[0]
    total_tokens = tok_rows * tok_count
    groups = kept.shape[0] // GBLK
    assert groups == gr_count == 2
    group_cols = GBLK * block_cols
    own_cols = rank // tok_count
    tok_pos = lax.axis_index("tok")
    gr_pos = lax.axis_index("gr")
    gc_pos = lax.axis_index("gc")
    first = (gr_pos * gc_count + gc_pos) * owned
    links = ((member[:, None] == member[None, :]).astype(jnp.int32) * kept).astype(jnp.float32)
    own_links = lax.dynamic_slice_in_dim(links, first, owned, 0)
    partner = ((gr_pos ^ 1) * gc_count + gc_pos) * owned
    partner_links = lax.dynamic_slice_in_dim(links, partner, owned, 0)
    own_groups = lax.dynamic_slice_in_dim(member, first, owned, 0)

    own_x = acts.reshape(tok_rows, owned, block_cols)
    turned_x = jnp.concatenate(
        [
            lax.dynamic_slice_in_dim(own_x, (tok_pos ^ k) * slice_rows, slice_rows, 2)
            for k in range(tok_count)
        ],
        axis=2,
    )
    init_bf = init_basis.astype(jnp.bfloat16)
    width = rank // CHUNKS
    init_pieces = [
        collect(init_bf[:, :, c * width : (c + 1) * width], "tok") for c in range(CHUNKS)
    ]
    init_pieces[-1], acts_late = lax.optimization_barrier((init_pieces[-1], acts))
    x_pieces = collect_relayed(acts_late, "tok")

    def combine(rows_of_links, pieces, sources):
        total = 0.0
        for piece, source in zip(pieces, sources):
            weights = lax.dynamic_slice_in_dim(rows_of_links, source, owned, 1)
            for j in range(owned):
                total += weights[:, j][:, None, None] * piece[j][None].astype(jnp.float32)
        return total

    near = []
    for part in init_pieces:
        proj = jnp.einsum(
            "tob,obr->otr",
            turned_x,
            jnp.concatenate(part, axis=1),
            preferred_element_type=jnp.float32,
        ).astype(jnp.bfloat16)
        near.append(collect(proj, "gc"))
    near[-1], x_pieces = lax.optimization_barrier((near[-1], x_pieces))
    full_x = jnp.concatenate(x_pieces, axis=0).reshape(total_tokens, owned, block_cols)
    basis_bf = jnp.concatenate(
        [
            jnp.concatenate(
                [lax.select_n(tok_pos ^ a, *part) for a in range(tok_count)], axis=1
            )
            for part in init_pieces
        ],
        axis=2,
    )
    sources = [(gr_pos * gc_count + (gc_pos ^ b)) * owned for b in range(gc_count)]
    mixed = []
    for pieces in near:
        own = combine(own_links, pieces, sources)
        other = combine(partner_links, pieces, sources)
        mixed.append((own + swap(other, "gr", 1)).astype(jnp.bfloat16))

    def image_of(parts, basis_bf):
        full = jnp.concatenate(
            [jnp.concatenate(collect(part, "tok"), axis=1) for part in parts], axis=2
        )
        cover = jnp.einsum("tob,otr->obr", full_x, full, preferred_element_type=jnp.float32)
        return cover / total_tokens + ridge * basis_bf.astype(jnp.float32)

    def seen_by(image):
        return sum(
            jnp.einsum("tob,obr->otr", own_x, part, preferred_element_type=jnp.float32)
            for part in split(image)
        )

    def factor(image, last, beside=None, aside=None):
        precision = HIGHEST if last else HIGH
        own = lax.dynamic_slice_in_dim(image, tok_pos * own_cols, own_cols, 2)
        grams = jnp.einsum("obr,obs->ors", own, image, precision=precision)

        def group_sum(g):
            mask = (own_groups == g).astype(jnp.float32)
            return jnp.sum(mask[:, None, None] * grams, axis=0)

        total = group_sum(gr_pos) + swap(group_sum(gr_pos ^ 1), "gr", 1)
        packed = tok_count == 4 and own_cols % PANEL == 0
        if packed:
            total = jnp.concatenate(
                [
                    lax.dynamic_slice_in_dim(
                        total, (tok_pos + d) % tok_count * own_cols, own_cols, 1
                    )
                    for d in range(tok_count // 2 + 1)
                ],
                axis=1,
            )
        step = 1
        while step < gc_count:
            if aside is not None and 2 * step == gc_count:
                total, aside = lax.optimization_barrier((total, aside))
            total += swap(total, "gc", step)
            step *= 2
        if packed:
            pieces = collect(total, "tok")
        else:
            pieces = [lax.all_gather(total, "tok", axis=0, tiled=True)]
        own = inverse_factor(pieces, last, 1.0 / group_cols)
        other = swap(own, "gr", 1)
        if beside is not None:
            other, beside = lax.optimization_barrier((other, beside))
        of_block = jnp.stack(
            [jnp.where(own_groups[o] == gr_pos, own, other) for o in range(owned)]
        )
        of_group = [jnp.where(gr_pos == g, own, other) for g in range(groups)]
        return of_block, of_group, beside, aside

    image = image_of(mixed, basis_bf)
    seen = lax.all_gather(seen_by(image), ("gr", "gc"), axis=0, tiled=True)
    second = 0.0
    for j in range(seen.shape[0]):
        second += own_links[:, j][:, None, None] * seen[j][None]
    of_block, _, second, _ = factor(image, False, second)
    mixed = jnp.einsum("otr,osr->ots", second, of_block, precision=HIGH).astype(jnp.bfloat16)
    basis_bf = jnp.einsum("obr,osr->obs", image, of_block, precision=HIGH).astype(jnp.bfloat16)
    image = image_of([mixed], basis_bf)
    codes = seen_by(image)
    placed = jnp.concatenate(
        [
            jnp.sum((own_groups == g).astype(jnp.float32)[:, None, None] * codes, axis=0)
            for g in range(groups)
        ],
        axis=1,
    )
    of_block, of_group, _, placed = factor(image, True, aside=placed)
    rows = lax.dynamic_slice_in_dim(image, tok_pos * slice_rows, slice_rows, 1)
    basis = jnp.einsum("obr,osr->obs", rows, of_block, precision=HIGH)
    placed = lax.psum_scatter(placed, ("gr", "gc"), scatter_dimension=0, tiled=True)
    latent = jnp.concatenate(
        [
            jnp.einsum(
                "tr,sr->ts",
                placed[:, g * rank : (g + 1) * rank],
                of_group[g],
                precision=HIGH,
            )
            for g in range(groups)
        ],
        axis=1,
    )
    latent = latent * (1.0 / math.sqrt(group_cols))
    return (basis, latent.astype(jnp.bfloat16))


def solution(mesh):
    placed = (P("tok", ("gr", "gc")), P(("gr", "gc"), "tok", None), P(), P())
    return jax.shard_map(
        per_device,
        mesh=mesh,
        in_specs=placed,
        out_specs=(P(("gr", "gc"), "tok", None), P(("tok", "gr", "gc"), None)),
        check_vma=False,
    )
```

```python
import functools
import math

import jax
import jax.numpy as jnp
from jax import lax
from jax.experimental import pallas as pl
from jax.experimental.pallas import tpu as pltpu
from jax.sharding import PartitionSpec as P

GBLK = 8
PANEL = 128
SUB = 8
CHUNKS = 2

ridge = 2.0
HIGHEST = lax.Precision.HIGHEST
HIGH = lax.Precision.HIGH


def split(value):
    high = lax.reduce_precision(value, 8, 7)
    return high.astype(jnp.bfloat16), (value - high).astype(jnp.bfloat16)


def kernel_dot(left, right, exact):
    if exact:
        return jnp.dot(left, right, preferred_element_type=jnp.float32, precision=HIGHEST)
    parts = []
    for value in (left, right):
        high = value.astype(jnp.bfloat16)
        parts.append((high, (value - high.astype(jnp.float32)).astype(jnp.bfloat16)))
    (a, b), (c, d) = parts
    return sum(
        jnp.dot(x, y, preferred_element_type=jnp.float32) for x, y in ((b, c), (a, d), (a, c))
    )


def eliminate(tiles, inv_ref):
    shape = (SUB, PANEL)
    lane = lax.broadcasted_iota(jnp.int32, shape, 1)
    sub = lax.broadcasted_iota(jnp.int32, shape, 0)

    def spread(column):
        return jnp.broadcast_to(column, shape)

    tiles = list(tiles)
    for s in range(PANEL // SUB):
        start = s * SUB
        tile = tiles[s]
        inside = (lane >= start) & (lane < start + SUB)
        columns = [spread(tile[:, start + c : start + c + 1]) for c in range(SUB)]
        pivot = [
            [spread(columns[c][i : i + 1, :]) if c >= i else None for c in range(SUB)]
            for i in range(SUB)
        ]
        base = jnp.where(inside, jnp.where(lane == start + sub, 1.0, 0.0), tile)
        rows = [spread(base[i : i + 1, :]) for i in range(SUB)]
        below = [[None] * SUB for _ in range(SUB)]
        inverse = []
        for b in range(0, SUB, 2):
            head, side, tail = pivot[b][b], pivot[b][b + 1], pivot[b + 1][b + 1]
            det = head * tail - side * side
            inverse.append(pl.reciprocal(head, approx=True))
            inverse.append(head * pl.reciprocal(det, approx=True))
            link = side * inverse[b]
            below[b + 1][b] = link
            rows[b + 1] = rows[b + 1] - link * rows[b]
            pivot[b + 1][b + 1] = det * inverse[b]
            for i in range(b + 2, SUB):
                pivot[b + 1][i] = pivot[b + 1][i] - link * pivot[b][i]
                below[i][b] = pivot[b][i] * inverse[b]
                below[i][b + 1] = pivot[b + 1][i] * inverse[b + 1]
            for i in range(b + 2, SUB):
                for c in range(i, SUB):
                    pivot[i][c] = (pivot[i][c] - below[i][b] * pivot[b][c]) - (
                        below[i][b + 1] * pivot[b + 1][c]
                    )
                rows[i] = (rows[i] - below[i][b] * rows[b]) - below[i][b + 1] * rows[b + 1]
        result = jnp.zeros(shape, jnp.float32)
        for b in range(SUB):
            result = jnp.where(sub == b, rows[b] * lax.rsqrt(pivot[b][b]), result)
        inv_ref[start : start + SUB, :] = jnp.where(lane < start + SUB, result, 0.0)
        solved = [None] * SUB
        for b in reversed(range(SUB)):
            value = rows[b] * inverse[b]
            for i in reversed(range(b + 1, SUB)):
                value = value - below[i][b] * solved[i]
            solved[b] = value
        for q in range(s + 1, PANEL // SUB):
            parts = [
                spread(tiles[q][:, start + b : start + b + 1]) * solved[b] for b in range(SUB)
            ]
            while len(parts) > 1:
                parts = [x + y for x, y in zip(parts[::2], parts[1::2])]
            tiles[q] = jnp.where(inside, 0.0, tiles[q]) - parts[0]


def factor_kernel(scale, exact, pos_ref, *refs):
    *piece_refs, out_ref, work_ref, inv_ref = refs
    rank = work_ref.shape[0]
    panels = rank // PANEL
    count = len(piece_refs)
    if count == 1:
        work_ref[...] = piece_refs[0][...] * scale
    else:
        work_ref[...] = jnp.zeros((rank, rank), jnp.float32)
    own_cols = rank // count
    for k in range(count if count > 1 else 0):
        for s in range(count):

            @pl.when(pos_ref[0] ^ k == s)
            def _():
                for d in range(piece_refs[k].shape[1] // own_cols):
                    other = (s + d) % count
                    block = piece_refs[k][:, d * own_cols : (d + 1) * own_cols] * scale
                    low, high = min(s, other), max(s, other)
                    if s > other and 2 * d == count:
                        continue
                    work_ref[
                        low * own_cols : (low + 1) * own_cols,
                        high * own_cols : (high + 1) * own_cols,
                    ] = block.T if s > other else block

    on_diag = lax.broadcasted_iota(jnp.int32, (PANEL, PANEL), 0) == lax.broadcasted_iota(
        jnp.int32, (PANEL, PANEL), 1
    )
    by_column = []
    for k in range(panels):
        panel = slice(k * PANEL, (k + 1) * PANEL)
        diag = jnp.where(on_diag, work_ref[panel, panel], 0.0)
        by_column.append(lax.rsqrt(jnp.sum(diag, axis=0, keepdims=True)))
        work_ref[panel, :] *= lax.rsqrt(jnp.sum(diag, axis=1, keepdims=True))
    for k in range(panels):
        work_ref[:, k * PANEL : (k + 1) * PANEL] *= by_column[k]

    def panel_step(k, carry):
        here = pl.ds(pl.multiple_of(k * PANEL, PANEL), PANEL)
        diag = work_ref[here, here]

        eliminate([diag[SUB * q : SUB * (q + 1), :] for q in range(PANEL // SUB)], inv_ref)
        for here_k in range(panels):

            @pl.when(k == here_k)
            def _():
                panel = slice(here_k * PANEL, (here_k + 1) * PANEL)
                rest = slice((here_k + 1) * PANEL, rank)
                inv = inv_ref[...]
                work_ref[panel, :] = kernel_dot(inv, work_ref[panel, :], exact)
                work_ref[panel, panel] = inv
                if here_k < panels - 1:
                    lower = work_ref[panel, rest].T
                    work_ref[rest, panel] = jnp.zeros((rank - rest.start, PANEL), jnp.float32)
                    work_ref[rest, :] -= kernel_dot(lower, work_ref[panel, :], exact)

        return carry

    lax.fori_loop(0, panels, panel_step, 0)
    for i in range(panels - 1):
        work_ref[i * PANEL : (i + 1) * PANEL, (i + 1) * PANEL :] = jnp.zeros(
            (PANEL, rank - (i + 1) * PANEL), jnp.float32
        )
    for k in range(panels):
        panel = slice(k * PANEL, (k + 1) * PANEL)
        out_ref[:, panel] = work_ref[:, panel] * by_column[k]


def inverse_factor(pieces, exact, scale):
    rank = pieces[0].shape[0] * len(pieces)
    pos = lax.axis_index("tok").astype(jnp.int32).reshape(1)
    return pl.pallas_call(
        functools.partial(factor_kernel, scale, exact),
        out_shape=jax.ShapeDtypeStruct((rank, rank), jnp.float32),
        in_specs=[
            pl.BlockSpec(memory_space=pltpu.SMEM),
            *[pl.BlockSpec(memory_space=pltpu.VMEM) for _ in pieces],
        ],
        out_specs=pl.BlockSpec(memory_space=pltpu.VMEM),
        scratch_shapes=[
            pltpu.VMEM((rank, rank), jnp.float32),
            pltpu.VMEM((PANEL, PANEL), jnp.float32),
        ],
        compiler_params=pltpu.CompilerParams(vmem_limit_bytes=32 * 1024 * 1024),
        cost_estimate=pl.CostEstimate(
            flops=96 * rank**3, bytes_accessed=8 * rank**2, transcendentals=0
        ),
        name="inverse_factor",
    )(pos, *pieces)


def swap(value, axis, k):
    if k == 0:
        return value
    return lax.ppermute(value, axis, [(i, i ^ k) for i in range(lax.axis_size(axis))])


def collect(value, axis):
    return [swap(value, axis, k) for k in range(lax.axis_size(axis))]


def collect_relayed(value, axis, dim):
    if lax.axis_size(axis) != 4:
        return collect(value, axis)
    near, side = swap(value, axis, 1), swap(value, axis, 2)
    far = [
        swap(jnp.split(side, 2, axis=dim)[0], axis, 1),
        swap(jnp.split(near, 2, axis=dim)[1], axis, 2),
    ]
    return [value, near, side, jnp.concatenate(far, axis=dim)]


def per_device(acts, init_basis, kept, member):
    owned = init_basis.shape[0]
    slice_rows = init_basis.shape[1]
    rank = init_basis.shape[2]
    tok_count = lax.axis_size("tok")
    gr_count = lax.axis_size("gr")
    gc_count = lax.axis_size("gc")
    block_cols = slice_rows * tok_count
    tok_rows = acts.shape[0]
    total_tokens = tok_rows * tok_count
    groups = kept.shape[0] // GBLK
    assert groups == gr_count == 2
    group_cols = GBLK * block_cols
    own_cols = rank // tok_count
    tok_pos = lax.axis_index("tok")
    gr_pos = lax.axis_index("gr")
    gc_pos = lax.axis_index("gc")
    first = (gr_pos * gc_count + gc_pos) * owned
    links = ((member[:, None] == member[None, :]).astype(jnp.int32) * kept).astype(jnp.float32)
    own_links = lax.dynamic_slice_in_dim(links, first, owned, 0)
    partner = ((gr_pos ^ 1) * gc_count + gc_pos) * owned
    partner_links = lax.dynamic_slice_in_dim(links, partner, owned, 0)
    own_groups = lax.dynamic_slice_in_dim(member, first, owned, 0)

    own_x = acts.reshape(tok_rows, owned, block_cols)
    turned_x = jnp.concatenate(
        [
            lax.dynamic_slice_in_dim(own_x, (tok_pos ^ k) * slice_rows, slice_rows, 2)
            for k in range(tok_count)
        ],
        axis=2,
    )
    init_bf = init_basis.astype(jnp.bfloat16)
    width = rank // CHUNKS
    init_pieces = [
        collect_relayed(init_bf[:, :, c * width : (c + 1) * width], "tok", 1)
        for c in range(CHUNKS)
    ]
    init_pieces[-1], acts_late = lax.optimization_barrier((init_pieces[-1], acts))
    x_pieces = collect_relayed(acts_late, "tok", 0)

    def combine(rows_of_links, pieces, sources):
        total = 0.0
        for piece, source in zip(pieces, sources):
            weights = lax.dynamic_slice_in_dim(rows_of_links, source, owned, 1)
            for j in range(owned):
                total += weights[:, j][:, None, None] * piece[j][None].astype(jnp.float32)
        return total

    near = []
    for part in init_pieces:
        proj = jnp.einsum(
            "tob,obr->otr",
            turned_x,
            jnp.concatenate(part, axis=1),
            preferred_element_type=jnp.float32,
        ).astype(jnp.bfloat16)
        near.append(collect(proj, "gc"))
    sources = [(gr_pos * gc_count + (gc_pos ^ b)) * owned for b in range(gc_count)]

    def mix(pieces):
        own = combine(own_links, pieces, sources)
        other = combine(partner_links, pieces, sources)
        return collect((own + swap(other, "gr", 1)).astype(jnp.bfloat16), "tok")

    mixed = [mix(pieces) for pieces in near[:-1]]
    near[-1], x_pieces, mixed = lax.optimization_barrier((near[-1], x_pieces, mixed))
    mixed.append(mix(near[-1]))
    full_x = jnp.concatenate(x_pieces, axis=0).reshape(total_tokens, owned, block_cols)
    basis_bf = jnp.concatenate(
        [
            jnp.concatenate(
                [lax.select_n(tok_pos ^ a, *part) for a in range(tok_count)], axis=1
            )
            for part in init_pieces
        ],
        axis=2,
    )

    def image_of(parts, basis_bf):
        full = jnp.concatenate([jnp.concatenate(part, axis=1) for part in parts], axis=2)
        cover = jnp.einsum("tob,otr->obr", full_x, full, preferred_element_type=jnp.float32)
        return cover / total_tokens + ridge * basis_bf.astype(jnp.float32)

    def seen_by(image):
        return sum(
            jnp.einsum("tob,obr->otr", own_x, part, preferred_element_type=jnp.float32)
            for part in split(image)
        )

    def factor(image, last, beside):
        precision = HIGHEST if last else HIGH
        own = lax.dynamic_slice_in_dim(image, tok_pos * own_cols, own_cols, 2)
        grams = jnp.einsum("obr,obs->ors", own, image, precision=precision)

        def group_sum(g):
            mask = (own_groups == g).astype(jnp.float32)
            return jnp.sum(mask[:, None, None] * grams, axis=0)

        total = group_sum(gr_pos) + swap(group_sum(gr_pos ^ 1), "gr", 1)
        packed = tok_count == 4 and own_cols % PANEL == 0
        if packed:
            total = jnp.concatenate(
                [
                    lax.dynamic_slice_in_dim(
                        total, (tok_pos + d) % tok_count * own_cols, own_cols, 1
                    )
                    for d in range(tok_count // 2 + 1)
                ],
                axis=1,
            )
        step = 1
        while step < gc_count:
            if last and 2 * step == gc_count:
                total, beside = lax.optimization_barrier((total, beside))
            total += swap(total, "gc", step)
            step *= 2
        if not last:
            total, beside = lax.optimization_barrier((total, beside))
            beside = mix_seen(beside)
        if packed:
            pieces = collect(total, "tok")
        else:
            pieces = [lax.all_gather(total, "tok", axis=0, tiled=True)]
        own = inverse_factor(pieces, last, 1.0 / group_cols)
        other = swap(own, "gr", 1)
        if not last:
            other, beside = lax.optimization_barrier((other, beside))
        of_block = jnp.stack(
            [jnp.where(own_groups[o] == gr_pos, own, other) for o in range(owned)]
        )
        of_group = [jnp.where(gr_pos == g, own, other) for g in range(groups)]
        return of_block, of_group, beside

    image = image_of(mixed, basis_bf)
    def mix_seen(seen):
        seen = lax.all_gather(seen, ("gr", "gc"), axis=0, tiled=True)
        total = 0.0
        for j in range(seen.shape[0]):
            total += own_links[:, j][:, None, None] * seen[j][None]
        return total

    of_block, _, second = factor(image, False, seen_by(image))
    mixed = jnp.einsum("otr,osr->ots", second, of_block, precision=HIGH).astype(jnp.bfloat16)
    basis_bf = jnp.einsum("obr,osr->obs", image, of_block, precision=HIGH).astype(jnp.bfloat16)
    image = image_of([collect(mixed, "tok")], basis_bf)
    codes = seen_by(image)
    placed = jnp.concatenate(
        [
            jnp.sum((own_groups == g).astype(jnp.float32)[:, None, None] * codes, axis=0)
            for g in range(groups)
        ],
        axis=1,
    )
    of_block, of_group, placed = factor(image, True, placed)
    rows = lax.dynamic_slice_in_dim(image, tok_pos * slice_rows, slice_rows, 1)
    basis = jnp.einsum("obr,osr->obs", rows, of_block, precision=HIGH)
    placed = lax.psum_scatter(placed, ("gr", "gc"), scatter_dimension=0, tiled=True)
    latent = jnp.concatenate(
        [
            jnp.einsum(
                "tr,sr->ts",
                placed[:, g * rank : (g + 1) * rank],
                of_group[g],
                precision=HIGH,
            )
            for g in range(groups)
        ],
        axis=1,
    )
    latent = latent * (1.0 / math.sqrt(group_cols))
    return (basis, latent.astype(jnp.bfloat16))


def solution(mesh):
    placed = (P("tok", ("gr", "gc")), P(("gr", "gc"), "tok", None), P(), P())
    return jax.shard_map(
        per_device,
        mesh=mesh,
        in_specs=placed,
        out_specs=(P(("gr", "gc"), "tok", None), P(("tok", "gr", "gc"), None)),
        check_vma=False,
    )
```

```python
import functools
import math

import jax
import jax.numpy as jnp
from jax import lax
from jax.experimental import pallas as pl
from jax.experimental.pallas import tpu as pltpu
from jax.sharding import PartitionSpec as P

GBLK = 8
PANEL = 128
SUB = 8
CHUNKS = 2

ridge = 2.0
HIGHEST = lax.Precision.HIGHEST
HIGH = lax.Precision.HIGH


def split(value):
    high = lax.reduce_precision(value, 8, 7)
    return high.astype(jnp.bfloat16), (value - high).astype(jnp.bfloat16)


def kernel_dot(left, right, exact):
    if exact:
        return jnp.dot(left, right, preferred_element_type=jnp.float32, precision=HIGHEST)
    parts = []
    for value in (left, right):
        high = value.astype(jnp.bfloat16)
        parts.append((high, (value - high.astype(jnp.float32)).astype(jnp.bfloat16)))
    (a, b), (c, d) = parts
    return sum(
        jnp.dot(x, y, preferred_element_type=jnp.float32) for x, y in ((b, c), (a, d), (a, c))
    )


def eliminate(tiles, inv_ref):
    shape = (SUB, PANEL)
    lane = lax.broadcasted_iota(jnp.int32, shape, 1)
    sub = lax.broadcasted_iota(jnp.int32, shape, 0)

    def spread(column):
        return jnp.broadcast_to(column, shape)

    tiles = list(tiles)
    for s in range(PANEL // SUB):
        start = s * SUB
        tile = tiles[s]
        inside = (lane >= start) & (lane < start + SUB)
        columns = [spread(tile[:, start + c : start + c + 1]) for c in range(SUB)]
        pivot = [
            [spread(columns[c][i : i + 1, :]) if c >= i else None for c in range(SUB)]
            for i in range(SUB)
        ]
        base = jnp.where(inside, jnp.where(lane == start + sub, 1.0, 0.0), tile)
        rows = [spread(base[i : i + 1, :]) for i in range(SUB)]
        below = [[None] * SUB for _ in range(SUB)]
        inverse = []
        for b in range(0, SUB, 2):
            head, side, tail = pivot[b][b], pivot[b][b + 1], pivot[b + 1][b + 1]
            det = head * tail - side * side
            inverse.append(pl.reciprocal(head, approx=True))
            inverse.append(head * pl.reciprocal(det, approx=True))
            link = side * inverse[b]
            below[b + 1][b] = link
            rows[b + 1] = rows[b + 1] - link * rows[b]
            pivot[b + 1][b + 1] = det * inverse[b]
            for i in range(b + 2, SUB):
                pivot[b + 1][i] = pivot[b + 1][i] - link * pivot[b][i]
                below[i][b] = pivot[b][i] * inverse[b]
                below[i][b + 1] = pivot[b + 1][i] * inverse[b + 1]
            for i in range(b + 2, SUB):
                for c in range(i, SUB):
                    pivot[i][c] = (pivot[i][c] - below[i][b] * pivot[b][c]) - (
                        below[i][b + 1] * pivot[b + 1][c]
                    )
                rows[i] = (rows[i] - below[i][b] * rows[b]) - below[i][b + 1] * rows[b + 1]
        result = jnp.zeros(shape, jnp.float32)
        for b in range(SUB):
            result = jnp.where(sub == b, rows[b] * lax.rsqrt(pivot[b][b]), result)
        inv_ref[start : start + SUB, :] = jnp.where(lane < start + SUB, result, 0.0)
        solved = [None] * SUB
        for b in reversed(range(SUB)):
            value = rows[b] * inverse[b]
            for i in reversed(range(b + 1, SUB)):
                value = value - below[i][b] * solved[i]
            solved[b] = value
        for q in range(s + 1, PANEL // SUB):
            parts = [
                spread(tiles[q][:, start + b : start + b + 1]) * solved[b] for b in range(SUB)
            ]
            while len(parts) > 1:
                parts = [x + y for x, y in zip(parts[::2], parts[1::2])]
            tiles[q] = jnp.where(inside, 0.0, tiles[q]) - parts[0]


def factor_kernel(scale, exact, pos_ref, *refs):
    *piece_refs, out_ref, work_ref, inv_ref = refs
    rank = work_ref.shape[0]
    panels = rank // PANEL
    count = len(piece_refs)
    if count == 1:
        work_ref[...] = piece_refs[0][...] * scale
    else:
        work_ref[...] = jnp.zeros((rank, rank), jnp.float32)
    own_cols = rank // count
    for k in range(count if count > 1 else 0):
        for s in range(count):

            @pl.when(pos_ref[0] ^ k == s)
            def _():
                for d in range(piece_refs[k].shape[1] // own_cols):
                    other = (s + d) % count
                    block = piece_refs[k][:, d * own_cols : (d + 1) * own_cols] * scale
                    low, high = min(s, other), max(s, other)
                    if s > other and 2 * d == count:
                        continue
                    work_ref[
                        low * own_cols : (low + 1) * own_cols,
                        high * own_cols : (high + 1) * own_cols,
                    ] = block.T if s > other else block

    on_diag = lax.broadcasted_iota(jnp.int32, (PANEL, PANEL), 0) == lax.broadcasted_iota(
        jnp.int32, (PANEL, PANEL), 1
    )
    by_column = []
    for k in range(panels):
        panel = slice(k * PANEL, (k + 1) * PANEL)
        diag = jnp.where(on_diag, work_ref[panel, panel], 0.0)
        by_column.append(lax.rsqrt(jnp.sum(diag, axis=0, keepdims=True)))
        work_ref[panel, :] *= lax.rsqrt(jnp.sum(diag, axis=1, keepdims=True))
    for k in range(panels):
        work_ref[:, k * PANEL : (k + 1) * PANEL] *= by_column[k]

    def panel_step(k, carry):
        here = pl.ds(pl.multiple_of(k * PANEL, PANEL), PANEL)
        diag = work_ref[here, here]

        eliminate([diag[SUB * q : SUB * (q + 1), :] for q in range(PANEL // SUB)], inv_ref)
        for here_k in range(panels):

            @pl.when(k == here_k)
            def _():
                panel = slice(here_k * PANEL, (here_k + 1) * PANEL)
                rest = slice((here_k + 1) * PANEL, rank)
                inv = inv_ref[...]
                work_ref[panel, :] = kernel_dot(inv, work_ref[panel, :], exact)
                work_ref[panel, panel] = inv
                if here_k < panels - 1:
                    lower = work_ref[panel, rest].T
                    work_ref[rest, panel] = jnp.zeros((rank - rest.start, PANEL), jnp.float32)
                    work_ref[rest, :] -= kernel_dot(lower, work_ref[panel, :], exact)

        return carry

    lax.fori_loop(0, panels, panel_step, 0)
    for i in range(panels - 1):
        work_ref[i * PANEL : (i + 1) * PANEL, (i + 1) * PANEL :] = jnp.zeros(
            (PANEL, rank - (i + 1) * PANEL), jnp.float32
        )
    for k in range(panels):
        panel = slice(k * PANEL, (k + 1) * PANEL)
        out_ref[:, panel] = work_ref[:, panel] * by_column[k]


def inverse_factor(pieces, exact, scale):
    rank = pieces[0].shape[0] * len(pieces)
    pos = lax.axis_index("tok").astype(jnp.int32).reshape(1)
    return pl.pallas_call(
        functools.partial(factor_kernel, scale, exact),
        out_shape=jax.ShapeDtypeStruct((rank, rank), jnp.float32),
        in_specs=[
            pl.BlockSpec(memory_space=pltpu.SMEM),
            *[pl.BlockSpec(memory_space=pltpu.VMEM) for _ in pieces],
        ],
        out_specs=pl.BlockSpec(memory_space=pltpu.VMEM),
        scratch_shapes=[
            pltpu.VMEM((rank, rank), jnp.float32),
            pltpu.VMEM((PANEL, PANEL), jnp.float32),
        ],
        compiler_params=pltpu.CompilerParams(vmem_limit_bytes=32 * 1024 * 1024),
        cost_estimate=pl.CostEstimate(
            flops=96 * rank**3, bytes_accessed=8 * rank**2, transcendentals=0
        ),
        name="inverse_factor",
    )(pos, *pieces)


def swap(value, axis, k):
    if k == 0:
        return value
    return lax.ppermute(value, axis, [(i, i ^ k) for i in range(lax.axis_size(axis))])


def collect(value, axis):
    return [swap(value, axis, k) for k in range(lax.axis_size(axis))]


def per_device(acts, init_basis, kept, member):
    owned = init_basis.shape[0]
    slice_rows = init_basis.shape[1]
    rank = init_basis.shape[2]
    tok_count = lax.axis_size("tok")
    gr_count = lax.axis_size("gr")
    gc_count = lax.axis_size("gc")
    block_cols = slice_rows * tok_count
    tok_rows = acts.shape[0]
    total_tokens = tok_rows * tok_count
    groups = kept.shape[0] // GBLK
    assert groups == gr_count == 2
    group_cols = GBLK * block_cols
    own_cols = rank // tok_count
    tok_pos = lax.axis_index("tok")
    gr_pos = lax.axis_index("gr")
    gc_pos = lax.axis_index("gc")
    first = (gr_pos * gc_count + gc_pos) * owned
    links = ((member[:, None] == member[None, :]).astype(jnp.int32) * kept).astype(jnp.float32)
    own_links = lax.dynamic_slice_in_dim(links, first, owned, 0)
    partner = ((gr_pos ^ 1) * gc_count + gc_pos) * owned
    partner_links = lax.dynamic_slice_in_dim(links, partner, owned, 0)
    own_groups = lax.dynamic_slice_in_dim(member, first, owned, 0)

    own_x = acts.reshape(tok_rows, owned, block_cols)
    turned_x = jnp.concatenate(
        [
            lax.dynamic_slice_in_dim(own_x, (tok_pos ^ k) * slice_rows, slice_rows, 2)
            for k in range(tok_count)
        ],
        axis=2,
    )
    init_bf = init_basis.astype(jnp.bfloat16)
    width = rank // CHUNKS
    init_pieces = [
        collect(init_bf[:, :, c * width : (c + 1) * width], "tok") for c in range(CHUNKS)
    ]
    gathered_x = lax.all_gather(acts, "tok", axis=0, tiled=True)
    full_x = jnp.concatenate(
        [
            lax.dynamic_slice_in_dim(gathered_x, (tok_pos ^ k) * tok_rows, tok_rows, 0)
            for k in range(tok_count)
        ],
        axis=0,
    ).reshape(total_tokens, owned, block_cols)

    def combine(rows_of_links, pieces, sources):
        total = 0.0
        for piece, source in zip(pieces, sources):
            weights = lax.dynamic_slice_in_dim(rows_of_links, source, owned, 1)
            for j in range(owned):
                total += weights[:, j][:, None, None] * piece[j][None].astype(jnp.float32)
        return total

    near = []
    for part in init_pieces:
        proj = jnp.einsum(
            "tob,obr->otr",
            turned_x,
            jnp.concatenate(part, axis=1),
            preferred_element_type=jnp.float32,
        ).astype(jnp.bfloat16)
        near.append(collect(proj, "gc"))
    sources = [(gr_pos * gc_count + (gc_pos ^ b)) * owned for b in range(gc_count)]

    def mix(pieces):
        own = combine(own_links, pieces, sources)
        other = combine(partner_links, pieces, sources)
        return (own + swap(other, "gr", 1)).astype(jnp.bfloat16)

    mixed = jnp.concatenate([mix(pieces) for pieces in near], axis=2)
    basis_bf = jnp.concatenate(
        [
            jnp.concatenate(
                [lax.select_n(tok_pos ^ a, *part) for a in range(tok_count)], axis=1
            )
            for part in init_pieces
        ],
        axis=2,
    )

    def image_of(mixed, basis_bf):
        full = jnp.concatenate(collect(mixed, "tok"), axis=1)
        cover = jnp.einsum("tob,otr->obr", full_x, full, preferred_element_type=jnp.float32)
        return cover / total_tokens + ridge * basis_bf.astype(jnp.float32)

    def seen_by(image):
        return sum(
            jnp.einsum("tob,obr->otr", own_x, part, preferred_element_type=jnp.float32)
            for part in split(image)
        )

    def factor(image, last, beside):
        precision = HIGHEST if last else HIGH
        own = lax.dynamic_slice_in_dim(image, tok_pos * own_cols, own_cols, 2)
        grams = jnp.einsum("obr,obs->ors", own, image, precision=precision)

        def group_sum(g):
            mask = (own_groups == g).astype(jnp.float32)
            return jnp.sum(mask[:, None, None] * grams, axis=0)

        total = group_sum(gr_pos) + swap(group_sum(gr_pos ^ 1), "gr", 1)
        packed = tok_count == 4 and own_cols % PANEL == 0
        if packed:
            total = jnp.concatenate(
                [
                    lax.dynamic_slice_in_dim(
                        total, (tok_pos + d) % tok_count * own_cols, own_cols, 1
                    )
                    for d in range(tok_count // 2 + 1)
                ],
                axis=1,
            )
        step = 1
        while step < gc_count:
            if last and 2 * step == gc_count:
                total, beside = lax.optimization_barrier((total, beside))
            total += swap(total, "gc", step)
            step *= 2
        if not last:
            total, beside = lax.optimization_barrier((total, beside))
            beside = mix_seen(beside)
        if packed:
            pieces = collect(total, "tok")
        else:
            pieces = [lax.all_gather(total, "tok", axis=0, tiled=True)]
        own = inverse_factor(pieces, last, 1.0 / group_cols)
        other = swap(own, "gr", 1)
        if not last:
            other, beside = lax.optimization_barrier((other, beside))
        of_block = jnp.stack(
            [jnp.where(own_groups[o] == gr_pos, own, other) for o in range(owned)]
        )
        of_group = [jnp.where(gr_pos == g, own, other) for g in range(groups)]
        return of_block, of_group, beside

    image = image_of(mixed, basis_bf)
    def mix_seen(seen):
        seen = lax.all_gather(seen, ("gr", "gc"), axis=0, tiled=True)
        total = 0.0
        for j in range(seen.shape[0]):
            total += own_links[:, j][:, None, None] * seen[j][None]
        return total

    of_block, _, second = factor(image, False, seen_by(image))
    mixed = jnp.einsum("otr,osr->ots", second, of_block, precision=HIGH).astype(jnp.bfloat16)
    basis_bf = jnp.einsum("obr,osr->obs", image, of_block, precision=HIGH).astype(jnp.bfloat16)
    image = image_of(mixed, basis_bf)
    codes = seen_by(image)
    placed = jnp.concatenate(
        [
            jnp.sum((own_groups == g).astype(jnp.float32)[:, None, None] * codes, axis=0)
            for g in range(groups)
        ],
        axis=1,
    )
    of_block, of_group, placed = factor(image, True, placed)
    rows = lax.dynamic_slice_in_dim(image, tok_pos * slice_rows, slice_rows, 1)
    basis = jnp.einsum("obr,osr->obs", rows, of_block, precision=HIGH)
    placed = lax.psum_scatter(placed, ("gr", "gc"), scatter_dimension=0, tiled=True)
    latent = jnp.concatenate(
        [
            jnp.einsum(
                "tr,sr->ts",
                placed[:, g * rank : (g + 1) * rank],
                of_group[g],
                precision=HIGH,
            )
            for g in range(groups)
        ],
        axis=1,
    )
    latent = latent * (1.0 / math.sqrt(group_cols))
    return (basis, latent.astype(jnp.bfloat16))


def solution(mesh):
    placed = (P("tok", ("gr", "gc")), P(("gr", "gc"), "tok", None), P(), P())
    return jax.shard_map(
        per_device,
        mesh=mesh,
        in_specs=placed,
        out_specs=(P(("gr", "gc"), "tok", None), P(("tok", "gr", "gc"), None)),
        check_vma=False,
    )
```

```python
import functools
import math

import jax
import jax.numpy as jnp
from jax import lax
from jax.experimental import pallas as pl
from jax.experimental.pallas import tpu as pltpu
from jax.sharding import PartitionSpec as P

GBLK = 8
PANEL = 128
SUB = 8
CHUNKS = 2

ridge = 2.0
HIGHEST = lax.Precision.HIGHEST
HIGH = lax.Precision.HIGH


def split(value):
    high = lax.reduce_precision(value, 8, 7)
    return high.astype(jnp.bfloat16), (value - high).astype(jnp.bfloat16)


def kernel_dot(left, right, exact):
    if exact:
        return jnp.dot(left, right, preferred_element_type=jnp.float32, precision=HIGHEST)
    parts = []
    for value in (left, right):
        high = value.astype(jnp.bfloat16)
        parts.append((high, (value - high.astype(jnp.float32)).astype(jnp.bfloat16)))
    (a, b), (c, d) = parts
    return sum(
        jnp.dot(x, y, preferred_element_type=jnp.float32) for x, y in ((b, c), (a, d), (a, c))
    )


def eliminate(tiles, inv_ref):
    shape = (SUB, PANEL)
    lane = lax.broadcasted_iota(jnp.int32, shape, 1)
    sub = lax.broadcasted_iota(jnp.int32, shape, 0)

    def spread(column):
        return jnp.broadcast_to(column, shape)

    tiles = list(tiles)
    for s in range(PANEL // SUB):
        start = s * SUB
        tile = tiles[s]
        inside = (lane >= start) & (lane < start + SUB)
        columns = [spread(tile[:, start + c : start + c + 1]) for c in range(SUB)]
        pivot = [
            [spread(columns[c][i : i + 1, :]) if c >= i else None for c in range(SUB)]
            for i in range(SUB)
        ]
        base = jnp.where(inside, jnp.where(lane == start + sub, 1.0, 0.0), tile)
        rows = [spread(base[i : i + 1, :]) for i in range(SUB)]
        below = [[None] * SUB for _ in range(SUB)]
        inverse = []
        for b in range(0, SUB, 2):
            head, side, tail = pivot[b][b], pivot[b][b + 1], pivot[b + 1][b + 1]
            det = head * tail - side * side
            inverse.append(pl.reciprocal(head, approx=True))
            inverse.append(head * pl.reciprocal(det, approx=True))
            link = side * inverse[b]
            below[b + 1][b] = link
            rows[b + 1] = rows[b + 1] - link * rows[b]
            pivot[b + 1][b + 1] = det * inverse[b]
            for i in range(b + 2, SUB):
                pivot[b + 1][i] = pivot[b + 1][i] - link * pivot[b][i]
                below[i][b] = pivot[b][i] * inverse[b]
                below[i][b + 1] = pivot[b + 1][i] * inverse[b + 1]
            for i in range(b + 2, SUB):
                for c in range(i, SUB):
                    pivot[i][c] = (pivot[i][c] - below[i][b] * pivot[b][c]) - (
                        below[i][b + 1] * pivot[b + 1][c]
                    )
                rows[i] = (rows[i] - below[i][b] * rows[b]) - below[i][b + 1] * rows[b + 1]
        result = jnp.zeros(shape, jnp.float32)
        for b in range(SUB):
            result = jnp.where(sub == b, rows[b] * lax.rsqrt(pivot[b][b]), result)
        inv_ref[start : start + SUB, :] = jnp.where(lane < start + SUB, result, 0.0)
        solved = [None] * SUB
        for b in reversed(range(SUB)):
            value = rows[b] * inverse[b]
            for i in reversed(range(b + 1, SUB)):
                value = value - below[i][b] * solved[i]
            solved[b] = value
        for q in range(s + 1, PANEL // SUB):
            parts = [
                spread(tiles[q][:, start + b : start + b + 1]) * solved[b] for b in range(SUB)
            ]
            while len(parts) > 1:
                parts = [x + y for x, y in zip(parts[::2], parts[1::2])]
            tiles[q] = jnp.where(inside, 0.0, tiles[q]) - parts[0]


def factor_kernel(scale, exact, pos_ref, *refs):
    *piece_refs, out_ref, work_ref, inv_ref = refs
    rank = work_ref.shape[0]
    panels = rank // PANEL
    count = len(piece_refs)
    if count == 1:
        work_ref[...] = piece_refs[0][...] * scale
    else:
        work_ref[...] = jnp.zeros((rank, rank), jnp.float32)
    own_cols = rank // count
    for k in range(count if count > 1 else 0):
        for s in range(count):

            @pl.when(pos_ref[0] ^ k == s)
            def _():
                for d in range(piece_refs[k].shape[1] // own_cols):
                    other = (s + d) % count
                    block = piece_refs[k][:, d * own_cols : (d + 1) * own_cols] * scale
                    low, high = min(s, other), max(s, other)
                    if s > other and 2 * d == count:
                        continue
                    work_ref[
                        low * own_cols : (low + 1) * own_cols,
                        high * own_cols : (high + 1) * own_cols,
                    ] = block.T if s > other else block

    on_diag = lax.broadcasted_iota(jnp.int32, (PANEL, PANEL), 0) == lax.broadcasted_iota(
        jnp.int32, (PANEL, PANEL), 1
    )
    by_column = []
    for k in range(panels):
        panel = slice(k * PANEL, (k + 1) * PANEL)
        diag = jnp.where(on_diag, work_ref[panel, panel], 0.0)
        by_column.append(lax.rsqrt(jnp.sum(diag, axis=0, keepdims=True)))
        work_ref[panel, :] *= lax.rsqrt(jnp.sum(diag, axis=1, keepdims=True))
    for k in range(panels):
        work_ref[:, k * PANEL : (k + 1) * PANEL] *= by_column[k]

    def panel_step(k, carry):
        here = pl.ds(pl.multiple_of(k * PANEL, PANEL), PANEL)
        diag = work_ref[here, here]

        eliminate([diag[SUB * q : SUB * (q + 1), :] for q in range(PANEL // SUB)], inv_ref)
        for here_k in range(panels):

            @pl.when(k == here_k)
            def _():
                panel = slice(here_k * PANEL, (here_k + 1) * PANEL)
                rest = slice((here_k + 1) * PANEL, rank)
                inv = inv_ref[...]
                work_ref[panel, :] = kernel_dot(inv, work_ref[panel, :], exact)
                work_ref[panel, panel] = inv
                if here_k < panels - 1:
                    lower = work_ref[panel, rest].T
                    work_ref[rest, panel] = jnp.zeros((rank - rest.start, PANEL), jnp.float32)
                    work_ref[rest, :] -= kernel_dot(lower, work_ref[panel, :], exact)

        return carry

    lax.fori_loop(0, panels, panel_step, 0)
    for i in range(panels - 1):
        work_ref[i * PANEL : (i + 1) * PANEL, (i + 1) * PANEL :] = jnp.zeros(
            (PANEL, rank - (i + 1) * PANEL), jnp.float32
        )
    for k in range(panels):
        panel = slice(k * PANEL, (k + 1) * PANEL)
        out_ref[:, panel] = work_ref[:, panel] * by_column[k]


def inverse_factor(pieces, exact, scale):
    rank = pieces[0].shape[0] * len(pieces)
    pos = lax.axis_index("tok").astype(jnp.int32).reshape(1)
    return pl.pallas_call(
        functools.partial(factor_kernel, scale, exact),
        out_shape=jax.ShapeDtypeStruct((rank, rank), jnp.float32),
        in_specs=[
            pl.BlockSpec(memory_space=pltpu.SMEM),
            *[pl.BlockSpec(memory_space=pltpu.VMEM) for _ in pieces],
        ],
        out_specs=pl.BlockSpec(memory_space=pltpu.VMEM),
        scratch_shapes=[
            pltpu.VMEM((rank, rank), jnp.float32),
            pltpu.VMEM((PANEL, PANEL), jnp.float32),
        ],
        compiler_params=pltpu.CompilerParams(vmem_limit_bytes=32 * 1024 * 1024),
        cost_estimate=pl.CostEstimate(
            flops=96 * rank**3, bytes_accessed=8 * rank**2, transcendentals=0
        ),
        name="inverse_factor",
    )(pos, *pieces)


def swap(value, axis, k):
    if k == 0:
        return value
    return lax.ppermute(value, axis, [(i, i ^ k) for i in range(lax.axis_size(axis))])


def collect(value, axis):
    return [swap(value, axis, k) for k in range(lax.axis_size(axis))]


def per_device(acts, init_basis, kept, member):
    owned = init_basis.shape[0]
    slice_rows = init_basis.shape[1]
    rank = init_basis.shape[2]
    tok_count = lax.axis_size("tok")
    gr_count = lax.axis_size("gr")
    gc_count = lax.axis_size("gc")
    block_cols = slice_rows * tok_count
    tok_rows = acts.shape[0]
    total_tokens = tok_rows * tok_count
    groups = kept.shape[0] // GBLK
    assert groups == gr_count == 2
    group_cols = GBLK * block_cols
    own_cols = rank // tok_count
    tok_pos = lax.axis_index("tok")
    gr_pos = lax.axis_index("gr")
    gc_pos = lax.axis_index("gc")
    first = (gr_pos * gc_count + gc_pos) * owned
    links = ((member[:, None] == member[None, :]).astype(jnp.int32) * kept).astype(jnp.float32)
    own_links = lax.dynamic_slice_in_dim(links, first, owned, 0)
    partner = ((gr_pos ^ 1) * gc_count + gc_pos) * owned
    partner_links = lax.dynamic_slice_in_dim(links, partner, owned, 0)
    own_groups = lax.dynamic_slice_in_dim(member, first, owned, 0)

    own_x = acts.reshape(tok_rows, owned, block_cols)
    turned_x = jnp.concatenate(
        [
            lax.dynamic_slice_in_dim(own_x, (tok_pos ^ k) * slice_rows, slice_rows, 2)
            for k in range(tok_count)
        ],
        axis=2,
    )
    init_bf = init_basis.astype(jnp.bfloat16)
    width = rank // CHUNKS
    init_pieces = [
        collect(init_bf[:, :, c * width : (c + 1) * width], "tok") for c in range(CHUNKS)
    ]
    gathered_x = lax.all_gather(acts, "tok", axis=0, tiled=True)
    full_x = jnp.concatenate(
        [
            lax.dynamic_slice_in_dim(gathered_x, (tok_pos ^ k) * tok_rows, tok_rows, 0)
            for k in range(tok_count)
        ],
        axis=0,
    ).reshape(total_tokens, owned, block_cols)

    def combine(rows_of_links, pieces, sources):
        total = 0.0
        for piece, source in zip(pieces, sources):
            weights = lax.dynamic_slice_in_dim(rows_of_links, source, owned, 1)
            for j in range(owned):
                total += weights[:, j][:, None, None] * piece[j][None].astype(jnp.float32)
        return total

    near = []
    for part in init_pieces:
        proj = jnp.einsum(
            "tob,obr->otr",
            turned_x,
            jnp.concatenate(part, axis=1),
            preferred_element_type=jnp.float32,
        ).astype(jnp.bfloat16)
        near.append(collect(proj, "gc"))
    sources = [(gr_pos * gc_count + (gc_pos ^ b)) * owned for b in range(gc_count)]

    def mix(pieces):
        own = combine(own_links, pieces, sources)
        other = combine(partner_links, pieces, sources)
        return (own + swap(other, "gr", 1)).astype(jnp.bfloat16)

    mixed = jnp.concatenate([mix(pieces) for pieces in near], axis=2)
    basis_bf = jnp.concatenate(
        [
            jnp.concatenate(
                [lax.select_n(tok_pos ^ a, *part) for a in range(tok_count)], axis=1
            )
            for part in init_pieces
        ],
        axis=2,
    )

    def image_of(*operands):
        *parts, basis_bf = operands
        full = jnp.concatenate(
            [jnp.concatenate(collect(part, "tok"), axis=1) for part in parts], axis=2
        )
        cover = jnp.einsum("tob,otr->obr", full_x, full, preferred_element_type=jnp.float32)
        return cover / total_tokens + ridge * basis_bf.astype(jnp.float32)

    def seen_by(image):
        return sum(
            jnp.einsum("tob,obr->otr", own_x, part, preferred_element_type=jnp.float32)
            for part in split(image)
        )

    def factor(image, last, beside):
        precision = HIGHEST if last else HIGH
        own = lax.dynamic_slice_in_dim(image, tok_pos * own_cols, own_cols, 2)
        grams = jnp.einsum("obr,obs->ors", own, image, precision=precision)

        def group_sum(g):
            mask = (own_groups == g).astype(jnp.float32)
            return jnp.sum(mask[:, None, None] * grams, axis=0)

        total = group_sum(gr_pos) + swap(group_sum(gr_pos ^ 1), "gr", 1)
        packed = tok_count == 4 and own_cols % PANEL == 0
        if packed:
            total = jnp.concatenate(
                [
                    lax.dynamic_slice_in_dim(
                        total, (tok_pos + d) % tok_count * own_cols, own_cols, 1
                    )
                    for d in range(tok_count // 2 + 1)
                ],
                axis=1,
            )
        step = 1
        while step < gc_count:
            if last and 2 * step == gc_count:
                total, beside = lax.optimization_barrier((total, beside))
            total += swap(total, "gc", step)
            step *= 2
        if not last:
            total, beside = lax.optimization_barrier((total, beside))
            beside = mix_seen(beside)
        if packed:
            pieces = collect(total, "tok")
        else:
            pieces = [lax.all_gather(total, "tok", axis=0, tiled=True)]
        own = inverse_factor(pieces, last, 1.0 / group_cols)
        other = swap(own, "gr", 1)
        if not last:
            other, beside = lax.optimization_barrier((other, beside))
        of_block = jnp.stack(
            [jnp.where(own_groups[o] == gr_pos, own, other) for o in range(owned)]
        )
        of_group = [jnp.where(gr_pos == g, own, other) for g in range(groups)]
        return of_block, of_group, beside

    image = image_of(mixed, basis_bf)
    wide = rank // 2

    def mix_seen(seen):
        pieces = lax.all_gather(seen[:, :, :wide], ("gr", "gc"), axis=0, tiled=True)
        total = 0.0
        for j in range(pieces.shape[0]):
            total += own_links[:, j][:, None, None] * pieces[j][None]
        return total

    seen = seen_by(image)
    of_block, _, second = factor(image, False, seen)
    proj = jnp.einsum("otr,osr->ots", seen, of_block[:, wide:], precision=HIGH)
    proj = proj.astype(jnp.bfloat16)
    first_part = jnp.einsum(
        "otr,osr->ots", second, of_block[:, :wide, :wide], precision=HIGH
    ).astype(jnp.bfloat16)
    last_part = mix(collect(proj, "gc"))
    basis_bf = jnp.einsum("obr,osr->obs", image, of_block, precision=HIGH).astype(jnp.bfloat16)
    image = image_of(first_part, last_part, basis_bf)
    codes = seen_by(image)
    placed = jnp.concatenate(
        [
            jnp.sum((own_groups == g).astype(jnp.float32)[:, None, None] * codes, axis=0)
            for g in range(groups)
        ],
        axis=1,
    )
    of_block, of_group, placed = factor(image, True, placed)
    rows = lax.dynamic_slice_in_dim(image, tok_pos * slice_rows, slice_rows, 1)
    basis = jnp.einsum("obr,osr->obs", rows, of_block, precision=HIGH)
    placed = lax.psum_scatter(placed, ("gr", "gc"), scatter_dimension=0, tiled=True)
    latent = jnp.concatenate(
        [
            jnp.einsum(
                "tr,sr->ts",
                placed[:, g * rank : (g + 1) * rank],
                of_group[g],
                precision=HIGH,
            )
            for g in range(groups)
        ],
        axis=1,
    )
    latent = latent * (1.0 / math.sqrt(group_cols))
    return (basis, latent.astype(jnp.bfloat16))


def solution(mesh):
    placed = (P("tok", ("gr", "gc")), P(("gr", "gc"), "tok", None), P(), P())
    return jax.shard_map(
        per_device,
        mesh=mesh,
        in_specs=placed,
        out_specs=(P(("gr", "gc"), "tok", None), P(("tok", "gr", "gc"), None)),
        check_vma=False,
    )
```

```python
import functools
import math

import jax
import jax.numpy as jnp
from jax import lax
from jax.experimental import pallas as pl
from jax.experimental.pallas import tpu as pltpu
from jax.sharding import PartitionSpec as P

GBLK = 8
PANEL = 128
SUB = 8
CHUNKS = 2

ridge = 2.0
HIGHEST = lax.Precision.HIGHEST
HIGH = lax.Precision.HIGH


def split(value):
    high = lax.reduce_precision(value, 8, 7)
    return high.astype(jnp.bfloat16), (value - high).astype(jnp.bfloat16)


def kernel_dot(left, right, exact):
    if exact:
        return jnp.dot(left, right, preferred_element_type=jnp.float32, precision=HIGHEST)
    parts = []
    for value in (left, right):
        high = value.astype(jnp.bfloat16)
        parts.append((high, (value - high.astype(jnp.float32)).astype(jnp.bfloat16)))
    (a, b), (c, d) = parts
    return sum(
        jnp.dot(x, y, preferred_element_type=jnp.float32) for x, y in ((b, c), (a, d), (a, c))
    )


def eliminate(tiles, inv_ref):
    shape = (SUB, PANEL)
    lane = lax.broadcasted_iota(jnp.int32, shape, 1)
    sub = lax.broadcasted_iota(jnp.int32, shape, 0)

    def spread(column):
        return jnp.broadcast_to(column, shape)

    tiles = list(tiles)
    for s in range(PANEL // SUB):
        start = s * SUB
        tile = tiles[s]
        inside = (lane >= start) & (lane < start + SUB)
        columns = [spread(tile[:, start + c : start + c + 1]) for c in range(SUB)]
        pivot = [
            [spread(columns[c][i : i + 1, :]) if c >= i else None for c in range(SUB)]
            for i in range(SUB)
        ]
        base = jnp.where(inside, jnp.where(lane == start + sub, 1.0, 0.0), tile)
        rows = [spread(base[i : i + 1, :]) for i in range(SUB)]
        below = [[None] * SUB for _ in range(SUB)]
        inverse = []
        for b in range(0, SUB, 2):
            head, side, tail = pivot[b][b], pivot[b][b + 1], pivot[b + 1][b + 1]
            det = head * tail - side * side
            inverse.append(pl.reciprocal(head, approx=True))
            inverse.append(head * pl.reciprocal(det, approx=True))
            link = side * inverse[b]
            below[b + 1][b] = link
            rows[b + 1] = rows[b + 1] - link * rows[b]
            pivot[b + 1][b + 1] = det * inverse[b]
            for i in range(b + 2, SUB):
                pivot[b + 1][i] = pivot[b + 1][i] - link * pivot[b][i]
                below[i][b] = pivot[b][i] * inverse[b]
                below[i][b + 1] = pivot[b + 1][i] * inverse[b + 1]
            for i in range(b + 2, SUB):
                for c in range(i, SUB):
                    pivot[i][c] = (pivot[i][c] - below[i][b] * pivot[b][c]) - (
                        below[i][b + 1] * pivot[b + 1][c]
                    )
                rows[i] = (rows[i] - below[i][b] * rows[b]) - below[i][b + 1] * rows[b + 1]
        result = jnp.zeros(shape, jnp.float32)
        for b in range(SUB):
            result = jnp.where(sub == b, rows[b] * lax.rsqrt(pivot[b][b]), result)
        inv_ref[start : start + SUB, :] = jnp.where(lane < start + SUB, result, 0.0)
        solved = [None] * SUB
        for b in reversed(range(SUB)):
            value = rows[b] * inverse[b]
            for i in reversed(range(b + 1, SUB)):
                value = value - below[i][b] * solved[i]
            solved[b] = value
        for q in range(s + 1, PANEL // SUB):
            parts = [
                spread(tiles[q][:, start + b : start + b + 1]) * solved[b] for b in range(SUB)
            ]
            while len(parts) > 1:
                parts = [x + y for x, y in zip(parts[::2], parts[1::2])]
            tiles[q] = jnp.where(inside, 0.0, tiles[q]) - parts[0]


def factor_kernel(scale, exact, pos_ref, *refs):
    *piece_refs, out_ref, work_ref, inv_ref = refs
    rank = work_ref.shape[0]
    panels = rank // PANEL
    count = len(piece_refs)
    if count == 1:
        work_ref[...] = piece_refs[0][...] * scale
    else:
        work_ref[...] = jnp.zeros((rank, rank), jnp.float32)
    own_cols = rank // count
    for k in range(count if count > 1 else 0):
        for s in range(count):

            @pl.when(pos_ref[0] ^ k == s)
            def _():
                for d in range(piece_refs[k].shape[1] // own_cols):
                    other = (s + d) % count
                    block = piece_refs[k][:, d * own_cols : (d + 1) * own_cols] * scale
                    low, high = min(s, other), max(s, other)
                    if s > other and 2 * d == count:
                        continue
                    work_ref[
                        low * own_cols : (low + 1) * own_cols,
                        high * own_cols : (high + 1) * own_cols,
                    ] = block.T if s > other else block

    on_diag = lax.broadcasted_iota(jnp.int32, (PANEL, PANEL), 0) == lax.broadcasted_iota(
        jnp.int32, (PANEL, PANEL), 1
    )
    by_column = []
    for k in range(panels):
        panel = slice(k * PANEL, (k + 1) * PANEL)
        diag = jnp.where(on_diag, work_ref[panel, panel], 0.0)
        by_column.append(lax.rsqrt(jnp.sum(diag, axis=0, keepdims=True)))
        work_ref[panel, :] *= lax.rsqrt(jnp.sum(diag, axis=1, keepdims=True))
    for k in range(panels):
        work_ref[:, k * PANEL : (k + 1) * PANEL] *= by_column[k]

    def panel_step(k, carry):
        here = pl.ds(pl.multiple_of(k * PANEL, PANEL), PANEL)
        diag = work_ref[here, here]

        eliminate([diag[SUB * q : SUB * (q + 1), :] for q in range(PANEL // SUB)], inv_ref)
        for here_k in range(panels):

            @pl.when(k == here_k)
            def _():
                panel = slice(here_k * PANEL, (here_k + 1) * PANEL)
                rest = slice((here_k + 1) * PANEL, rank)
                inv = inv_ref[...]
                work_ref[panel, :] = kernel_dot(inv, work_ref[panel, :], exact)
                work_ref[panel, panel] = inv
                if here_k < panels - 1:
                    lower = work_ref[panel, rest].T
                    work_ref[rest, panel] = jnp.zeros((rank - rest.start, PANEL), jnp.float32)
                    work_ref[rest, :] -= kernel_dot(lower, work_ref[panel, :], exact)

        return carry

    lax.fori_loop(0, panels, panel_step, 0)
    for i in range(panels - 1):
        work_ref[i * PANEL : (i + 1) * PANEL, (i + 1) * PANEL :] = jnp.zeros(
            (PANEL, rank - (i + 1) * PANEL), jnp.float32
        )
    for k in range(panels):
        panel = slice(k * PANEL, (k + 1) * PANEL)
        out_ref[:, panel] = work_ref[:, panel] * by_column[k]


def inverse_factor(pieces, exact, scale):
    rank = pieces[0].shape[0] * len(pieces)
    pos = lax.axis_index("tok").astype(jnp.int32).reshape(1)
    return pl.pallas_call(
        functools.partial(factor_kernel, scale, exact),
        out_shape=jax.ShapeDtypeStruct((rank, rank), jnp.float32),
        in_specs=[
            pl.BlockSpec(memory_space=pltpu.SMEM),
            *[pl.BlockSpec(memory_space=pltpu.VMEM) for _ in pieces],
        ],
        out_specs=pl.BlockSpec(memory_space=pltpu.VMEM),
        scratch_shapes=[
            pltpu.VMEM((rank, rank), jnp.float32),
            pltpu.VMEM((PANEL, PANEL), jnp.float32),
        ],
        compiler_params=pltpu.CompilerParams(vmem_limit_bytes=32 * 1024 * 1024),
        cost_estimate=pl.CostEstimate(
            flops=96 * rank**3, bytes_accessed=8 * rank**2, transcendentals=0
        ),
        name="inverse_factor",
    )(pos, *pieces)


def swap(value, axis, k):
    if k == 0:
        return value
    return lax.ppermute(value, axis, [(i, i ^ k) for i in range(lax.axis_size(axis))])


def collect(value, axis):
    return [swap(value, axis, k) for k in range(lax.axis_size(axis))]


def per_device(acts, init_basis, kept, member):
    owned = init_basis.shape[0]
    slice_rows = init_basis.shape[1]
    rank = init_basis.shape[2]
    tok_count = lax.axis_size("tok")
    gr_count = lax.axis_size("gr")
    gc_count = lax.axis_size("gc")
    block_cols = slice_rows * tok_count
    tok_rows = acts.shape[0]
    total_tokens = tok_rows * tok_count
    groups = kept.shape[0] // GBLK
    assert groups == gr_count == 2
    group_cols = GBLK * block_cols
    own_cols = rank // tok_count
    tok_pos = lax.axis_index("tok")
    gr_pos = lax.axis_index("gr")
    gc_pos = lax.axis_index("gc")
    first = (gr_pos * gc_count + gc_pos) * owned
    links = ((member[:, None] == member[None, :]).astype(jnp.int32) * kept).astype(jnp.float32)
    own_links = lax.dynamic_slice_in_dim(links, first, owned, 0)
    partner = ((gr_pos ^ 1) * gc_count + gc_pos) * owned
    partner_links = lax.dynamic_slice_in_dim(links, partner, owned, 0)
    own_groups = lax.dynamic_slice_in_dim(member, first, owned, 0)

    own_x = acts.reshape(tok_rows, owned, block_cols)
    turned_x = jnp.concatenate(
        [
            lax.dynamic_slice_in_dim(own_x, (tok_pos ^ k) * slice_rows, slice_rows, 2)
            for k in range(tok_count)
        ],
        axis=2,
    )
    init_bf = init_basis.astype(jnp.bfloat16)
    width = rank // CHUNKS
    init_pieces = [
        collect(init_bf[:, :, c * width : (c + 1) * width], "tok") for c in range(CHUNKS)
    ]
    gathered_x = lax.all_gather(acts, "tok", axis=0, tiled=True)
    full_x = jnp.concatenate(
        [
            lax.dynamic_slice_in_dim(gathered_x, (tok_pos ^ k) * tok_rows, tok_rows, 0)
            for k in range(tok_count)
        ],
        axis=0,
    ).reshape(total_tokens, owned, block_cols)

    def combine(rows_of_links, pieces, sources):
        total = 0.0
        for piece, source in zip(pieces, sources):
            weights = lax.dynamic_slice_in_dim(rows_of_links, source, owned, 1)
            for j in range(owned):
                total += weights[:, j][:, None, None] * piece[j][None].astype(jnp.float32)
        return total

    near = []
    for part in init_pieces:
        proj = jnp.einsum(
            "tob,obr->otr",
            turned_x,
            jnp.concatenate(part, axis=1),
            preferred_element_type=jnp.float32,
        ).astype(jnp.bfloat16)
        near.append(collect(proj, "gc"))
    sources = [(gr_pos * gc_count + (gc_pos ^ b)) * owned for b in range(gc_count)]

    def mix(pieces):
        own = combine(own_links, pieces, sources)
        other = combine(partner_links, pieces, sources)
        return (own + swap(other, "gr", 1)).astype(jnp.bfloat16)

    mixed = jnp.concatenate([mix(pieces) for pieces in near], axis=2)
    basis_bf = jnp.concatenate(
        [
            jnp.concatenate(
                [lax.select_n(tok_pos ^ a, *part) for a in range(tok_count)], axis=1
            )
            for part in init_pieces
        ],
        axis=2,
    )

    def image_of(*operands):
        *parts, basis_bf = operands
        full = jnp.concatenate(
            [jnp.concatenate(part, axis=1) for part in parts], axis=2
        )
        cover = jnp.einsum("tob,otr->obr", full_x, full, preferred_element_type=jnp.float32)
        return cover / total_tokens + ridge * basis_bf.astype(jnp.float32)

    def seen_by(image):
        return sum(
            jnp.einsum("tob,obr->otr", own_x, part, preferred_element_type=jnp.float32)
            for part in split(image)
        )

    def half_over_gr(value):
        half = value.shape[0] // 2
        own = lax.dynamic_slice_in_dim(value, gr_pos * half, half, 0)
        other = lax.dynamic_slice_in_dim(value, (gr_pos ^ 1) * half, half, 0)
        return own + swap(other, "gr", 1)

    def factor(image, last, beside):
        precision = HIGHEST if last else HIGH
        own = lax.dynamic_slice_in_dim(image, tok_pos * own_cols, own_cols, 2)
        grams = jnp.einsum("obr,obs->ors", own, image, precision=precision)

        def group_sum(g):
            mask = (own_groups == g).astype(jnp.float32)
            return jnp.sum(mask[:, None, None] * grams, axis=0)

        total = group_sum(gr_pos) + swap(group_sum(gr_pos ^ 1), "gr", 1)
        packed = tok_count == 4 and own_cols % PANEL == 0
        if packed:
            total = jnp.concatenate(
                [
                    lax.dynamic_slice_in_dim(
                        total, (tok_pos + d) % tok_count * own_cols, own_cols, 1
                    )
                    for d in range(tok_count // 2 + 1)
                ],
                axis=1,
            )
        step = 1
        while step < gc_count:
            if last and 2 * step == gc_count:
                total, beside = lax.optimization_barrier((total, beside))
                beside = half_over_gr(beside)
            total += swap(total, "gc", step)
            step *= 2
        total, beside = lax.optimization_barrier((total, beside))
        if not last:
            beside = mix_seen(beside)
        if packed:
            pieces = collect(total, "tok")
        else:
            pieces = [lax.all_gather(total, "tok", axis=0, tiled=True)]
        own = inverse_factor(pieces, last, 1.0 / group_cols)
        other = swap(own, "gr", 1)
        if not last:
            other, beside = lax.optimization_barrier((other, beside))
        of_block = jnp.stack(
            [jnp.where(own_groups[o] == gr_pos, own, other) for o in range(owned)]
        )
        of_group = [jnp.where(gr_pos == g, own, other) for g in range(groups)]
        return of_block, of_group, beside

    image = image_of(collect(mixed, "tok"), basis_bf)
    wide = rank // 2

    def mix_seen(seen):
        pieces = lax.all_gather(seen[:, :, :wide], ("gr", "gc"), axis=0, tiled=True)
        total = 0.0
        for j in range(pieces.shape[0]):
            total += own_links[:, j][:, None, None] * pieces[j][None]
        return total

    seen = seen_by(image)
    of_block, _, second = factor(image, False, seen)
    proj = jnp.einsum("otr,osr->ots", seen, of_block[:, wide:], precision=HIGH)
    proj = proj.astype(jnp.bfloat16)
    first_part = jnp.einsum(
        "otr,osr->ots", second, of_block[:, :wide, :wide], precision=HIGH
    ).astype(jnp.bfloat16)
    near, first_pieces = lax.optimization_barrier((collect(proj, "gc"), collect(first_part, "tok")))
    last_pieces = collect(mix(near), "tok")
    basis_bf = jnp.einsum("obr,osr->obs", image, of_block, precision=HIGH).astype(jnp.bfloat16)
    image = image_of(first_pieces, last_pieces, basis_bf)
    codes = seen_by(image)
    placed = jnp.concatenate(
        [
            jnp.sum((own_groups == g).astype(jnp.float32)[:, None, None] * codes, axis=0)
            for g in range(groups)
        ],
        axis=1,
    )
    of_block, of_group, placed = factor(image, True, placed)
    rows = lax.dynamic_slice_in_dim(image, tok_pos * slice_rows, slice_rows, 1)
    basis = jnp.einsum("obr,osr->obs", rows, of_block, precision=HIGH)
    placed = lax.psum_scatter(placed, "gc", scatter_dimension=0, tiled=True)
    latent = jnp.concatenate(
        [
            jnp.einsum(
                "tr,sr->ts",
                placed[:, g * rank : (g + 1) * rank],
                of_group[g],
                precision=HIGH,
            )
            for g in range(groups)
        ],
        axis=1,
    )
    latent = latent * (1.0 / math.sqrt(group_cols))
    return (basis, latent.astype(jnp.bfloat16))


def solution(mesh):
    placed = (P("tok", ("gr", "gc")), P(("gr", "gc"), "tok", None), P(), P())
    return jax.shard_map(
        per_device,
        mesh=mesh,
        in_specs=placed,
        out_specs=(P(("gr", "gc"), "tok", None), P(("tok", "gr", "gc"), None)),
        check_vma=False,
    )
```

```python
import functools
import math

import jax
import jax.numpy as jnp
from jax import lax
from jax.experimental import pallas as pl
from jax.experimental.pallas import tpu as pltpu
from jax.sharding import PartitionSpec as P

GBLK = 8
PANEL = 128
SUB = 8
CHUNKS = 2

ridge = 2.0
HIGHEST = lax.Precision.HIGHEST
HIGH = lax.Precision.HIGH


def split(value):
    high = lax.reduce_precision(value, 8, 7)
    return high.astype(jnp.bfloat16), (value - high).astype(jnp.bfloat16)


def kernel_dot(left, right, exact):
    if exact:
        return jnp.dot(left, right, preferred_element_type=jnp.float32, precision=HIGHEST)
    parts = []
    for value in (left, right):
        high = value.astype(jnp.bfloat16)
        parts.append((high, (value - high.astype(jnp.float32)).astype(jnp.bfloat16)))
    (a, b), (c, d) = parts
    return sum(
        jnp.dot(x, y, preferred_element_type=jnp.float32) for x, y in ((b, c), (a, d), (a, c))
    )


def eliminate(tiles, inv_ref):
    shape = (SUB, PANEL)
    lane = lax.broadcasted_iota(jnp.int32, shape, 1)
    sub = lax.broadcasted_iota(jnp.int32, shape, 0)

    def spread(column):
        return jnp.broadcast_to(column, shape)

    tiles = list(tiles)
    for s in range(PANEL // SUB):
        start = s * SUB
        tile = tiles[s]
        inside = (lane >= start) & (lane < start + SUB)
        columns = [spread(tile[:, start + c : start + c + 1]) for c in range(SUB)]
        pivot = [
            [spread(columns[c][i : i + 1, :]) if c >= i else None for c in range(SUB)]
            for i in range(SUB)
        ]
        base = jnp.where(inside, jnp.where(lane == start + sub, 1.0, 0.0), tile)
        rows = [spread(base[i : i + 1, :]) for i in range(SUB)]
        below = [[None] * SUB for _ in range(SUB)]
        inverse = []
        for b in range(0, SUB, 2):
            head, side, tail = pivot[b][b], pivot[b][b + 1], pivot[b + 1][b + 1]
            det = head * tail - side * side
            inverse.append(pl.reciprocal(head, approx=True))
            inverse.append(head * pl.reciprocal(det, approx=True))
            link = side * inverse[b]
            below[b + 1][b] = link
            rows[b + 1] = rows[b + 1] - link * rows[b]
            pivot[b + 1][b + 1] = det * inverse[b]
            for i in range(b + 2, SUB):
                pivot[b + 1][i] = pivot[b + 1][i] - link * pivot[b][i]
                below[i][b] = pivot[b][i] * inverse[b]
                below[i][b + 1] = pivot[b + 1][i] * inverse[b + 1]
            for i in range(b + 2, SUB):
                for c in range(i, SUB):
                    pivot[i][c] = (pivot[i][c] - below[i][b] * pivot[b][c]) - (
                        below[i][b + 1] * pivot[b + 1][c]
                    )
                rows[i] = (rows[i] - below[i][b] * rows[b]) - below[i][b + 1] * rows[b + 1]
        result = jnp.zeros(shape, jnp.float32)
        for b in range(SUB):
            result = jnp.where(sub == b, rows[b] * lax.rsqrt(pivot[b][b]), result)
        inv_ref[start : start + SUB, :] = jnp.where(lane < start + SUB, result, 0.0)
        solved = [None] * SUB
        for b in reversed(range(SUB)):
            value = rows[b] * inverse[b]
            for i in reversed(range(b + 1, SUB)):
                value = value - below[i][b] * solved[i]
            solved[b] = value
        for q in range(s + 1, PANEL // SUB):
            parts = [
                spread(tiles[q][:, start + b : start + b + 1]) * solved[b] for b in range(SUB)
            ]
            while len(parts) > 1:
                parts = [x + y for x, y in zip(parts[::2], parts[1::2])]
            tiles[q] = jnp.where(inside, 0.0, tiles[q]) - parts[0]


def factor_kernel(scale, exact, pos_ref, *refs):
    *piece_refs, out_ref, work_ref, inv_ref = refs
    rank = work_ref.shape[0]
    panels = rank // PANEL
    count = len(piece_refs)
    if count == 1:
        work_ref[...] = piece_refs[0][...] * scale
    else:
        work_ref[...] = jnp.zeros((rank, rank), jnp.float32)
    own_cols = rank // count
    for k in range(count if count > 1 else 0):
        for s in range(count):

            @pl.when(pos_ref[0] ^ k == s)
            def _():
                for d in range(piece_refs[k].shape[1] // own_cols):
                    other = (s + d) % count
                    block = piece_refs[k][:, d * own_cols : (d + 1) * own_cols] * scale
                    low, high = min(s, other), max(s, other)
                    if s > other and 2 * d == count:
                        continue
                    work_ref[
                        low * own_cols : (low + 1) * own_cols,
                        high * own_cols : (high + 1) * own_cols,
                    ] = block.T if s > other else block

    on_diag = lax.broadcasted_iota(jnp.int32, (PANEL, PANEL), 0) == lax.broadcasted_iota(
        jnp.int32, (PANEL, PANEL), 1
    )
    by_column = []
    for k in range(panels):
        panel = slice(k * PANEL, (k + 1) * PANEL)
        diag = jnp.where(on_diag, work_ref[panel, panel], 0.0)
        by_column.append(lax.rsqrt(jnp.sum(diag, axis=0, keepdims=True)))
        work_ref[panel, :] *= lax.rsqrt(jnp.sum(diag, axis=1, keepdims=True))
    for k in range(panels):
        work_ref[:, k * PANEL : (k + 1) * PANEL] *= by_column[k]

    def panel_step(k, carry):
        here = pl.ds(pl.multiple_of(k * PANEL, PANEL), PANEL)
        diag = work_ref[here, here]

        eliminate([diag[SUB * q : SUB * (q + 1), :] for q in range(PANEL // SUB)], inv_ref)
        for here_k in range(panels):

            @pl.when(k == here_k)
            def _():
                panel = slice(here_k * PANEL, (here_k + 1) * PANEL)
                rest = slice((here_k + 1) * PANEL, rank)
                inv = inv_ref[...]
                work_ref[panel, :] = kernel_dot(inv, work_ref[panel, :], exact)
                work_ref[panel, panel] = inv
                if here_k < panels - 1:
                    lower = work_ref[panel, rest].T
                    work_ref[rest, panel] = jnp.zeros((rank - rest.start, PANEL), jnp.float32)
                    work_ref[rest, :] -= kernel_dot(lower, work_ref[panel, :], exact)

        return carry

    lax.fori_loop(0, panels, panel_step, 0)
    for i in range(panels - 1):
        work_ref[i * PANEL : (i + 1) * PANEL, (i + 1) * PANEL :] = jnp.zeros(
            (PANEL, rank - (i + 1) * PANEL), jnp.float32
        )
    for k in range(panels):
        panel = slice(k * PANEL, (k + 1) * PANEL)
        out_ref[:, panel] = work_ref[:, panel] * by_column[k]


def inverse_factor(pieces, exact, scale):
    rank = pieces[0].shape[0] * len(pieces)
    pos = lax.axis_index("tok").astype(jnp.int32).reshape(1)
    return pl.pallas_call(
        functools.partial(factor_kernel, scale, exact),
        out_shape=jax.ShapeDtypeStruct((rank, rank), jnp.float32),
        in_specs=[
            pl.BlockSpec(memory_space=pltpu.SMEM),
            *[pl.BlockSpec(memory_space=pltpu.VMEM) for _ in pieces],
        ],
        out_specs=pl.BlockSpec(memory_space=pltpu.VMEM),
        scratch_shapes=[
            pltpu.VMEM((rank, rank), jnp.float32),
            pltpu.VMEM((PANEL, PANEL), jnp.float32),
        ],
        compiler_params=pltpu.CompilerParams(vmem_limit_bytes=32 * 1024 * 1024),
        cost_estimate=pl.CostEstimate(
            flops=96 * rank**3, bytes_accessed=8 * rank**2, transcendentals=0
        ),
        name="inverse_factor",
    )(pos, *pieces)


def swap(value, axis, k):
    if k == 0:
        return value
    return lax.ppermute(value, axis, [(i, i ^ k) for i in range(lax.axis_size(axis))])


def collect(value, axis):
    return [swap(value, axis, k) for k in range(lax.axis_size(axis))]


def per_device(acts, init_basis, kept, member):
    owned = init_basis.shape[0]
    slice_rows = init_basis.shape[1]
    rank = init_basis.shape[2]
    tok_count = lax.axis_size("tok")
    gr_count = lax.axis_size("gr")
    gc_count = lax.axis_size("gc")
    block_cols = slice_rows * tok_count
    tok_rows = acts.shape[0]
    total_tokens = tok_rows * tok_count
    groups = kept.shape[0] // GBLK
    assert groups == gr_count == 2
    group_cols = GBLK * block_cols
    own_cols = rank // tok_count
    tok_pos = lax.axis_index("tok")
    gr_pos = lax.axis_index("gr")
    gc_pos = lax.axis_index("gc")
    first = (gr_pos * gc_count + gc_pos) * owned
    links = ((member[:, None] == member[None, :]).astype(jnp.int32) * kept).astype(jnp.float32)
    own_links = lax.dynamic_slice_in_dim(links, first, owned, 0)
    partner = ((gr_pos ^ 1) * gc_count + gc_pos) * owned
    partner_links = lax.dynamic_slice_in_dim(links, partner, owned, 0)
    own_groups = lax.dynamic_slice_in_dim(member, first, owned, 0)

    own_x = acts.reshape(tok_rows, owned, block_cols)
    turned_x = jnp.concatenate(
        [
            lax.dynamic_slice_in_dim(own_x, (tok_pos ^ k) * slice_rows, slice_rows, 2)
            for k in range(tok_count)
        ],
        axis=2,
    )
    init_bf = init_basis.astype(jnp.bfloat16)
    width = rank // CHUNKS
    init_pieces = [
        collect(init_bf[:, :, c * width : (c + 1) * width], "tok") for c in range(CHUNKS)
    ]
    gathered_x = lax.all_gather(acts, "tok", axis=0, tiled=True)
    full_x = jnp.concatenate(
        [
            lax.dynamic_slice_in_dim(gathered_x, (tok_pos ^ k) * tok_rows, tok_rows, 0)
            for k in range(tok_count)
        ],
        axis=0,
    ).reshape(total_tokens, owned, block_cols)

    def combine(rows_of_links, pieces, sources):
        total = 0.0
        for piece, source in zip(pieces, sources):
            weights = lax.dynamic_slice_in_dim(rows_of_links, source, owned, 1)
            for j in range(owned):
                total += weights[:, j][:, None, None] * piece[j][None].astype(jnp.float32)
        return total

    near = []
    for part in init_pieces:
        proj = jnp.einsum(
            "tob,obr->otr",
            turned_x,
            jnp.concatenate(part, axis=1),
            preferred_element_type=jnp.float32,
        ).astype(jnp.bfloat16)
        near.append(collect(proj, "gc"))
    sources = [(gr_pos * gc_count + (gc_pos ^ b)) * owned for b in range(gc_count)]

    def mix(pieces):
        own = combine(own_links, pieces, sources)
        other = combine(partner_links, pieces, sources)
        return (own + swap(other, "gr", 1)).astype(jnp.bfloat16)

    mixed = jnp.concatenate([mix(pieces) for pieces in near], axis=2)
    basis_bf = jnp.concatenate(
        [
            jnp.concatenate(
                [lax.select_n(tok_pos ^ a, *part) for a in range(tok_count)], axis=1
            )
            for part in init_pieces
        ],
        axis=2,
    )

    def image_of(mixed, basis_bf):
        full = jnp.concatenate(collect(mixed, "tok"), axis=1)
        cover = jnp.einsum("tob,otr->obr", full_x, full, preferred_element_type=jnp.float32)
        return cover / total_tokens + ridge * basis_bf.astype(jnp.float32)

    def seen_by(image):
        return sum(
            jnp.einsum("tob,obr->otr", own_x, part, preferred_element_type=jnp.float32)
            for part in split(image)
        )

    def factor(image, last, beside):
        precision = HIGHEST if last else HIGH
        own = lax.dynamic_slice_in_dim(image, tok_pos * own_cols, own_cols, 2)
        grams = jnp.einsum("obr,obs->ors", own, image, precision=precision)

        def group_sum(g):
            mask = (own_groups == g).astype(jnp.float32)
            return jnp.sum(mask[:, None, None] * grams, axis=0)

        total = group_sum(gr_pos) + swap(group_sum(gr_pos ^ 1), "gr", 1)
        packed = tok_count == 4 and own_cols % PANEL == 0
        if packed:
            total = jnp.concatenate(
                [
                    lax.dynamic_slice_in_dim(
                        total, (tok_pos + d) % tok_count * own_cols, own_cols, 1
                    )
                    for d in range(tok_count // 2 + 1)
                ],
                axis=1,
            )
        step = 1
        while step < gc_count:
            if 2 * step == gc_count:
                total, beside = lax.optimization_barrier((total, beside))
                if not last:
                    beside = mix_seen(beside)
            total += swap(total, "gc", step)
            step *= 2
        if packed:
            pieces = collect(total, "tok")
        else:
            pieces = [lax.all_gather(total, "tok", axis=0, tiled=True)]
        own = inverse_factor(pieces, last, 1.0 / group_cols)
        other = swap(own, "gr", 1)
        if not last:
            other, beside = lax.optimization_barrier((other, beside))
        of_block = jnp.stack(
            [jnp.where(own_groups[o] == gr_pos, own, other) for o in range(owned)]
        )
        of_group = [jnp.where(gr_pos == g, own, other) for g in range(groups)]
        return of_block, of_group, beside

    image = image_of(mixed, basis_bf)
    def mix_seen(seen):
        seen = lax.all_gather(seen, ("gr", "gc"), axis=0, tiled=True)
        total = 0.0
        for j in range(seen.shape[0]):
            total += own_links[:, j][:, None, None] * seen[j][None]
        return total

    of_block, _, second = factor(image, False, seen_by(image))
    mixed = jnp.einsum("otr,osr->ots", second, of_block, precision=HIGH).astype(jnp.bfloat16)
    basis_bf = jnp.einsum("obr,osr->obs", image, of_block, precision=HIGH).astype(jnp.bfloat16)
    image = image_of(mixed, basis_bf)
    codes = seen_by(image)
    placed = jnp.concatenate(
        [
            jnp.sum((own_groups == g).astype(jnp.float32)[:, None, None] * codes, axis=0)
            for g in range(groups)
        ],
        axis=1,
    )
    of_block, of_group, placed = factor(image, True, placed)
    rows = lax.dynamic_slice_in_dim(image, tok_pos * slice_rows, slice_rows, 1)
    basis = jnp.einsum("obr,osr->obs", rows, of_block, precision=HIGH)
    placed = lax.psum_scatter(placed, ("gr", "gc"), scatter_dimension=0, tiled=True)
    latent = jnp.concatenate(
        [
            jnp.einsum(
                "tr,sr->ts",
                placed[:, g * rank : (g + 1) * rank],
                of_group[g],
                precision=HIGH,
            )
            for g in range(groups)
        ],
        axis=1,
    )
    latent = latent * (1.0 / math.sqrt(group_cols))
    return (basis, latent.astype(jnp.bfloat16))


def solution(mesh):
    placed = (P("tok", ("gr", "gc")), P(("gr", "gc"), "tok", None), P(), P())
    return jax.shard_map(
        per_device,
        mesh=mesh,
        in_specs=placed,
        out_specs=(P(("gr", "gc"), "tok", None), P(("tok", "gr", "gc"), None)),
        check_vma=False,
    )
```

```python
import functools
import math

import jax
import jax.numpy as jnp
from jax import lax
from jax.experimental import pallas as pl
from jax.experimental.pallas import tpu as pltpu
from jax.sharding import PartitionSpec as P

GBLK = 8
PANEL = 128
SUB = 8
CHUNKS = 2

ridge = 2.0
HIGHEST = lax.Precision.HIGHEST
HIGH = lax.Precision.HIGH


def split(value):
    high = lax.reduce_precision(value, 8, 7)
    return high.astype(jnp.bfloat16), (value - high).astype(jnp.bfloat16)


def kernel_dot(left, right, exact):
    if exact:
        return jnp.dot(left, right, preferred_element_type=jnp.float32, precision=HIGHEST)
    parts = []
    for value in (left, right):
        high = value.astype(jnp.bfloat16)
        parts.append((high, (value - high.astype(jnp.float32)).astype(jnp.bfloat16)))
    (a, b), (c, d) = parts
    return sum(
        jnp.dot(x, y, preferred_element_type=jnp.float32) for x, y in ((b, c), (a, d), (a, c))
    )


def eliminate(tiles, inv_ref):
    shape = (SUB, PANEL)
    lane = lax.broadcasted_iota(jnp.int32, shape, 1)
    sub = lax.broadcasted_iota(jnp.int32, shape, 0)

    def spread(column):
        return jnp.broadcast_to(column, shape)

    tiles = list(tiles)
    for s in range(PANEL // SUB):
        start = s * SUB
        tile = tiles[s]
        inside = (lane >= start) & (lane < start + SUB)
        columns = [spread(tile[:, start + c : start + c + 1]) for c in range(SUB)]
        pivot = [
            [spread(columns[c][i : i + 1, :]) if c >= i else None for c in range(SUB)]
            for i in range(SUB)
        ]
        base = jnp.where(inside, jnp.where(lane == start + sub, 1.0, 0.0), tile)
        rows = [spread(base[i : i + 1, :]) for i in range(SUB)]
        below = [[None] * SUB for _ in range(SUB)]
        inverse = []
        for b in range(0, SUB, 2):
            head, side, tail = pivot[b][b], pivot[b][b + 1], pivot[b + 1][b + 1]
            det = head * tail - side * side
            inverse.append(pl.reciprocal(head, approx=True))
            inverse.append(head * pl.reciprocal(det, approx=True))
            link = side * inverse[b]
            below[b + 1][b] = link
            rows[b + 1] = rows[b + 1] - link * rows[b]
            pivot[b + 1][b + 1] = det * inverse[b]
            for i in range(b + 2, SUB):
                pivot[b + 1][i] = pivot[b + 1][i] - link * pivot[b][i]
                below[i][b] = pivot[b][i] * inverse[b]
                below[i][b + 1] = pivot[b + 1][i] * inverse[b + 1]
            for i in range(b + 2, SUB):
                for c in range(i, SUB):
                    pivot[i][c] = (pivot[i][c] - below[i][b] * pivot[b][c]) - (
                        below[i][b + 1] * pivot[b + 1][c]
                    )
                rows[i] = (rows[i] - below[i][b] * rows[b]) - below[i][b + 1] * rows[b + 1]
        result = jnp.zeros(shape, jnp.float32)
        for b in range(SUB):
            result = jnp.where(sub == b, rows[b] * lax.rsqrt(pivot[b][b]), result)
        inv_ref[start : start + SUB, :] = jnp.where(lane < start + SUB, result, 0.0)
        solved = [None] * SUB
        for b in reversed(range(SUB)):
            value = rows[b] * inverse[b]
            for i in reversed(range(b + 1, SUB)):
                value = value - below[i][b] * solved[i]
            solved[b] = value
        for q in range(s + 1, PANEL // SUB):
            parts = [
                spread(tiles[q][:, start + b : start + b + 1]) * solved[b] for b in range(SUB)
            ]
            while len(parts) > 1:
                parts = [x + y for x, y in zip(parts[::2], parts[1::2])]
            tiles[q] = jnp.where(inside, 0.0, tiles[q]) - parts[0]


def factor_kernel(scale, exact, pos_ref, *refs):
    *piece_refs, out_ref, work_ref, inv_ref = refs
    rank = work_ref.shape[0]
    panels = rank // PANEL
    count = len(piece_refs)
    if count == 1:
        work_ref[...] = piece_refs[0][...] * scale
    else:
        work_ref[...] = jnp.zeros((rank, rank), jnp.float32)
    own_cols = rank // count
    for k in range(count if count > 1 else 0):
        for s in range(count):

            @pl.when(pos_ref[0] ^ k == s)
            def _():
                for d in range(piece_refs[k].shape[1] // own_cols):
                    other = (s + d) % count
                    block = piece_refs[k][:, d * own_cols : (d + 1) * own_cols] * scale
                    low, high = min(s, other), max(s, other)
                    if s > other and 2 * d == count:
                        continue
                    work_ref[
                        low * own_cols : (low + 1) * own_cols,
                        high * own_cols : (high + 1) * own_cols,
                    ] = block.T if s > other else block

    on_diag = lax.broadcasted_iota(jnp.int32, (PANEL, PANEL), 0) == lax.broadcasted_iota(
        jnp.int32, (PANEL, PANEL), 1
    )
    by_column = []
    for k in range(panels):
        panel = slice(k * PANEL, (k + 1) * PANEL)
        diag = jnp.where(on_diag, work_ref[panel, panel], 0.0)
        by_column.append(lax.rsqrt(jnp.sum(diag, axis=0, keepdims=True)))
        work_ref[panel, :] *= lax.rsqrt(jnp.sum(diag, axis=1, keepdims=True))
    for k in range(panels):
        work_ref[:, k * PANEL : (k + 1) * PANEL] *= by_column[k]

    def panel_step(k, carry):
        here = pl.ds(pl.multiple_of(k * PANEL, PANEL), PANEL)
        diag = work_ref[here, here]

        eliminate([diag[SUB * q : SUB * (q + 1), :] for q in range(PANEL // SUB)], inv_ref)
        for here_k in range(panels):

            @pl.when(k == here_k)
            def _():
                panel = slice(here_k * PANEL, (here_k + 1) * PANEL)
                rest = slice((here_k + 1) * PANEL, rank)
                inv = inv_ref[...]
                work_ref[panel, :] = kernel_dot(inv, work_ref[panel, :], exact)
                work_ref[panel, panel] = inv
                if here_k < panels - 1:
                    lower = work_ref[panel, rest].T
                    work_ref[rest, panel] = jnp.zeros((rank - rest.start, PANEL), jnp.float32)
                    work_ref[rest, :] -= kernel_dot(lower, work_ref[panel, :], exact)

        return carry

    lax.fori_loop(0, panels, panel_step, 0)
    for i in range(panels - 1):
        work_ref[i * PANEL : (i + 1) * PANEL, (i + 1) * PANEL :] = jnp.zeros(
            (PANEL, rank - (i + 1) * PANEL), jnp.float32
        )
    for k in range(panels):
        panel = slice(k * PANEL, (k + 1) * PANEL)
        out_ref[:, panel] = work_ref[:, panel] * by_column[k]


def inverse_factor(pieces, exact, scale):
    rank = pieces[0].shape[0] * len(pieces)
    pos = lax.axis_index("tok").astype(jnp.int32).reshape(1)
    return pl.pallas_call(
        functools.partial(factor_kernel, scale, exact),
        out_shape=jax.ShapeDtypeStruct((rank, rank), jnp.float32),
        in_specs=[
            pl.BlockSpec(memory_space=pltpu.SMEM),
            *[pl.BlockSpec(memory_space=pltpu.VMEM) for _ in pieces],
        ],
        out_specs=pl.BlockSpec(memory_space=pltpu.VMEM),
        scratch_shapes=[
            pltpu.VMEM((rank, rank), jnp.float32),
            pltpu.VMEM((PANEL, PANEL), jnp.float32),
        ],
        compiler_params=pltpu.CompilerParams(vmem_limit_bytes=32 * 1024 * 1024),
        cost_estimate=pl.CostEstimate(
            flops=96 * rank**3, bytes_accessed=8 * rank**2, transcendentals=0
        ),
        name="inverse_factor",
    )(pos, *pieces)


def swap(value, axis, k):
    if k == 0:
        return value
    return lax.ppermute(value, axis, [(i, i ^ k) for i in range(lax.axis_size(axis))])


def collect(value, axis):
    return [swap(value, axis, k) for k in range(lax.axis_size(axis))]


def per_device(acts, init_basis, kept, member):
    owned = init_basis.shape[0]
    slice_rows = init_basis.shape[1]
    rank = init_basis.shape[2]
    tok_count = lax.axis_size("tok")
    gr_count = lax.axis_size("gr")
    gc_count = lax.axis_size("gc")
    block_cols = slice_rows * tok_count
    tok_rows = acts.shape[0]
    total_tokens = tok_rows * tok_count
    groups = kept.shape[0] // GBLK
    assert groups == gr_count == 2
    group_cols = GBLK * block_cols
    own_cols = rank // tok_count
    tok_pos = lax.axis_index("tok")
    gr_pos = lax.axis_index("gr")
    gc_pos = lax.axis_index("gc")
    first = (gr_pos * gc_count + gc_pos) * owned
    links = ((member[:, None] == member[None, :]).astype(jnp.int32) * kept).astype(jnp.float32)
    own_links = lax.dynamic_slice_in_dim(links, first, owned, 0)
    partner = ((gr_pos ^ 1) * gc_count + gc_pos) * owned
    partner_links = lax.dynamic_slice_in_dim(links, partner, owned, 0)
    own_groups = lax.dynamic_slice_in_dim(member, first, owned, 0)

    own_x = acts.reshape(tok_rows, owned, block_cols)
    turned_x = jnp.concatenate(
        [
            lax.dynamic_slice_in_dim(own_x, (tok_pos ^ k) * slice_rows, slice_rows, 2)
            for k in range(tok_count)
        ],
        axis=2,
    )
    init_bf = init_basis.astype(jnp.bfloat16)
    width = rank // CHUNKS
    init_pieces = [
        collect(init_bf[:, :, c * width : (c + 1) * width], "tok") for c in range(CHUNKS)
    ]
    gathered_x = lax.all_gather(acts, "tok", axis=0, tiled=True)
    full_x = jnp.concatenate(
        [
            lax.dynamic_slice_in_dim(gathered_x, (tok_pos ^ k) * tok_rows, tok_rows, 0)
            for k in range(tok_count)
        ],
        axis=0,
    ).reshape(total_tokens, owned, block_cols)

    def combine(rows_of_links, pieces, sources):
        total = 0.0
        for piece, source in zip(pieces, sources):
            weights = lax.dynamic_slice_in_dim(rows_of_links, source, owned, 1)
            for j in range(owned):
                total += weights[:, j][:, None, None] * piece[j][None].astype(jnp.float32)
        return total

    near = []
    for part in init_pieces:
        proj = jnp.einsum(
            "tob,obr->otr",
            turned_x,
            jnp.concatenate(part, axis=1),
            preferred_element_type=jnp.float32,
        ).astype(jnp.bfloat16)
        near.append(collect(proj, "gc"))
    sources = [(gr_pos * gc_count + (gc_pos ^ b)) * owned for b in range(gc_count)]

    def mix(pieces):
        own = combine(own_links, pieces, sources)
        other = combine(partner_links, pieces, sources)
        return (own + swap(other, "gr", 1)).astype(jnp.bfloat16)

    mixed = jnp.concatenate([mix(pieces) for pieces in near], axis=2)
    basis_bf = jnp.concatenate(
        [
            jnp.concatenate(
                [lax.select_n(tok_pos ^ a, *part) for a in range(tok_count)], axis=1
            )
            for part in init_pieces
        ],
        axis=2,
    )

    def image_of(mixed, basis_bf):
        full = jnp.concatenate(collect(mixed, "tok"), axis=1)
        cover = jnp.einsum("tob,otr->obr", full_x, full, preferred_element_type=jnp.float32)
        return cover / total_tokens + ridge * basis_bf.astype(jnp.float32)

    def seen_by(image):
        return sum(
            jnp.einsum("tob,obr->otr", own_x, part, preferred_element_type=jnp.float32)
            for part in split(image)
        )

    def halve(value, axis, bit):
        half = value.shape[0] // 2
        mine = lax.axis_index(axis) // bit % 2
        own = lax.dynamic_slice_in_dim(value, mine * half, half, 0)
        other = lax.dynamic_slice_in_dim(value, (1 - mine) * half, half, 0)
        return own + swap(other, axis, bit)

    def factor(image, last, beside):
        precision = HIGHEST if last else HIGH
        own = lax.dynamic_slice_in_dim(image, tok_pos * own_cols, own_cols, 2)
        grams = jnp.einsum("obr,obs->ors", own, image, precision=precision)

        def group_sum(g):
            mask = (own_groups == g).astype(jnp.float32)
            return jnp.sum(mask[:, None, None] * grams, axis=0)

        total = group_sum(gr_pos) + swap(group_sum(gr_pos ^ 1), "gr", 1)
        packed = tok_count == 4 and own_cols % PANEL == 0
        if packed:
            total = jnp.concatenate(
                [
                    lax.dynamic_slice_in_dim(
                        total, (tok_pos + d) % tok_count * own_cols, own_cols, 1
                    )
                    for d in range(tok_count // 2 + 1)
                ],
                axis=1,
            )
        step = 1
        while step < gc_count:
            if 2 * step == gc_count:
                total, beside = lax.optimization_barrier((total, beside))
                beside = halve(beside, "gr", 1) if last else mix_seen(beside)
                if last and gc_count > 1:
                    beside = halve(beside, "gc", gc_count // 2)
            total += swap(total, "gc", step)
            step *= 2
        if last:
            total, beside = lax.optimization_barrier((total, beside))
            step = gc_count // 4
            while step:
                beside = halve(beside, "gc", step)
                step //= 2
        if packed:
            pieces = collect(total, "tok")
        else:
            pieces = [lax.all_gather(total, "tok", axis=0, tiled=True)]
        own = inverse_factor(pieces, last, 1.0 / group_cols)
        other = swap(own, "gr", 1)
        if not last:
            other, beside = lax.optimization_barrier((other, beside))
        of_block = jnp.stack(
            [jnp.where(own_groups[o] == gr_pos, own, other) for o in range(owned)]
        )
        of_group = [jnp.where(gr_pos == g, own, other) for g in range(groups)]
        return of_block, of_group, beside

    image = image_of(mixed, basis_bf)
    def mix_seen(seen):
        seen = lax.all_gather(seen, ("gr", "gc"), axis=0, tiled=True)
        total = 0.0
        for j in range(seen.shape[0]):
            total += own_links[:, j][:, None, None] * seen[j][None]
        return total

    of_block, _, second = factor(image, False, seen_by(image))
    mixed = jnp.einsum("otr,osr->ots", second, of_block, precision=HIGH).astype(jnp.bfloat16)
    basis_bf = jnp.einsum("obr,osr->obs", image, of_block, precision=HIGH).astype(jnp.bfloat16)
    image = image_of(mixed, basis_bf)
    codes = seen_by(image)
    placed = jnp.concatenate(
        [
            jnp.sum((own_groups == g).astype(jnp.float32)[:, None, None] * codes, axis=0)
            for g in range(groups)
        ],
        axis=1,
    )
    of_block, of_group, placed = factor(image, True, placed)
    rows = lax.dynamic_slice_in_dim(image, tok_pos * slice_rows, slice_rows, 1)
    basis = jnp.einsum("obr,osr->obs", rows, of_block, precision=HIGH)
    placed, basis = lax.optimization_barrier((placed, basis))
    latent = jnp.concatenate(
        [
            jnp.einsum(
                "tr,sr->ts",
                placed[:, g * rank : (g + 1) * rank],
                of_group[g],
                precision=HIGH,
            )
            for g in range(groups)
        ],
        axis=1,
    )
    latent = latent * (1.0 / math.sqrt(group_cols))
    return (basis, latent.astype(jnp.bfloat16))


def solution(mesh):
    placed = (P("tok", ("gr", "gc")), P(("gr", "gc"), "tok", None), P(), P())
    return jax.shard_map(
        per_device,
        mesh=mesh,
        in_specs=placed,
        out_specs=(P(("gr", "gc"), "tok", None), P(("tok", "gr", "gc"), None)),
        check_vma=False,
    )
```

```python
import functools
import math

import jax
import jax.numpy as jnp
from jax import lax
from jax.experimental import pallas as pl
from jax.experimental.pallas import tpu as pltpu
from jax.sharding import PartitionSpec as P

GBLK = 8
PANEL = 128
SUB = 8
CHUNKS = 2

ridge = 2.0
HIGHEST = lax.Precision.HIGHEST
HIGH = lax.Precision.HIGH


def split(value):
    high = lax.reduce_precision(value, 8, 7)
    return high.astype(jnp.bfloat16), (value - high).astype(jnp.bfloat16)


def kernel_dot(left, right, exact):
    if exact:
        return jnp.dot(left, right, preferred_element_type=jnp.float32, precision=HIGHEST)
    parts = []
    for value in (left, right):
        high = value.astype(jnp.bfloat16)
        parts.append((high, (value - high.astype(jnp.float32)).astype(jnp.bfloat16)))
    (a, b), (c, d) = parts
    return sum(
        jnp.dot(x, y, preferred_element_type=jnp.float32) for x, y in ((b, c), (a, d), (a, c))
    )


def eliminate(tiles, inv_ref):
    shape = (SUB, PANEL)
    lane = lax.broadcasted_iota(jnp.int32, shape, 1)
    sub = lax.broadcasted_iota(jnp.int32, shape, 0)

    def spread(column):
        return jnp.broadcast_to(column, shape)

    tiles = list(tiles)
    for s in range(PANEL // SUB):
        start = s * SUB
        tile = tiles[s]
        inside = (lane >= start) & (lane < start + SUB)
        columns = [spread(tile[:, start + c : start + c + 1]) for c in range(SUB)]
        pivot = [
            [spread(columns[c][i : i + 1, :]) if c >= i else None for c in range(SUB)]
            for i in range(SUB)
        ]
        base = jnp.where(inside, jnp.where(lane == start + sub, 1.0, 0.0), tile)
        rows = [spread(base[i : i + 1, :]) for i in range(SUB)]
        below = [[None] * SUB for _ in range(SUB)]
        inverse = []
        for b in range(0, SUB, 2):
            head, side, tail = pivot[b][b], pivot[b][b + 1], pivot[b + 1][b + 1]
            det = head * tail - side * side
            inverse.append(pl.reciprocal(head, approx=True))
            inverse.append(head * pl.reciprocal(det, approx=True))
            link = side * inverse[b]
            below[b + 1][b] = link
            rows[b + 1] = rows[b + 1] - link * rows[b]
            pivot[b + 1][b + 1] = det * inverse[b]
            for i in range(b + 2, SUB):
                pivot[b + 1][i] = pivot[b + 1][i] - link * pivot[b][i]
                below[i][b] = pivot[b][i] * inverse[b]
                below[i][b + 1] = pivot[b + 1][i] * inverse[b + 1]
            for i in range(b + 2, SUB):
                for c in range(i, SUB):
                    pivot[i][c] = (pivot[i][c] - below[i][b] * pivot[b][c]) - (
                        below[i][b + 1] * pivot[b + 1][c]
                    )
                rows[i] = (rows[i] - below[i][b] * rows[b]) - below[i][b + 1] * rows[b + 1]
        result = jnp.zeros(shape, jnp.float32)
        for b in range(SUB):
            result = jnp.where(sub == b, rows[b] * lax.rsqrt(pivot[b][b]), result)
        inv_ref[start : start + SUB, :] = jnp.where(lane < start + SUB, result, 0.0)
        solved = [None] * SUB
        for b in reversed(range(SUB)):
            value = rows[b] * inverse[b]
            for i in reversed(range(b + 1, SUB)):
                value = value - below[i][b] * solved[i]
            solved[b] = value
        for q in range(s + 1, PANEL // SUB):
            parts = [
                spread(tiles[q][:, start + b : start + b + 1]) * solved[b] for b in range(SUB)
            ]
            while len(parts) > 1:
                parts = [x + y for x, y in zip(parts[::2], parts[1::2])]
            tiles[q] = jnp.where(inside, 0.0, tiles[q]) - parts[0]


def factor_kernel(scale, exact, pos_ref, *refs):
    *piece_refs, out_ref, work_ref, inv_ref = refs
    rank = work_ref.shape[0]
    panels = rank // PANEL
    count = len(piece_refs)
    if count == 1:
        work_ref[...] = piece_refs[0][...] * scale
    else:
        work_ref[...] = jnp.zeros((rank, rank), jnp.float32)
    own_cols = rank // count
    for k in range(count if count > 1 else 0):
        for s in range(count):

            @pl.when(pos_ref[0] ^ k == s)
            def _():
                for d in range(piece_refs[k].shape[1] // own_cols):
                    other = (s + d) % count
                    block = piece_refs[k][:, d * own_cols : (d + 1) * own_cols] * scale
                    low, high = min(s, other), max(s, other)
                    if s > other and 2 * d == count:
                        continue
                    work_ref[
                        low * own_cols : (low + 1) * own_cols,
                        high * own_cols : (high + 1) * own_cols,
                    ] = block.T if s > other else block

    on_diag = lax.broadcasted_iota(jnp.int32, (PANEL, PANEL), 0) == lax.broadcasted_iota(
        jnp.int32, (PANEL, PANEL), 1
    )
    by_column = []
    for k in range(panels):
        panel = slice(k * PANEL, (k + 1) * PANEL)
        diag = jnp.where(on_diag, work_ref[panel, panel], 0.0)
        by_column.append(lax.rsqrt(jnp.sum(diag, axis=0, keepdims=True)))
        work_ref[panel, :] *= lax.rsqrt(jnp.sum(diag, axis=1, keepdims=True))
    for k in range(panels):
        work_ref[:, k * PANEL : (k + 1) * PANEL] *= by_column[k]

    def panel_step(k, carry):
        here = pl.ds(pl.multiple_of(k * PANEL, PANEL), PANEL)
        diag = work_ref[here, here]

        eliminate([diag[SUB * q : SUB * (q + 1), :] for q in range(PANEL // SUB)], inv_ref)
        for here_k in range(panels):

            @pl.when(k == here_k)
            def _():
                panel = slice(here_k * PANEL, (here_k + 1) * PANEL)
                rest = slice((here_k + 1) * PANEL, rank)
                inv = inv_ref[...]
                work_ref[panel, :] = kernel_dot(inv, work_ref[panel, :], exact)
                work_ref[panel, panel] = inv
                if here_k < panels - 1:
                    lower = work_ref[panel, rest].T
                    work_ref[rest, panel] = jnp.zeros((rank - rest.start, PANEL), jnp.float32)
                    work_ref[rest, :] -= kernel_dot(lower, work_ref[panel, :], exact)

        return carry

    lax.fori_loop(0, panels, panel_step, 0)
    for i in range(panels - 1):
        work_ref[i * PANEL : (i + 1) * PANEL, (i + 1) * PANEL :] = jnp.zeros(
            (PANEL, rank - (i + 1) * PANEL), jnp.float32
        )
    for k in range(panels):
        panel = slice(k * PANEL, (k + 1) * PANEL)
        out_ref[:, panel] = work_ref[:, panel] * by_column[k]


def inverse_factor(pieces, exact, scale):
    rank = pieces[0].shape[0] * len(pieces)
    pos = lax.axis_index("tok").astype(jnp.int32).reshape(1)
    return pl.pallas_call(
        functools.partial(factor_kernel, scale, exact),
        out_shape=jax.ShapeDtypeStruct((rank, rank), jnp.float32),
        in_specs=[
            pl.BlockSpec(memory_space=pltpu.SMEM),
            *[pl.BlockSpec(memory_space=pltpu.VMEM) for _ in pieces],
        ],
        out_specs=pl.BlockSpec(memory_space=pltpu.VMEM),
        scratch_shapes=[
            pltpu.VMEM((rank, rank), jnp.float32),
            pltpu.VMEM((PANEL, PANEL), jnp.float32),
        ],
        compiler_params=pltpu.CompilerParams(vmem_limit_bytes=32 * 1024 * 1024),
        cost_estimate=pl.CostEstimate(
            flops=96 * rank**3, bytes_accessed=8 * rank**2, transcendentals=0
        ),
        name="inverse_factor",
    )(pos, *pieces)


def swap(value, axis, k):
    if k == 0:
        return value
    return lax.ppermute(value, axis, [(i, i ^ k) for i in range(lax.axis_size(axis))])


def collect(value, axis):
    return [swap(value, axis, k) for k in range(lax.axis_size(axis))]


def per_device(acts, init_basis, kept, member):
    owned = init_basis.shape[0]
    slice_rows = init_basis.shape[1]
    rank = init_basis.shape[2]
    tok_count = lax.axis_size("tok")
    gr_count = lax.axis_size("gr")
    gc_count = lax.axis_size("gc")
    block_cols = slice_rows * tok_count
    tok_rows = acts.shape[0]
    total_tokens = tok_rows * tok_count
    groups = kept.shape[0] // GBLK
    assert groups == gr_count == 2
    group_cols = GBLK * block_cols
    own_cols = rank // tok_count
    tok_pos = lax.axis_index("tok")
    gr_pos = lax.axis_index("gr")
    gc_pos = lax.axis_index("gc")
    first = (gr_pos * gc_count + gc_pos) * owned
    links = ((member[:, None] == member[None, :]).astype(jnp.int32) * kept).astype(jnp.float32)
    own_links = lax.dynamic_slice_in_dim(links, first, owned, 0)
    partner = ((gr_pos ^ 1) * gc_count + gc_pos) * owned
    partner_links = lax.dynamic_slice_in_dim(links, partner, owned, 0)
    own_groups = lax.dynamic_slice_in_dim(member, first, owned, 0)

    own_x = acts.reshape(tok_rows, owned, block_cols)
    turned_x = jnp.concatenate(
        [
            lax.dynamic_slice_in_dim(own_x, (tok_pos ^ k) * slice_rows, slice_rows, 2)
            for k in range(tok_count)
        ],
        axis=2,
    )
    init_bf = init_basis.astype(jnp.bfloat16)
    width = rank // CHUNKS
    init_pieces = [
        collect(init_bf[:, :, c * width : (c + 1) * width], "tok") for c in range(CHUNKS)
    ]
    gathered_x = lax.all_gather(acts, "tok", axis=0, tiled=True)
    full_x = jnp.concatenate(
        [
            lax.dynamic_slice_in_dim(gathered_x, (tok_pos ^ k) * tok_rows, tok_rows, 0)
            for k in range(tok_count)
        ],
        axis=0,
    ).reshape(total_tokens, owned, block_cols)

    def combine(rows_of_links, pieces, sources):
        total = 0.0
        for piece, source in zip(pieces, sources):
            weights = lax.dynamic_slice_in_dim(rows_of_links, source, owned, 1)
            for j in range(owned):
                total += weights[:, j][:, None, None] * piece[j][None].astype(jnp.float32)
        return total

    near = []
    for part in init_pieces:
        proj = jnp.einsum(
            "tob,obr->otr",
            turned_x,
            jnp.concatenate(part, axis=1),
            preferred_element_type=jnp.float32,
        ).astype(jnp.bfloat16)
        near.append(collect(proj, "gc"))
    sources = [(gr_pos * gc_count + (gc_pos ^ b)) * owned for b in range(gc_count)]

    def mix(pieces):
        own = combine(own_links, pieces, sources)
        other = combine(partner_links, pieces, sources)
        return (own + swap(other, "gr", 1)).astype(jnp.bfloat16)

    mixed = jnp.concatenate([mix(pieces) for pieces in near], axis=2)
    basis_bf = jnp.concatenate(
        [
            jnp.concatenate(
                [lax.select_n(tok_pos ^ a, *part) for a in range(tok_count)], axis=1
            )
            for part in init_pieces
        ],
        axis=2,
    )
    full_x, basis_bf = lax.optimization_barrier((full_x, basis_bf))

    def image_of(mixed, basis_bf):
        full = jnp.concatenate(collect(mixed, "tok"), axis=1)
        cover = jnp.einsum("tob,otr->obr", full_x, full, preferred_element_type=jnp.float32)
        return cover / total_tokens + ridge * basis_bf.astype(jnp.float32)

    def seen_by(image):
        return sum(
            jnp.einsum("tob,obr->otr", own_x, part, preferred_element_type=jnp.float32)
            for part in split(image)
        )

    def half_over_gr(value):
        half = value.shape[0] // 2
        own = lax.dynamic_slice_in_dim(value, gr_pos * half, half, 0)
        other = lax.dynamic_slice_in_dim(value, (gr_pos ^ 1) * half, half, 0)
        return own + swap(other, "gr", 1)

    def factor(image, last, beside):
        precision = HIGHEST if last else HIGH
        own = lax.dynamic_slice_in_dim(image, tok_pos * own_cols, own_cols, 2)
        grams = jnp.einsum("obr,obs->ors", own, image, precision=precision)

        def group_sum(g):
            mask = (own_groups == g).astype(jnp.float32)
            return jnp.sum(mask[:, None, None] * grams, axis=0)

        total = group_sum(gr_pos) + swap(group_sum(gr_pos ^ 1), "gr", 1)
        packed = tok_count == 4 and own_cols % PANEL == 0
        if packed:
            total = jnp.concatenate(
                [
                    lax.dynamic_slice_in_dim(
                        total, (tok_pos + d) % tok_count * own_cols, own_cols, 1
                    )
                    for d in range(tok_count // 2 + 1)
                ],
                axis=1,
            )
        step = 1
        while step < gc_count:
            if 2 * step == gc_count:
                total, beside = lax.optimization_barrier((total, beside))
                beside = half_over_gr(beside) if last else mix_seen(beside)
            total += swap(total, "gc", step)
            step *= 2
        if last:
            total, beside = lax.optimization_barrier((total, beside))
            beside = lax.psum_scatter(beside, "gc", scatter_dimension=0, tiled=True)
        if packed:
            pieces = collect(total, "tok")
        else:
            pieces = [lax.all_gather(total, "tok", axis=0, tiled=True)]
        own = inverse_factor(pieces, last, 1.0 / group_cols)
        if last:
            own, beside = lax.optimization_barrier((own, beside))
        other = swap(own, "gr", 1)
        if not last:
            other, beside = lax.optimization_barrier((other, beside))
        of_block = jnp.stack(
            [jnp.where(own_groups[o] == gr_pos, own, other) for o in range(owned)]
        )
        of_group = [jnp.where(gr_pos == g, own, other) for g in range(groups)]
        return of_block, of_group, beside

    image = image_of(mixed, basis_bf)
    def mix_seen(seen):
        seen = lax.all_gather(seen, ("gr", "gc"), axis=0, tiled=True)
        total = 0.0
        for j in range(seen.shape[0]):
            total += own_links[:, j][:, None, None] * seen[j][None]
        return total

    of_block, _, second = factor(image, False, seen_by(image))
    mixed = jnp.einsum("otr,osr->ots", second, of_block, precision=HIGH).astype(jnp.bfloat16)
    basis_bf = jnp.einsum("obr,osr->obs", image, of_block, precision=HIGH).astype(jnp.bfloat16)
    image = image_of(mixed, basis_bf)
    codes = seen_by(image)
    placed = jnp.concatenate(
        [
            jnp.sum((own_groups == g).astype(jnp.float32)[:, None, None] * codes, axis=0)
            for g in range(groups)
        ],
        axis=1,
    )
    of_block, of_group, placed = factor(image, True, placed)
    rows = lax.dynamic_slice_in_dim(image, tok_pos * slice_rows, slice_rows, 1)
    basis = jnp.einsum("obr,osr->obs", rows, of_block, precision=HIGH)
    latent = jnp.concatenate(
        [
            jnp.einsum(
                "tr,sr->ts",
                placed[:, g * rank : (g + 1) * rank],
                of_group[g],
                precision=HIGH,
            )
            for g in range(groups)
        ],
        axis=1,
    )
    latent = latent * (1.0 / math.sqrt(group_cols))
    return (basis, latent.astype(jnp.bfloat16))


def solution(mesh):
    placed = (P("tok", ("gr", "gc")), P(("gr", "gc"), "tok", None), P(), P())
    return jax.shard_map(
        per_device,
        mesh=mesh,
        in_specs=placed,
        out_specs=(P(("gr", "gc"), "tok", None), P(("tok", "gr", "gc"), None)),
        check_vma=False,
    )
```

```python
import functools
import math

import jax
import jax.numpy as jnp
from jax import lax
from jax.experimental import pallas as pl
from jax.experimental.pallas import tpu as pltpu
from jax.sharding import PartitionSpec as P

GBLK = 8
PANEL = 128
SUB = 8
CHUNKS = 2

ridge = 2.0
HIGHEST = lax.Precision.HIGHEST
HIGH = lax.Precision.HIGH


def split(value):
    high = lax.reduce_precision(value, 8, 7)
    return high.astype(jnp.bfloat16), (value - high).astype(jnp.bfloat16)


def kernel_dot(left, right, exact):
    if exact:
        return jnp.dot(left, right, preferred_element_type=jnp.float32, precision=HIGHEST)
    parts = []
    for value in (left, right):
        high = value.astype(jnp.bfloat16)
        parts.append((high, (value - high.astype(jnp.float32)).astype(jnp.bfloat16)))
    (a, b), (c, d) = parts
    return sum(
        jnp.dot(x, y, preferred_element_type=jnp.float32) for x, y in ((b, c), (a, d), (a, c))
    )


def eliminate(tiles, inv_ref):
    shape = (SUB, PANEL)
    lane = lax.broadcasted_iota(jnp.int32, shape, 1)
    sub = lax.broadcasted_iota(jnp.int32, shape, 0)

    def spread(column):
        return jnp.broadcast_to(column, shape)

    tiles = list(tiles)
    for s in range(PANEL // SUB):
        start = s * SUB
        tile = tiles[s]
        inside = (lane >= start) & (lane < start + SUB)
        columns = [spread(tile[:, start + c : start + c + 1]) for c in range(SUB)]
        pivot = [
            [spread(columns[c][i : i + 1, :]) if c >= i else None for c in range(SUB)]
            for i in range(SUB)
        ]
        base = jnp.where(inside, jnp.where(lane == start + sub, 1.0, 0.0), tile)
        rows = [spread(base[i : i + 1, :]) for i in range(SUB)]
        below = [[None] * SUB for _ in range(SUB)]
        inverse = []
        for b in range(0, SUB, 2):
            head, side, tail = pivot[b][b], pivot[b][b + 1], pivot[b + 1][b + 1]
            det = head * tail - side * side
            inverse.append(pl.reciprocal(head, approx=True))
            inverse.append(head * pl.reciprocal(det, approx=True))
            link = side * inverse[b]
            below[b + 1][b] = link
            rows[b + 1] = rows[b + 1] - link * rows[b]
            pivot[b + 1][b + 1] = det * inverse[b]
            for i in range(b + 2, SUB):
                pivot[b + 1][i] = pivot[b + 1][i] - link * pivot[b][i]
                below[i][b] = pivot[b][i] * inverse[b]
                below[i][b + 1] = pivot[b + 1][i] * inverse[b + 1]
            for i in range(b + 2, SUB):
                for c in range(i, SUB):
                    pivot[i][c] = (pivot[i][c] - below[i][b] * pivot[b][c]) - (
                        below[i][b + 1] * pivot[b + 1][c]
                    )
                rows[i] = (rows[i] - below[i][b] * rows[b]) - below[i][b + 1] * rows[b + 1]
        result = jnp.zeros(shape, jnp.float32)
        for b in range(SUB):
            result = jnp.where(sub == b, rows[b] * lax.rsqrt(pivot[b][b]), result)
        inv_ref[start : start + SUB, :] = jnp.where(lane < start + SUB, result, 0.0)
        solved = [None] * SUB
        for b in reversed(range(SUB)):
            value = rows[b] * inverse[b]
            for i in reversed(range(b + 1, SUB)):
                value = value - below[i][b] * solved[i]
            solved[b] = value
        for q in range(s + 1, PANEL // SUB):
            parts = [
                spread(tiles[q][:, start + b : start + b + 1]) * solved[b] for b in range(SUB)
            ]
            while len(parts) > 1:
                parts = [x + y for x, y in zip(parts[::2], parts[1::2])]
            tiles[q] = jnp.where(inside, 0.0, tiles[q]) - parts[0]


def factor_kernel(scale, exact, pos_ref, *refs):
    *piece_refs, out_ref, work_ref, inv_ref = refs
    rank = work_ref.shape[0]
    panels = rank // PANEL
    count = len(piece_refs)
    if count == 1:
        work_ref[...] = piece_refs[0][...] * scale
    else:
        work_ref[...] = jnp.zeros((rank, rank), jnp.float32)
    own_cols = rank // count
    for k in range(count if count > 1 else 0):
        for s in range(count):

            @pl.when(pos_ref[0] ^ k == s)
            def _():
                for d in range(piece_refs[k].shape[1] // own_cols):
                    other = (s + d) % count
                    block = piece_refs[k][:, d * own_cols : (d + 1) * own_cols] * scale
                    low, high = min(s, other), max(s, other)
                    if s > other and 2 * d == count:
                        continue
                    work_ref[
                        low * own_cols : (low + 1) * own_cols,
                        high * own_cols : (high + 1) * own_cols,
                    ] = block.T if s > other else block

    on_diag = lax.broadcasted_iota(jnp.int32, (PANEL, PANEL), 0) == lax.broadcasted_iota(
        jnp.int32, (PANEL, PANEL), 1
    )
    by_column = []
    for k in range(panels):
        panel = slice(k * PANEL, (k + 1) * PANEL)
        diag = jnp.where(on_diag, work_ref[panel, panel], 0.0)
        by_column.append(lax.rsqrt(jnp.sum(diag, axis=0, keepdims=True)))
        work_ref[panel, :] *= lax.rsqrt(jnp.sum(diag, axis=1, keepdims=True))
    for k in range(panels):
        work_ref[:, k * PANEL : (k + 1) * PANEL] *= by_column[k]

    def panel_step(k, carry):
        here = pl.ds(pl.multiple_of(k * PANEL, PANEL), PANEL)
        diag = work_ref[here, here]

        eliminate([diag[SUB * q : SUB * (q + 1), :] for q in range(PANEL // SUB)], inv_ref)
        for here_k in range(panels):

            @pl.when(k == here_k)
            def _():
                panel = slice(here_k * PANEL, (here_k + 1) * PANEL)
                rest = slice((here_k + 1) * PANEL, rank)
                inv = inv_ref[...]
                work_ref[panel, :] = kernel_dot(inv, work_ref[panel, :], exact)
                work_ref[panel, panel] = inv
                if here_k < panels - 1:
                    lower = work_ref[panel, rest].T
                    work_ref[rest, panel] = jnp.zeros((rank - rest.start, PANEL), jnp.float32)
                    work_ref[rest, :] -= kernel_dot(lower, work_ref[panel, :], exact)

        return carry

    lax.fori_loop(0, panels, panel_step, 0)
    for i in range(panels - 1):
        work_ref[i * PANEL : (i + 1) * PANEL, (i + 1) * PANEL :] = jnp.zeros(
            (PANEL, rank - (i + 1) * PANEL), jnp.float32
        )
    for k in range(panels):
        panel = slice(k * PANEL, (k + 1) * PANEL)
        out_ref[:, panel] = work_ref[:, panel] * by_column[k]


def inverse_factor(pieces, exact, scale):
    rank = pieces[0].shape[0] * len(pieces)
    pos = lax.axis_index("tok").astype(jnp.int32).reshape(1)
    return pl.pallas_call(
        functools.partial(factor_kernel, scale, exact),
        out_shape=jax.ShapeDtypeStruct((rank, rank), jnp.float32),
        in_specs=[
            pl.BlockSpec(memory_space=pltpu.SMEM),
            *[pl.BlockSpec(memory_space=pltpu.VMEM) for _ in pieces],
        ],
        out_specs=pl.BlockSpec(memory_space=pltpu.VMEM),
        scratch_shapes=[
            pltpu.VMEM((rank, rank), jnp.float32),
            pltpu.VMEM((PANEL, PANEL), jnp.float32),
        ],
        compiler_params=pltpu.CompilerParams(vmem_limit_bytes=32 * 1024 * 1024),
        cost_estimate=pl.CostEstimate(
            flops=96 * rank**3, bytes_accessed=8 * rank**2, transcendentals=0
        ),
        name="inverse_factor",
    )(pos, *pieces)


def swap(value, axis, k):
    if k == 0:
        return value
    return lax.ppermute(value, axis, [(i, i ^ k) for i in range(lax.axis_size(axis))])


def collect(value, axis):
    return [swap(value, axis, k) for k in range(lax.axis_size(axis))]


def per_device(acts, init_basis, kept, member):
    owned = init_basis.shape[0]
    slice_rows = init_basis.shape[1]
    rank = init_basis.shape[2]
    tok_count = lax.axis_size("tok")
    gr_count = lax.axis_size("gr")
    gc_count = lax.axis_size("gc")
    block_cols = slice_rows * tok_count
    tok_rows = acts.shape[0]
    total_tokens = tok_rows * tok_count
    groups = kept.shape[0] // GBLK
    assert groups == gr_count == 2
    group_cols = GBLK * block_cols
    own_cols = rank // tok_count
    tok_pos = lax.axis_index("tok")
    gr_pos = lax.axis_index("gr")
    gc_pos = lax.axis_index("gc")
    first = (gr_pos * gc_count + gc_pos) * owned
    links = ((member[:, None] == member[None, :]).astype(jnp.int32) * kept).astype(jnp.float32)
    own_links = lax.dynamic_slice_in_dim(links, first, owned, 0)
    partner = ((gr_pos ^ 1) * gc_count + gc_pos) * owned
    partner_links = lax.dynamic_slice_in_dim(links, partner, owned, 0)
    own_groups = lax.dynamic_slice_in_dim(member, first, owned, 0)

    own_x = acts.reshape(tok_rows, owned, block_cols)
    turned_x = jnp.concatenate(
        [
            lax.dynamic_slice_in_dim(own_x, (tok_pos ^ k) * slice_rows, slice_rows, 2)
            for k in range(tok_count)
        ],
        axis=2,
    )
    init_bf = init_basis.astype(jnp.bfloat16)
    width = rank // CHUNKS
    init_pieces = [
        collect(init_bf[:, :, c * width : (c + 1) * width], "tok") for c in range(CHUNKS)
    ]
    gathered_x = lax.all_gather(acts, "tok", axis=0, tiled=True)
    def combine(rows_of_links, pieces, sources):
        total = 0.0
        for piece, source in zip(pieces, sources):
            weights = lax.dynamic_slice_in_dim(rows_of_links, source, owned, 1)
            for j in range(owned):
                total += weights[:, j][:, None, None] * piece[j][None].astype(jnp.float32)
        return total

    near = []
    for part in init_pieces:
        proj = jnp.einsum(
            "tob,obr->otr",
            turned_x,
            jnp.concatenate(part, axis=1),
            preferred_element_type=jnp.float32,
        ).astype(jnp.bfloat16)
        near.append(collect(proj, "gc"))
    sources = [(gr_pos * gc_count + (gc_pos ^ b)) * owned for b in range(gc_count)]

    def mix(pieces):
        own = combine(own_links, pieces, sources)
        other = combine(partner_links, pieces, sources)
        return (own + swap(other, "gr", 1)).astype(jnp.bfloat16)

    mixed = jnp.concatenate([mix(pieces) for pieces in near], axis=2)
    basis_bf = jnp.concatenate(
        [
            jnp.concatenate(
                [lax.select_n(tok_pos ^ a, *part) for a in range(tok_count)], axis=1
            )
            for part in init_pieces
        ],
        axis=2,
    )
    gathered_x, basis_bf = lax.optimization_barrier((gathered_x, basis_bf))
    full_x = jnp.concatenate(
        [
            lax.dynamic_slice_in_dim(gathered_x, (tok_pos ^ k) * tok_rows, tok_rows, 0)
            for k in range(tok_count)
        ],
        axis=0,
    ).reshape(total_tokens, owned, block_cols)

    def image_of(mixed, basis_bf):
        full = jnp.concatenate(collect(mixed, "tok"), axis=1)
        cover = jnp.einsum("tob,otr->obr", full_x, full, preferred_element_type=jnp.float32)
        return cover / total_tokens + ridge * basis_bf.astype(jnp.float32)

    def seen_by(image):
        return sum(
            jnp.einsum("tob,obr->otr", own_x, part, preferred_element_type=jnp.float32)
            for part in split(image)
        )

    def half_over_gr(value):
        half = value.shape[0] // 2
        own = lax.dynamic_slice_in_dim(value, gr_pos * half, half, 0)
        other = lax.dynamic_slice_in_dim(value, (gr_pos ^ 1) * half, half, 0)
        return own + swap(other, "gr", 1)

    def factor(image, last, beside):
        precision = HIGHEST if last else HIGH
        own = lax.dynamic_slice_in_dim(image, tok_pos * own_cols, own_cols, 2)
        grams = jnp.einsum("obr,obs->ors", own, image, precision=precision)

        def group_sum(g):
            mask = (own_groups == g).astype(jnp.float32)
            return jnp.sum(mask[:, None, None] * grams, axis=0)

        total = group_sum(gr_pos) + swap(group_sum(gr_pos ^ 1), "gr", 1)
        packed = tok_count == 4 and own_cols % PANEL == 0
        if packed:
            total = jnp.concatenate(
                [
                    lax.dynamic_slice_in_dim(
                        total, (tok_pos + d) % tok_count * own_cols, own_cols, 1
                    )
                    for d in range(tok_count // 2 + 1)
                ],
                axis=1,
            )
        step = 1
        while step < gc_count:
            if 2 * step == gc_count:
                total, beside = lax.optimization_barrier((total, beside))
                beside = half_over_gr(beside) if last else mix_seen(beside)
            total += swap(total, "gc", step)
            step *= 2
        if last:
            total, beside = lax.optimization_barrier((total, beside))
            beside = lax.psum_scatter(beside, "gc", scatter_dimension=0, tiled=True)
        if packed:
            pieces = collect(total, "tok")
        else:
            pieces = [lax.all_gather(total, "tok", axis=0, tiled=True)]
        own = inverse_factor(pieces, last, 1.0 / group_cols)
        if last:
            own, beside = lax.optimization_barrier((own, beside))
        other = swap(own, "gr", 1)
        if not last:
            other, beside = lax.optimization_barrier((other, beside))
        of_block = jnp.stack(
            [jnp.where(own_groups[o] == gr_pos, own, other) for o in range(owned)]
        )
        of_group = [jnp.where(gr_pos == g, own, other) for g in range(groups)]
        return of_block, of_group, beside

    image = image_of(mixed, basis_bf)
    def mix_seen(seen):
        seen = lax.all_gather(seen, ("gr", "gc"), axis=0, tiled=True)
        return jnp.sum(own_links[:, :, None, None] * seen[None], axis=1)

    of_block, _, second = factor(image, False, seen_by(image))
    mixed = jnp.einsum("otr,osr->ots", second, of_block, precision=HIGH).astype(jnp.bfloat16)
    basis_bf = jnp.einsum("obr,osr->obs", image, of_block, precision=HIGH).astype(jnp.bfloat16)
    image = image_of(mixed, basis_bf)
    codes = seen_by(image)
    placed = jnp.concatenate(
        [
            jnp.sum((own_groups == g).astype(jnp.float32)[:, None, None] * codes, axis=0)
            for g in range(groups)
        ],
        axis=1,
    )
    of_block, of_group, placed = factor(image, True, placed)
    rows = lax.dynamic_slice_in_dim(image, tok_pos * slice_rows, slice_rows, 1)
    basis = jnp.einsum("obr,osr->obs", rows, of_block, precision=HIGH)
    latent = jnp.concatenate(
        [
            jnp.einsum(
                "tr,sr->ts",
                placed[:, g * rank : (g + 1) * rank],
                of_group[g],
                precision=HIGH,
            )
            for g in range(groups)
        ],
        axis=1,
    )
    latent = latent * (1.0 / math.sqrt(group_cols))
    return (basis, latent.astype(jnp.bfloat16))


def solution(mesh):
    placed = (P("tok", ("gr", "gc")), P(("gr", "gc"), "tok", None), P(), P())
    return jax.shard_map(
        per_device,
        mesh=mesh,
        in_specs=placed,
        out_specs=(P(("gr", "gc"), "tok", None), P(("tok", "gr", "gc"), None)),
        check_vma=False,
    )
```

```python
import functools
import math

import jax
import jax.numpy as jnp
from jax import lax
from jax.experimental import pallas as pl
from jax.experimental.pallas import tpu as pltpu
from jax.sharding import PartitionSpec as P

GBLK = 8
PANEL = 128
SUB = 8
CHUNKS = 2

ridge = 2.0
HIGHEST = lax.Precision.HIGHEST
HIGH = lax.Precision.HIGH


def split(value):
    high = lax.reduce_precision(value, 8, 7)
    return high.astype(jnp.bfloat16), (value - high).astype(jnp.bfloat16)


def kernel_dot(left, right, exact):
    if exact:
        return jnp.dot(left, right, preferred_element_type=jnp.float32, precision=HIGHEST)
    parts = []
    for value in (left, right):
        high = value.astype(jnp.bfloat16)
        parts.append((high, (value - high.astype(jnp.float32)).astype(jnp.bfloat16)))
    (a, b), (c, d) = parts
    return sum(
        jnp.dot(x, y, preferred_element_type=jnp.float32) for x, y in ((b, c), (a, d), (a, c))
    )


def eliminate(tiles, inv_ref):
    shape = (SUB, PANEL)
    lane = lax.broadcasted_iota(jnp.int32, shape, 1)
    sub = lax.broadcasted_iota(jnp.int32, shape, 0)

    def spread(column):
        return jnp.broadcast_to(column, shape)

    tiles = list(tiles)
    for s in range(PANEL // SUB):
        start = s * SUB
        tile = tiles[s]
        inside = (lane >= start) & (lane < start + SUB)
        columns = [spread(tile[:, start + c : start + c + 1]) for c in range(SUB)]
        pivot = [
            [spread(columns[c][i : i + 1, :]) if c >= i else None for c in range(SUB)]
            for i in range(SUB)
        ]
        base = jnp.where(inside, jnp.where(lane == start + sub, 1.0, 0.0), tile)
        rows = [spread(base[i : i + 1, :]) for i in range(SUB)]
        below = [[None] * SUB for _ in range(SUB)]
        inverse = []
        for b in range(0, SUB, 2):
            head, side, tail = pivot[b][b], pivot[b][b + 1], pivot[b + 1][b + 1]
            det = head * tail - side * side
            inverse.append(pl.reciprocal(head, approx=True))
            inverse.append(head * pl.reciprocal(det, approx=True))
            link = side * inverse[b]
            below[b + 1][b] = link
            rows[b + 1] = rows[b + 1] - link * rows[b]
            pivot[b + 1][b + 1] = det * inverse[b]
            for i in range(b + 2, SUB):
                pivot[b + 1][i] = pivot[b + 1][i] - link * pivot[b][i]
                below[i][b] = pivot[b][i] * inverse[b]
                below[i][b + 1] = pivot[b + 1][i] * inverse[b + 1]
            for i in range(b + 2, SUB):
                for c in range(i, SUB):
                    pivot[i][c] = (pivot[i][c] - below[i][b] * pivot[b][c]) - (
                        below[i][b + 1] * pivot[b + 1][c]
                    )
                rows[i] = (rows[i] - below[i][b] * rows[b]) - below[i][b + 1] * rows[b + 1]
        result = jnp.zeros(shape, jnp.float32)
        for b in range(SUB):
            result = jnp.where(sub == b, rows[b] * lax.rsqrt(pivot[b][b]), result)
        inv_ref[start : start + SUB, :] = jnp.where(lane < start + SUB, result, 0.0)
        solved = [None] * SUB
        for b in reversed(range(SUB)):
            value = rows[b] * inverse[b]
            for i in reversed(range(b + 1, SUB)):
                value = value - below[i][b] * solved[i]
            solved[b] = value
        for q in range(s + 1, PANEL // SUB):
            parts = [
                spread(tiles[q][:, start + b : start + b + 1]) * solved[b] for b in range(SUB)
            ]
            while len(parts) > 1:
                parts = [x + y for x, y in zip(parts[::2], parts[1::2])]
            tiles[q] = jnp.where(inside, 0.0, tiles[q]) - parts[0]


def factor_kernel(scale, exact, pos_ref, *refs):
    *piece_refs, out_ref, work_ref, inv_ref = refs
    rank = work_ref.shape[0]
    panels = rank // PANEL
    count = len(piece_refs)
    if count == 1:
        work_ref[...] = piece_refs[0][...] * scale
    else:
        work_ref[...] = jnp.zeros((rank, rank), jnp.float32)
    own_cols = rank // count
    for k in range(count if count > 1 else 0):
        for s in range(count):

            @pl.when(pos_ref[0] ^ k == s)
            def _():
                for d in range(piece_refs[k].shape[1] // own_cols):
                    other = (s + d) % count
                    block = piece_refs[k][:, d * own_cols : (d + 1) * own_cols] * scale
                    low, high = min(s, other), max(s, other)
                    if s > other and 2 * d == count:
                        continue
                    work_ref[
                        low * own_cols : (low + 1) * own_cols,
                        high * own_cols : (high + 1) * own_cols,
                    ] = block.T if s > other else block

    on_diag = lax.broadcasted_iota(jnp.int32, (PANEL, PANEL), 0) == lax.broadcasted_iota(
        jnp.int32, (PANEL, PANEL), 1
    )
    by_column = []
    for k in range(panels):
        panel = slice(k * PANEL, (k + 1) * PANEL)
        diag = jnp.where(on_diag, work_ref[panel, panel], 0.0)
        by_column.append(lax.rsqrt(jnp.sum(diag, axis=0, keepdims=True)))
        work_ref[panel, :] *= lax.rsqrt(jnp.sum(diag, axis=1, keepdims=True))
    for k in range(panels):
        work_ref[:, k * PANEL : (k + 1) * PANEL] *= by_column[k]

    def panel_step(k, carry):
        here = pl.ds(pl.multiple_of(k * PANEL, PANEL), PANEL)
        diag = work_ref[here, here]

        eliminate([diag[SUB * q : SUB * (q + 1), :] for q in range(PANEL // SUB)], inv_ref)
        for here_k in range(panels):

            @pl.when(k == here_k)
            def _():
                panel = slice(here_k * PANEL, (here_k + 1) * PANEL)
                rest = slice((here_k + 1) * PANEL, rank)
                inv = inv_ref[...]
                work_ref[panel, :] = kernel_dot(inv, work_ref[panel, :], exact)
                work_ref[panel, panel] = inv
                if here_k < panels - 1:
                    lower = work_ref[panel, rest].T
                    work_ref[rest, panel] = jnp.zeros((rank - rest.start, PANEL), jnp.float32)
                    work_ref[rest, :] -= kernel_dot(lower, work_ref[panel, :], exact)

        return carry

    lax.fori_loop(0, panels, panel_step, 0)
    for i in range(panels - 1):
        work_ref[i * PANEL : (i + 1) * PANEL, (i + 1) * PANEL :] = jnp.zeros(
            (PANEL, rank - (i + 1) * PANEL), jnp.float32
        )
    for k in range(panels):
        panel = slice(k * PANEL, (k + 1) * PANEL)
        out_ref[:, panel] = work_ref[:, panel] * by_column[k]


def inverse_factor(pieces, exact, scale):
    rank = pieces[0].shape[0] * len(pieces)
    pos = lax.axis_index("tok").astype(jnp.int32).reshape(1)
    return pl.pallas_call(
        functools.partial(factor_kernel, scale, exact),
        out_shape=jax.ShapeDtypeStruct((rank, rank), jnp.float32),
        in_specs=[
            pl.BlockSpec(memory_space=pltpu.SMEM),
            *[pl.BlockSpec(memory_space=pltpu.VMEM) for _ in pieces],
        ],
        out_specs=pl.BlockSpec(memory_space=pltpu.VMEM),
        scratch_shapes=[
            pltpu.VMEM((rank, rank), jnp.float32),
            pltpu.VMEM((PANEL, PANEL), jnp.float32),
        ],
        compiler_params=pltpu.CompilerParams(vmem_limit_bytes=32 * 1024 * 1024),
        cost_estimate=pl.CostEstimate(
            flops=96 * rank**3, bytes_accessed=8 * rank**2, transcendentals=0
        ),
        name="inverse_factor",
    )(pos, *pieces)


def swap(value, axis, k):
    if k == 0:
        return value
    return lax.ppermute(value, axis, [(i, i ^ k) for i in range(lax.axis_size(axis))])


def collect(value, axis):
    return [swap(value, axis, k) for k in range(lax.axis_size(axis))]


def per_device(acts, init_basis, kept, member):
    owned = init_basis.shape[0]
    slice_rows = init_basis.shape[1]
    rank = init_basis.shape[2]
    tok_count = lax.axis_size("tok")
    gr_count = lax.axis_size("gr")
    gc_count = lax.axis_size("gc")
    block_cols = slice_rows * tok_count
    tok_rows = acts.shape[0]
    total_tokens = tok_rows * tok_count
    groups = kept.shape[0] // GBLK
    assert groups == gr_count == 2
    group_cols = GBLK * block_cols
    own_cols = rank // tok_count
    tok_pos = lax.axis_index("tok")
    gr_pos = lax.axis_index("gr")
    gc_pos = lax.axis_index("gc")
    first = (gr_pos * gc_count + gc_pos) * owned
    links = ((member[:, None] == member[None, :]).astype(jnp.int32) * kept).astype(jnp.float32)
    own_links = lax.dynamic_slice_in_dim(links, first, owned, 0)
    partner = ((gr_pos ^ 1) * gc_count + gc_pos) * owned
    partner_links = lax.dynamic_slice_in_dim(links, partner, owned, 0)
    own_groups = lax.dynamic_slice_in_dim(member, first, owned, 0)

    own_x = acts.reshape(tok_rows, owned, block_cols)
    turned_x = jnp.concatenate(
        [
            lax.dynamic_slice_in_dim(own_x, (tok_pos ^ k) * slice_rows, slice_rows, 2)
            for k in range(tok_count)
        ],
        axis=2,
    )
    init_bf = init_basis.astype(jnp.bfloat16)
    width = rank // CHUNKS
    init_pieces = [
        collect(init_bf[:, :, c * width : (c + 1) * width], "tok") for c in range(CHUNKS)
    ]
    gathered_x = lax.all_gather(acts, "tok", axis=0, tiled=True)
    def combine(rows_of_links, pieces, sources):
        total = 0.0
        for piece, source in zip(pieces, sources):
            weights = lax.dynamic_slice_in_dim(rows_of_links, source, owned, 1)
            for j in range(owned):
                total += weights[:, j][:, None, None] * piece[j][None].astype(jnp.float32)
        return total

    near = []
    for part in init_pieces:
        proj = jnp.einsum(
            "tob,obr->otr",
            turned_x,
            jnp.concatenate(part, axis=1),
            preferred_element_type=jnp.float32,
        ).astype(jnp.bfloat16)
        near.append(collect(proj, "gc"))
    sources = [(gr_pos * gc_count + (gc_pos ^ b)) * owned for b in range(gc_count)]

    def mix(pieces):
        own = combine(own_links, pieces, sources)
        other = combine(partner_links, pieces, sources)
        return (own + swap(other, "gr", 1)).astype(jnp.bfloat16)

    mixed = jnp.concatenate([mix(pieces) for pieces in near], axis=2)
    basis_bf = jnp.concatenate(
        [
            jnp.concatenate(
                [lax.select_n(tok_pos ^ a, *part) for a in range(tok_count)], axis=1
            )
            for part in init_pieces
        ],
        axis=2,
    )
    gathered_x, basis_bf = lax.optimization_barrier((gathered_x, basis_bf))
    full_x = jnp.concatenate(
        [
            lax.dynamic_slice_in_dim(gathered_x, (tok_pos ^ k) * tok_rows, tok_rows, 0)
            for k in range(tok_count)
        ],
        axis=0,
    ).reshape(total_tokens, owned, block_cols)

    def image_of(mixed, basis_bf):
        full = jnp.concatenate(collect(mixed, "tok"), axis=1)
        cover = jnp.einsum("tob,otr->obr", full_x, full, preferred_element_type=jnp.float32)
        return cover / total_tokens + ridge * basis_bf.astype(jnp.float32)

    def seen_by(image):
        return sum(
            jnp.einsum("tob,obr->otr", own_x, part, preferred_element_type=jnp.float32)
            for part in split(image)
        )

    def half_over_gr(value):
        half = value.shape[0] // 2
        own = lax.dynamic_slice_in_dim(value, gr_pos * half, half, 0)
        other = lax.dynamic_slice_in_dim(value, (gr_pos ^ 1) * half, half, 0)
        return own + swap(other, "gr", 1)

    def factor(image, last, beside):
        precision = HIGHEST if last else HIGH
        own = lax.dynamic_slice_in_dim(image, tok_pos * own_cols, own_cols, 2)
        grams = jnp.einsum("obr,obs->ors", own, image, precision=precision)

        def group_sum(g):
            mask = (own_groups == g).astype(jnp.float32)
            return jnp.sum(mask[:, None, None] * grams, axis=0)

        total = group_sum(gr_pos) + swap(group_sum(gr_pos ^ 1), "gr", 1)
        packed = tok_count == 4 and own_cols % PANEL == 0
        if packed:
            total = jnp.concatenate(
                [
                    lax.dynamic_slice_in_dim(
                        total, (tok_pos + d) % tok_count * own_cols, own_cols, 1
                    )
                    for d in range(tok_count // 2 + 1)
                ],
                axis=1,
            )
        step = 1
        while step < gc_count:
            if 2 * step == gc_count:
                total, beside = lax.optimization_barrier((total, beside))
                beside = half_over_gr(beside) if last else mix_seen(beside)
            total += swap(total, "gc", step)
            step *= 2
        if last:
            total, beside = lax.optimization_barrier((total, beside))
            beside = lax.psum_scatter(beside, "gc", scatter_dimension=0, tiled=True)
        if packed:
            pieces = collect(total, "tok")
        else:
            pieces = [lax.all_gather(total, "tok", axis=0, tiled=True)]
        own = inverse_factor(pieces, last, 1.0 / group_cols)
        if last:
            own, beside = lax.optimization_barrier((own, beside))
        other = swap(own, "gr", 1)
        if not last:
            other, beside = lax.optimization_barrier((other, beside))
        of_group = [jnp.where(gr_pos == g, own, other) for g in range(groups)]
        if last:
            return (own, other), of_group, beside
        of_block = jnp.stack(
            [jnp.where(own_groups[o] == gr_pos, own, other) for o in range(owned)]
        )
        return of_block, of_group, beside

    image = image_of(mixed, basis_bf)
    def mix_seen(seen):
        seen = lax.all_gather(seen, ("gr", "gc"), axis=0, tiled=True)
        return jnp.sum(own_links[:, :, None, None] * seen[None], axis=1)

    of_block, _, second = factor(image, False, seen_by(image))
    mixed = jnp.einsum("otr,osr->ots", second, of_block, precision=HIGH).astype(jnp.bfloat16)
    basis_bf = jnp.einsum("obr,osr->obs", image, of_block, precision=HIGH).astype(jnp.bfloat16)
    image = image_of(mixed, basis_bf)
    codes = seen_by(image)
    placed = jnp.concatenate(
        [
            jnp.sum((own_groups == g).astype(jnp.float32)[:, None, None] * codes, axis=0)
            for g in range(groups)
        ],
        axis=1,
    )
    of_block, of_group, placed = factor(image, True, placed)
    rows = lax.dynamic_slice_in_dim(image, tok_pos * slice_rows, slice_rows, 1)
    by_own, by_other = [
        jnp.einsum("obr,sr->obs", rows, inverse, precision=HIGH) for inverse in of_block
    ]
    basis = jnp.where((own_groups == gr_pos)[:, None, None], by_own, by_other)
    latent = jnp.concatenate(
        [
            jnp.einsum(
                "tr,sr->ts",
                placed[:, g * rank : (g + 1) * rank],
                of_group[g],
                precision=HIGH,
            )
            for g in range(groups)
        ],
        axis=1,
    )
    latent = latent * (1.0 / math.sqrt(group_cols))
    return (basis, latent.astype(jnp.bfloat16))


def solution(mesh):
    placed = (P("tok", ("gr", "gc")), P(("gr", "gc"), "tok", None), P(), P())
    return jax.shard_map(
        per_device,
        mesh=mesh,
        in_specs=placed,
        out_specs=(P(("gr", "gc"), "tok", None), P(("tok", "gr", "gc"), None)),
        check_vma=False,
    )
```

```python
import functools
import math

import jax
import jax.numpy as jnp
from jax import lax
from jax.experimental import pallas as pl
from jax.experimental.pallas import tpu as pltpu
from jax.sharding import PartitionSpec as P

GBLK = 8
PANEL = 128
SUB = 8
CHUNKS = 2

ridge = 2.0
HIGHEST = lax.Precision.HIGHEST
HIGH = lax.Precision.HIGH


def split(value):
    high = lax.reduce_precision(value, 8, 7)
    return high.astype(jnp.bfloat16), (value - high).astype(jnp.bfloat16)


def kernel_dot(left, right, exact):
    if exact:
        return jnp.dot(left, right, preferred_element_type=jnp.float32, precision=HIGHEST)
    parts = []
    for value in (left, right):
        high = value.astype(jnp.bfloat16)
        parts.append((high, (value - high.astype(jnp.float32)).astype(jnp.bfloat16)))
    (a, b), (c, d) = parts
    return sum(
        jnp.dot(x, y, preferred_element_type=jnp.float32) for x, y in ((b, c), (a, d), (a, c))
    )


def eliminate(tiles, inv_ref):
    shape = (SUB, PANEL)
    lane = lax.broadcasted_iota(jnp.int32, shape, 1)
    sub = lax.broadcasted_iota(jnp.int32, shape, 0)

    def spread(column):
        return jnp.broadcast_to(column, shape)

    tiles = list(tiles)
    for s in range(PANEL // SUB):
        start = s * SUB
        tile = tiles[s]
        inside = (lane >= start) & (lane < start + SUB)
        columns = [spread(tile[:, start + c : start + c + 1]) for c in range(SUB)]
        pivot = [
            [spread(columns[c][i : i + 1, :]) if c >= i else None for c in range(SUB)]
            for i in range(SUB)
        ]
        base = jnp.where(inside, jnp.where(lane == start + sub, 1.0, 0.0), tile)
        rows = [spread(base[i : i + 1, :]) for i in range(SUB)]
        below = [[None] * SUB for _ in range(SUB)]
        inverse = []
        for b in range(0, SUB, 2):
            head, side, tail = pivot[b][b], pivot[b][b + 1], pivot[b + 1][b + 1]
            det = head * tail - side * side
            inverse.append(pl.reciprocal(head, approx=True))
            inverse.append(head * pl.reciprocal(det, approx=True))
            link = side * inverse[b]
            below[b + 1][b] = link
            rows[b + 1] = rows[b + 1] - link * rows[b]
            pivot[b + 1][b + 1] = det * inverse[b]
            for i in range(b + 2, SUB):
                pivot[b + 1][i] = pivot[b + 1][i] - link * pivot[b][i]
                below[i][b] = pivot[b][i] * inverse[b]
                below[i][b + 1] = pivot[b + 1][i] * inverse[b + 1]
            for i in range(b + 2, SUB):
                for c in range(i, SUB):
                    pivot[i][c] = (pivot[i][c] - below[i][b] * pivot[b][c]) - (
                        below[i][b + 1] * pivot[b + 1][c]
                    )
                rows[i] = (rows[i] - below[i][b] * rows[b]) - below[i][b + 1] * rows[b + 1]
        result = jnp.zeros(shape, jnp.float32)
        for b in range(SUB):
            result = jnp.where(sub == b, rows[b] * lax.rsqrt(pivot[b][b]), result)
        inv_ref[start : start + SUB, :] = jnp.where(lane < start + SUB, result, 0.0)
        solved = [None] * SUB
        for b in reversed(range(SUB)):
            value = rows[b] * inverse[b]
            for i in reversed(range(b + 1, SUB)):
                value = value - below[i][b] * solved[i]
            solved[b] = value
        for q in range(s + 1, PANEL // SUB):
            parts = [
                spread(tiles[q][:, start + b : start + b + 1]) * solved[b] for b in range(SUB)
            ]
            while len(parts) > 1:
                parts = [x + y for x, y in zip(parts[::2], parts[1::2])]
            tiles[q] = jnp.where(inside, 0.0, tiles[q]) - parts[0]


def factor_kernel(scale, exact, pos_ref, *refs):
    *piece_refs, out_ref, work_ref, inv_ref = refs
    rank = work_ref.shape[0]
    panels = rank // PANEL
    count = len(piece_refs)
    if count == 1:
        work_ref[...] = piece_refs[0][...] * scale
    else:
        work_ref[...] = jnp.zeros((rank, rank), jnp.float32)
    own_cols = rank // count
    for k in range(count if count > 1 else 0):
        for s in range(count):

            @pl.when(pos_ref[0] ^ k == s)
            def _():
                for d in range(piece_refs[k].shape[1] // own_cols):
                    other = (s + d) % count
                    block = piece_refs[k][:, d * own_cols : (d + 1) * own_cols] * scale
                    low, high = min(s, other), max(s, other)
                    if s > other and 2 * d == count:
                        continue
                    work_ref[
                        low * own_cols : (low + 1) * own_cols,
                        high * own_cols : (high + 1) * own_cols,
                    ] = block.T if s > other else block

    on_diag = lax.broadcasted_iota(jnp.int32, (PANEL, PANEL), 0) == lax.broadcasted_iota(
        jnp.int32, (PANEL, PANEL), 1
    )
    by_column = []
    for k in range(panels):
        panel = slice(k * PANEL, (k + 1) * PANEL)
        diag = jnp.where(on_diag, work_ref[panel, panel], 0.0)
        by_column.append(lax.rsqrt(jnp.sum(diag, axis=0, keepdims=True)))
        work_ref[panel, :] *= lax.rsqrt(jnp.sum(diag, axis=1, keepdims=True))
    for k in range(panels):
        work_ref[:, k * PANEL : (k + 1) * PANEL] *= by_column[k]

    def panel_step(k, carry):
        here = pl.ds(pl.multiple_of(k * PANEL, PANEL), PANEL)
        diag = work_ref[here, here]

        eliminate([diag[SUB * q : SUB * (q + 1), :] for q in range(PANEL // SUB)], inv_ref)
        for here_k in range(panels):

            @pl.when(k == here_k)
            def _():
                panel = slice(here_k * PANEL, (here_k + 1) * PANEL)
                rest = slice((here_k + 1) * PANEL, rank)
                inv = inv_ref[...]
                work_ref[panel, :] = kernel_dot(inv, work_ref[panel, :], exact)
                work_ref[panel, panel] = inv
                if here_k < panels - 1:
                    lower = work_ref[panel, rest].T
                    work_ref[rest, panel] = jnp.zeros((rank - rest.start, PANEL), jnp.float32)
                    work_ref[rest, :] -= kernel_dot(lower, work_ref[panel, :], exact)

        return carry

    lax.fori_loop(0, panels, panel_step, 0)
    for i in range(panels - 1):
        work_ref[i * PANEL : (i + 1) * PANEL, (i + 1) * PANEL :] = jnp.zeros(
            (PANEL, rank - (i + 1) * PANEL), jnp.float32
        )
    for k in range(panels):
        panel = slice(k * PANEL, (k + 1) * PANEL)
        out_ref[:, panel] = work_ref[:, panel] * by_column[k]


def inverse_factor(pieces, exact, scale):
    rank = pieces[0].shape[0] * len(pieces)
    pos = lax.axis_index("tok").astype(jnp.int32).reshape(1)
    return pl.pallas_call(
        functools.partial(factor_kernel, scale, exact),
        out_shape=jax.ShapeDtypeStruct((rank, rank), jnp.float32),
        in_specs=[
            pl.BlockSpec(memory_space=pltpu.SMEM),
            *[pl.BlockSpec(memory_space=pltpu.VMEM) for _ in pieces],
        ],
        out_specs=pl.BlockSpec(memory_space=pltpu.VMEM),
        scratch_shapes=[
            pltpu.VMEM((rank, rank), jnp.float32),
            pltpu.VMEM((PANEL, PANEL), jnp.float32),
        ],
        compiler_params=pltpu.CompilerParams(vmem_limit_bytes=32 * 1024 * 1024),
        cost_estimate=pl.CostEstimate(
            flops=96 * rank**3, bytes_accessed=8 * rank**2, transcendentals=0
        ),
        name="inverse_factor",
    )(pos, *pieces)


def swap(value, axis, k):
    if k == 0:
        return value
    return lax.ppermute(value, axis, [(i, i ^ k) for i in range(lax.axis_size(axis))])


def collect(value, axis):
    return [swap(value, axis, k) for k in range(lax.axis_size(axis))]


def per_device(acts, init_basis, kept, member):
    owned = init_basis.shape[0]
    slice_rows = init_basis.shape[1]
    rank = init_basis.shape[2]
    tok_count = lax.axis_size("tok")
    gr_count = lax.axis_size("gr")
    gc_count = lax.axis_size("gc")
    block_cols = slice_rows * tok_count
    tok_rows = acts.shape[0]
    total_tokens = tok_rows * tok_count
    groups = kept.shape[0] // GBLK
    assert groups == gr_count == 2
    group_cols = GBLK * block_cols
    own_cols = rank // tok_count
    tok_pos = lax.axis_index("tok")
    gr_pos = lax.axis_index("gr")
    gc_pos = lax.axis_index("gc")
    first = (gr_pos * gc_count + gc_pos) * owned
    links = ((member[:, None] == member[None, :]).astype(jnp.int32) * kept).astype(jnp.float32)
    own_links = lax.dynamic_slice_in_dim(links, first, owned, 0)
    partner = ((gr_pos ^ 1) * gc_count + gc_pos) * owned
    partner_links = lax.dynamic_slice_in_dim(links, partner, owned, 0)
    own_groups = lax.dynamic_slice_in_dim(member, first, owned, 0)

    own_x = acts.reshape(tok_rows, owned, block_cols)
    turned_x = jnp.concatenate(
        [
            lax.dynamic_slice_in_dim(own_x, (tok_pos ^ k) * slice_rows, slice_rows, 2)
            for k in range(tok_count)
        ],
        axis=2,
    )
    init_bf = init_basis.astype(jnp.bfloat16)
    width = rank // CHUNKS
    init_pieces = [
        collect(init_bf[:, :, c * width : (c + 1) * width], "tok") for c in range(CHUNKS)
    ]
    gathered_x = lax.all_gather(acts, "tok", axis=0, tiled=True)
    def combine(rows_of_links, pieces, sources):
        total = 0.0
        for piece, source in zip(pieces, sources):
            weights = lax.dynamic_slice_in_dim(rows_of_links, source, owned, 1)
            for j in range(owned):
                total += weights[:, j][:, None, None] * piece[j][None].astype(jnp.float32)
        return total

    near = []
    for part in init_pieces:
        proj = jnp.einsum(
            "tob,obr->otr",
            turned_x,
            jnp.concatenate(part, axis=1),
            preferred_element_type=jnp.float32,
        ).astype(jnp.bfloat16)
        near.append(collect(proj, "gc"))
    sources = [(gr_pos * gc_count + (gc_pos ^ b)) * owned for b in range(gc_count)]

    def mix(pieces):
        own = combine(own_links, pieces, sources)
        other = combine(partner_links, pieces, sources)
        return (own + swap(other, "gr", 1)).astype(jnp.bfloat16)

    mixed = jnp.concatenate([mix(pieces) for pieces in near], axis=2)
    basis_bf = jnp.concatenate(
        [
            jnp.concatenate(
                [lax.select_n(tok_pos ^ a, *part) for a in range(tok_count)], axis=1
            )
            for part in init_pieces
        ],
        axis=2,
    )
    gathered_x, basis_bf = lax.optimization_barrier((gathered_x, basis_bf))
    full_x = jnp.concatenate(
        [
            lax.dynamic_slice_in_dim(gathered_x, (tok_pos ^ k) * tok_rows, tok_rows, 0)
            for k in range(tok_count)
        ],
        axis=0,
    ).reshape(total_tokens, owned, block_cols)

    def image_of(mixed, basis_bf):
        full = jnp.concatenate(collect(mixed, "tok"), axis=1)
        cover = jnp.einsum("tob,otr->obr", full_x, full, preferred_element_type=jnp.float32)
        return cover / total_tokens + ridge * basis_bf.astype(jnp.float32)

    def seen_by(image):
        return sum(
            jnp.einsum("tob,obr->otr", own_x, part, preferred_element_type=jnp.float32)
            for part in split(image)
        )

    def half_over_gr(value):
        half = value.shape[0] // 2
        own = lax.dynamic_slice_in_dim(value, gr_pos * half, half, 0)
        other = lax.dynamic_slice_in_dim(value, (gr_pos ^ 1) * half, half, 0)
        return own + swap(other, "gr", 1)

    def factor(image, last, beside):
        precision = HIGHEST if last else HIGH
        own = lax.dynamic_slice_in_dim(image, tok_pos * own_cols, own_cols, 2)
        grams = jnp.einsum("obr,obs->ors", own, image, precision=precision)

        def group_sum(g):
            mask = (own_groups == g).astype(jnp.float32)
            return jnp.sum(mask[:, None, None] * grams, axis=0)

        total = group_sum(gr_pos) + swap(group_sum(gr_pos ^ 1), "gr", 1)
        packed = tok_count == 4 and own_cols % PANEL == 0
        if packed:
            total = jnp.concatenate(
                [
                    lax.dynamic_slice_in_dim(
                        total, (tok_pos + d) % tok_count * own_cols, own_cols, 1
                    )
                    for d in range(tok_count // 2 + 1)
                ],
                axis=1,
            )
        step = 1
        while step < gc_count:
            if 2 * step == gc_count:
                total, beside = lax.optimization_barrier((total, beside))
                beside = half_over_gr(beside) if last else mix_seen(beside)
            total += swap(total, "gc", step)
            step *= 2
        if last:
            total, beside = lax.optimization_barrier((total, beside))
            beside = lax.psum_scatter(beside, "gc", scatter_dimension=0, tiled=True)
        if packed:
            pieces = collect(total, "tok")
        else:
            pieces = [lax.all_gather(total, "tok", axis=0, tiled=True)]
        own = inverse_factor(pieces, last, 1.0 / group_cols)
        if last:
            own, beside = lax.optimization_barrier((own, beside))
        other = swap(own, "gr", 1)
        if not last:
            other, beside = lax.optimization_barrier((other, beside))
        of_group = [jnp.where(gr_pos == g, own, other) for g in range(groups)]
        if last:
            return (own, other), of_group, beside
        of_block = jnp.stack(
            [jnp.where(own_groups[o] == gr_pos, own, other) for o in range(owned)]
        )
        return of_block, of_group, beside

    image = image_of(mixed, basis_bf)
    def mix_seen(seen):
        seen = lax.all_gather(seen, ("gr", "gc"), axis=0, tiled=True)
        return jnp.sum(own_links[:, :, None, None] * seen[None], axis=1)

    of_block, _, second = factor(image, False, seen_by(image))
    mixed = jnp.einsum("otr,osr->ots", second, of_block, precision=HIGH).astype(jnp.bfloat16)
    basis_bf = jnp.einsum("obr,osr->obs", image, of_block, precision=HIGH).astype(jnp.bfloat16)
    image = image_of(mixed, basis_bf)
    codes = seen_by(image)
    placed = jnp.concatenate(
        [
            jnp.sum((own_groups == g).astype(jnp.float32)[:, None, None] * codes, axis=0)
            for g in range(groups)
        ],
        axis=1,
    )
    rows = split(lax.dynamic_slice_in_dim(image, tok_pos * slice_rows, slice_rows, 1))
    rows = jnp.concatenate([rows[0], rows[0], rows[1]], axis=2)
    placed, rows = lax.optimization_barrier((placed, rows))
    of_block, of_group, placed = factor(image, True, placed)
    by_own, by_other = [
        jnp.einsum(
            "obk,sk->obs",
            rows,
            jnp.concatenate([split(inverse)[i] for i in (0, 1, 0)], axis=1),
            preferred_element_type=jnp.float32,
        )
        for inverse in of_block
    ]
    basis = jnp.where((own_groups == gr_pos)[:, None, None], by_own, by_other)
    latent = jnp.concatenate(
        [
            jnp.einsum(
                "tr,sr->ts",
                placed[:, g * rank : (g + 1) * rank],
                of_group[g],
                precision=HIGH,
            )
            for g in range(groups)
        ],
        axis=1,
    )
    latent = latent * (1.0 / math.sqrt(group_cols))
    return (basis, latent.astype(jnp.bfloat16))


def solution(mesh):
    placed = (P("tok", ("gr", "gc")), P(("gr", "gc"), "tok", None), P(), P())
    return jax.shard_map(
        per_device,
        mesh=mesh,
        in_specs=placed,
        out_specs=(P(("gr", "gc"), "tok", None), P(("tok", "gr", "gc"), None)),
        check_vma=False,
    )
```
